128 devices in a mesh: row: 16 (over z_lo, y, core), col: 8 (over z_hi, x).
Axes of the slice: x: 4, y: 4, z: 4 (z_hi: 2, z_lo: 2; z = z_hi * 2 + z_lo), core: 2. Of those that a mesh axis runs over, the one named last changes fastest.
Arguments:
- hidden_in: float32 [16384, 1024], P('row', 'col'), may hold values from -6 to 6
- joined_weight: bfloat16 [2, 1024, 3072], P(None, 'row', 'col'), may hold values from -0.1875 to 0.1875
- query_bias: bfloat16 [2, 1024], P(None, ('col', 'row')), may hold values from -3 to 3
- value_bias: bfloat16 [2, 1024], P(None, ('col', 'row')), may hold values from -1.75 to 1.75
- out_weight: bfloat16 [2, 1024, 1024], P(None, 'col', 'row'), may hold values from -0.5 to 0.5
- out_bias: bfloat16 [2, 1024], P(None, ('col', 'row')), may hold values from -1.75 to 1.75
- first_gain: bfloat16 [2, 1024], P(None, ('col', 'row')), may hold values from 0.25 to 1.75
- first_shift: bfloat16 [2, 1024], P(None, ('col', 'row')), may hold values from -1.75 to 1.75
- up_weight: bfloat16 [2, 1024, 4096], P(None, 'row', 'col'), may hold values from -0.1875 to 0.1875
- up_bias: bfloat16 [2, 4096], P(None, ('col', 'row')), may hold values from -1.75 to 1.75
- down_weight: bfloat16 [2, 4096, 1024], P(None, 'col', 'row'), may hold values from -0.09375 to 0.09375
- down_bias: bfloat16 [2, 1024], P(None, ('col', 'row')), may hold values from -1.75 to 1.75
- second_gain: bfloat16 [2, 1024], P(None, ('col', 'row')), may hold values from 0.25 to 1.75
- second_shift: bfloat16 [2, 1024], P(None, ('col', 'row')), may hold values from -1.75 to 1.75
- seq_lengths: int32 [16, 4], P('row'), may hold values from 0 to 1024, as said below
- cotangent: float32 [16384, 1024], P('row', 'col'), may hold values from -6 to 6
Outputs:
- hidden_out: float32 [16384, 1024], P('row', 'col')
- grad_hidden: float32 [16384, 1024], P('row', 'col')
- grad_joined_weight: float32 [2, 1024, 3072], P(None, 'row', 'col')
- grad_query_bias: float32 [2, 1024], P(None, ('col', 'row'))
- grad_value_bias: float32 [2, 1024], P(None, ('col', 'row'))
- grad_out_weight: float32 [2, 1024, 1024], P(None, 'col', 'row')
- grad_out_bias: float32 [2, 1024], P(None, ('col', 'row'))
- grad_first_gain: float32 [2, 1024], P(None, ('col', 'row'))
- grad_first_shift: float32 [2, 1024], P(None, ('col', 'row'))
- grad_up_weight: float32 [2, 1024, 4096], P(None, 'row', 'col')
- grad_up_bias: float32 [2, 4096], P(None, ('col', 'row'))
- grad_down_weight: float32 [2, 4096, 1024], P(None, 'col', 'row')
- grad_down_bias: float32 [2, 1024], P(None, ('col', 'row'))
- grad_second_gain: float32 [2, 1024], P(None, ('col', 'row'))
- grad_second_shift: float32 [2, 1024], P(None, ('col', 'row'))
The draws below stay inside these ranges and needn't reach their ends.
Inputs may be any that keep to these rules, and one draw needn't show every extreme that they name: `seq_lengths`: each group's 4 lengths sum to between 512 and 1024, the rest of its 1024 rows being padding; in one group, drawn from the seed, a single sequence fills all 1024 rows. Lengths may be 0.
All inputs are finite; a program needn't handle non-finite values.
Results may differ from the reference program's by a relative error of at most 0.04.
Values may be sent and summed in bfloat16 or wider, within the bound.
A program may use at most 128 MiB of HBM per device.

```python
import jax
import jax.numpy as jnp
from jax import lax

D = 1024
HEADS = 16
FF = 4096
HDIM = 64
LAYERS = 2
SLOTS = 4
CAP = 1024
GROUPS = 16
TOKENS = 16384


def draw_seq_lengths(key, part):
    key = jax.random.fold_in(key, 7)
    used_key, cut_key, full_key = jax.random.split(key, 3)
    used_tokens = jax.random.randint(used_key, (GROUPS, 1), CAP // 2, CAP + 1)
    cut_points = jax.random.randint(cut_key, (GROUPS, SLOTS - 1), 0, CAP + 1)
    cut_points = jnp.sort(jnp.minimum(cut_points, used_tokens), axis=1)
    bounds = jnp.concatenate([jnp.zeros((GROUPS, 1), jnp.int32), cut_points, used_tokens], axis=1)
    span_sizes = bounds[:, 1:] - bounds[:, :-1]
    chosen = jax.random.randint(full_key, (), 0, GROUPS)
    single = jnp.concatenate([jnp.full((1,), CAP, jnp.int32), jnp.zeros((SLOTS - 1,), jnp.int32)])
    span_sizes = jnp.where((jnp.arange(GROUPS) == chosen)[:, None], single[None, :], span_sizes)
    return span_sizes.astype(jnp.int32)


def steps_of(own_key, dims, pieces, low, high):
    factor_of = 1.0
    for axis_at, blocks in pieces:
        draws = jax.random.uniform(jax.random.fold_in(jax.random.fold_in(own_key, 6), axis_at), (blocks,), jnp.float32, low / len(pieces), high / len(pieces))
        factor_of = factor_of * jnp.repeat(jnp.exp(draws), dims[axis_at] // blocks).reshape((-1,) + (1,) * (len(dims) - 1 - axis_at))
    return factor_of


def normal_values(key, extent, deviation, most, cuts=(), kind=jnp.bfloat16):
    loudness = steps_of(key, extent, cuts, -0.22, 0.18) if cuts else 1.0
    array = jax.random.normal(key, extent, jnp.float32) * deviation * loudness
    return jnp.minimum(jnp.maximum(array, -most), most).astype(kind)


def setup_inputs(seed: int = 0) -> dict:
    splits = jax.random.split(jax.random.key(seed), 17)
    hidden_in = normal_values(splits[0], (TOKENS, D), 1.0, 6.0, ((0, 16), (1, 8)), jnp.float32)
    joined_weight = normal_values(splits[1], (LAYERS, D, 3 * D), D ** -0.5, 0.1875, ((1, 16), (2, 8)))
    query_bias = normal_values(splits[2], (LAYERS, D), 0.5, 3.0, ((1, 128),))
    value_bias = normal_values(splits[3], (LAYERS, D), 0.3, 1.75, ((1, 128),))
    out_weight = normal_values(splits[4], (LAYERS, D, D), (D // 8) ** -0.5, 0.5, ((1, 8), (2, 16)))
    out_bias = normal_values(splits[5], (LAYERS, D), 0.3, 1.75, ((1, 128),))
    first_gain = jnp.clip(1.0 + 0.15 * jax.random.normal(splits[6], (LAYERS, D), jnp.float32), 0.25, 1.75).astype(jnp.bfloat16)
    first_shift = normal_values(splits[7], (LAYERS, D), 0.3, 1.75, ((1, 128),))
    up_weight = normal_values(splits[8], (LAYERS, D, FF), D ** -0.5, 0.1875, ((1, 16), (2, 8)))
    up_bias = normal_values(splits[9], (LAYERS, FF), 0.3, 1.75, ((1, 128),))
    down_weight = normal_values(splits[10], (LAYERS, FF, D), FF ** -0.5, 0.09375, ((1, 8), (2, 16)))
    down_bias = normal_values(splits[11], (LAYERS, D), 0.3, 1.75, ((1, 128),))
    second_gain = jnp.clip(1.0 + 0.15 * jax.random.normal(splits[12], (LAYERS, D), jnp.float32), 0.25, 1.75).astype(jnp.bfloat16)
    second_shift = normal_values(splits[13], (LAYERS, D), 0.3, 1.75, ((1, 128),))
    seq_lengths = draw_seq_lengths(jax.random.fold_in(splits[16], 71), 0)
    cotangent = normal_values(splits[15], (TOKENS, D), 1.0, 6.0, ((0, 16), (1, 8)), jnp.float32)
    return dict(hidden_in=hidden_in, joined_weight=joined_weight, query_bias=query_bias, value_bias=value_bias, out_weight=out_weight, out_bias=out_bias, first_gain=first_gain, first_shift=first_shift, up_weight=up_weight, up_bias=up_bias, down_weight=down_weight, down_bias=down_bias, second_gain=second_gain, second_shift=second_shift, seq_lengths=seq_lengths, cotangent=cotangent)


EPS = 1e-05
NEG = -1000000000.0
HIGH = lax.Precision.HIGHEST

@jax.custom_vjp
def low(v):
    return lax.optimization_barrier(v.astype(jnp.bfloat16)).astype(jnp.float32)

@jax.custom_vjp
def low_back(v):
    return v

def low_keep(v):
    return (low(v), None)

def low_pass(kept, grad):
    return (grad,)

def back_keep(v):
    return (v, None)

def back_low(kept, grad):
    return (low(grad),)
low.defvjp(low_keep, low_pass)
low_back.defvjp(back_keep, back_low)

def gelu_tanh(values):
    return 0.5 * values * (1.0 + jnp.tanh(0.7978845608028654 * (values + 0.044715 * values * values * values)))

def layer_norm(values, gain, shift):
    mean_rows = lax.optimization_barrier(jnp.mean(values, axis=-1, keepdims=True))
    variance = lax.optimization_barrier(jnp.mean(jnp.square(values - mean_rows), axis=-1, keepdims=True))
    return (values - mean_rows) * lax.rsqrt(variance + EPS) * gain + shift

def attend_group(group_items):
    query_rows, key_rows, value_rows, lengths_row = group_items
    seq_ends = jnp.cumsum(lengths_row)
    positions = jnp.arange(CAP, dtype=jnp.int32)
    segment = lax.optimization_barrier(jnp.sum((positions[:, None] >= seq_ends[None, :]).astype(jnp.int32), axis=1))
    offset = (positions[None, :] - positions[:, None]).astype(jnp.float32)
    slopes = jnp.exp2(-8.0 * (jnp.arange(HEADS, dtype=jnp.float32) + 1.0) / HEADS)
    scores = jnp.einsum('qhd,khd->hqk', query_rows, key_rows, precision=HIGH) * HDIM ** (-0.5)
    scores = low_back(scores + slopes[:, None, None] * offset[None])
    allowed = (segment[:, None] == segment[None, :]) & (positions[None, :] <= positions[:, None])
    scores = jnp.where(allowed[None], scores, NEG)
    soft_probs = low(jax.nn.softmax(scores, axis=-1))
    return jnp.einsum('hqk,khd->qhd', soft_probs, value_rows, precision=HIGH)

def run_layer(hidden, weights, seq_lengths):
    joined_weight, query_bias, value_bias, out_weight, out_bias, first_gain, first_shift, up_weight, up_bias, down_weight, down_bias, second_gain, second_shift = weights
    first_rows = low(layer_norm(hidden, first_gain, first_shift))
    joined_rows = jnp.dot(first_rows, joined_weight, precision=HIGH).reshape(TOKENS, HEADS, 3, HDIM)
    query_rows = low_back(low(joined_rows[:, :, 0] + query_bias.reshape(HEADS, HDIM)))
    key_rows = low_back(low(joined_rows[:, :, 1]))
    value_rows = low_back(low(joined_rows[:, :, 2] + value_bias.reshape(HEADS, HDIM)))
    group_shape = (GROUPS, CAP, HEADS, HDIM)
    mixed_heads = lax.map(jax.checkpoint(attend_group), (query_rows.reshape(group_shape), key_rows.reshape(group_shape), value_rows.reshape(group_shape), seq_lengths))
    heads_out = low_back(low(mixed_heads.reshape(TOKENS, D)))
    branch = low_back(jnp.dot(heads_out, out_weight, precision=HIGH) + out_bias)
    middle = hidden + branch
    second_rows = low(layer_norm(middle, second_gain, second_shift))
    up_rows = low_back(jnp.dot(second_rows, up_weight, precision=HIGH) + up_bias)
    activated = low(gelu_tanh(up_rows))
    down_rows = low_back(jnp.dot(activated, down_weight, precision=HIGH) + down_bias)
    return middle + down_rows

def reference(hidden_in, joined_weight, query_bias, value_bias, out_weight, out_bias, first_gain, first_shift, up_weight, up_bias, down_weight, down_bias, second_gain, second_shift, seq_lengths, cotangent):
    params = tuple((weight_array.astype(jnp.float32) for weight_array in (joined_weight, query_bias, value_bias, out_weight, out_bias, first_gain, first_shift, up_weight, up_bias, down_weight, down_bias, second_gain, second_shift)))

    def forward(hidden, weights_all):
        for layer_index in range(LAYERS):
            hidden = run_layer(hidden, tuple((member[layer_index] for member in weights_all)), seq_lengths)
        return hidden
    result, pullback = jax.vjp(forward, hidden_in.astype(jnp.float32), params)
    grad_hidden, weight_grads = pullback(cotangent.astype(jnp.float32))
    return (result, grad_hidden, weight_grads[0], weight_grads[1], weight_grads[2], weight_grads[3], weight_grads[4], weight_grads[5], weight_grads[6], weight_grads[7], weight_grads[8], weight_grads[9], weight_grads[10], weight_grads[11], weight_grads[12])
```

```python
import functools

import jax
import jax.numpy as jnp
from jax import lax
from jax.experimental import pallas as pl
from jax.experimental.pallas import tpu as pltpu
from jax.sharding import PartitionSpec as P

D = 1024
HEADS = 16
HDIM = 64
FF = 4096
LAYERS = 2
CAP = 1024
PARTS = 8
ROWS = CAP // PARTS
LOCAL_HEADS = HEADS // PARTS
EPS = 1e-05
NEG = -1000000000.0
MESH = pl.DeviceIdType.MESH


def place():
    row = lax.axis_index("row")
    col = lax.axis_index("col")
    return (
        lax.div(col, 4),
        lax.rem(col, 4),
        lax.div(row, 8),
        lax.div(lax.rem(row, 8), 2),
        lax.rem(row, 2),
    )


def device(h, x, zl, y, c):
    return (zl * 8 + y * 2 + c, h * 4 + x)


def turn(value, by, size):
    return lax.rem(value + by, size)


def rows_at(start, size):
    return pl.ds(pl.multiple_of(start, size), size)


def push(src, dst, send_sem, recv_sem, target):
    return pltpu.make_async_remote_copy(
        src_ref=src,
        dst_ref=dst,
        send_sem=send_sem,
        recv_sem=recv_sem,
        device_id=target,
        device_id_type=MESH,
    )


def greet(target):
    pl.semaphore_signal(
        pltpu.get_barrier_semaphore(), inc=1, device_id=target, device_id_type=MESH
    )


def await_greetings(count):
    pl.semaphore_wait(pltpu.get_barrier_semaphore(), count)


def unless(flag, run):
    pl.when(jnp.logical_not(flag))(run)


def together(*parts):
    alive = list(parts)
    while alive:
        alive = [part for part in alive if next(part, alive) is not alive]


def landed(view, send_sem, recv_sem):
    row, col = lax.axis_index("row"), lax.axis_index("col")
    push(view, view, send_sem, recv_sem, (row, lax.rem(col + 1, 8))).wait_recv()


def neighbours(where):
    h, x, zl, y, c = where
    return (
        device(h, turn(x, 1, 4), zl, y, c),
        device(h, turn(x, 3, 4), zl, y, c),
        device(h, x, zl, y, 1 - c),
    )


def greet_line(where):
    for other in neighbours(where):
        greet(other)
    return 3


def greet_ring(where, inward):
    h, x, zl, y, c = where
    home = lax.rem(h + c, 2) == 0
    for d in range(2):
        if inward:
            source = device(c, x, zl, y, turn(c, d, 2))
        else:
            source = device(turn(h, d, 2), x, zl, y, h)
        if d == 0:
            unless(home, functools.partial(greet, source))
        else:
            greet(source)
    for step in (1, 3):
        greet(device(h, x, zl, turn(y, step, 4), c))
    greet(device(h, x, 1 - zl, y, c))
    return 4 + lax.rem(h + c, 2)


def greet_swap(where, inward):
    h, x, zl, y, c = where
    home = lax.rem(h + c, 2) == 0
    for j in range(4):
        for d in range(2):
            if inward:
                source = device(turn(h, d, 2), turn(x, j, 4), zl, y, h)
            else:
                source = device(c, turn(x, j, 4), zl, y, turn(c, d, 2))
            if j == 0 and d == 0:
                unless(home, functools.partial(greet, source))
            else:
                greet(source)
    return 7 + lax.rem(h + c, 2)


def greet_parts(where):
    h, x, zl, y, c = where
    for j in range(4):
        for d in range(2):
            if j or d:
                greet(device(h, turn(x, j, 4), zl, y, turn(c, d, 2)))
    return 7


def move(src, dst, send_sem, recv_sem, target, home):
    unless(home, push(src, dst, send_sem, recv_sem, target).start)
    pl.when(home)(lambda: pltpu.make_async_copy(src, dst, recv_sem).start())


def moved_in(dst, send_sem, recv_sem, home):
    unless(home, functools.partial(landed, dst, send_sem, recv_sem))
    pl.when(home)(lambda: pltpu.make_async_copy(dst, dst, recv_sem).wait())


def moved_out(src, send_sem, recv_sem, target, home):
    unless(home, push(src, src, send_sem, recv_sem, target).wait_send)


def gather_line(where, src, out, own_sem, send, recv):
    h, x, zl, y, c = where
    right, left, mate = neighbours(where)
    half = ROWS // 2

    def block(core, step, first=0, size=ROWS):
        return out.at[rows_at((core * 4 + turn(x, step, 4)) * ROWS + first, size)]

    started = []

    def copy(index, view, target, source=None):
        source = view if source is None else source
        item = push(source, view, send.at[index], recv.at[index], target)
        item.start()
        started.append(item)

    def arrived(index, view):
        landed(view, send.at[index], recv.at[index])

    own = pltpu.make_async_copy(src, block(c, 0), own_sem)
    own.start()
    low, high = src.at[pl.ds(0, half)], src.at[pl.ds(half, half)]
    copy(0, block(c, 0, 0, half), right, low)
    copy(2, block(c, 0, half, half), left, high)
    copy(1, block(c, 0, half, half), right, high)
    copy(3, block(c, 0, 0, half), left, low)
    copy(4, block(c, 0), mate, src)
    yield
    arrived(0, block(c, 3, 0, half))
    copy(5, block(c, 3, 0, half), right)
    arrived(2, block(c, 1, half, half))
    copy(6, block(c, 1, half, half), left)
    yield
    arrived(1, block(c, 3, half, half))
    copy(7, block(c, 3), mate)
    arrived(3, block(c, 1, 0, half))
    copy(8, block(c, 1), mate)
    yield
    arrived(5, block(c, 2, 0, half))
    copy(9, block(c, 2, 0, half), mate)
    arrived(6, block(c, 2, half, half))
    copy(10, block(c, 2, half, half), mate)
    yield
    arrived(4, block(1 - c, 0))
    arrived(7, block(1 - c, 3))
    arrived(8, block(1 - c, 1))
    arrived(9, block(1 - c, 2, 0, half))
    arrived(10, block(1 - c, 2, half, half))
    for item in started:
        item.wait_send()
    own.wait()


LINE_SEMS = [
    pltpu.SemaphoreType.DMA,
    pltpu.SemaphoreType.DMA((11,)),
    pltpu.SemaphoreType.DMA((11,)),
]
RING_SEMS = [pltpu.SemaphoreType.DMA((9,)), pltpu.SemaphoreType.DMA((9,))]


def spread_line(where, part, out, core_in, sums, hop, final, send, recv):
    h, x, zl, y, c = where
    right, left, mate = neighbours(where)
    half = ROWS // 2
    low, high = pl.ds(0, half), pl.ds(half, half)

    def mine(core, step):
        return part.at[rows_at((core * 4 + turn(x, step, 4)) * ROWS, ROWS)]

    started = []

    def copy(index, source, view, target):
        item = push(source, view, send.at[index], recv.at[index], target)
        item.start()
        started.append(item)

    def arrived(index, view):
        landed(view, send.at[index], recv.at[index])

    for index, step in enumerate((2, 1, 3, 0)):
        copy(index, mine(1 - c, step), core_in.at[step], mate)
    yield

    def core_sum(step):
        return mine(c, step)[...].astype(jnp.float32) + core_in[step].astype(jnp.float32)

    arrived(0, core_in.at[2])
    sums[2] = core_sum(2).astype(jnp.bfloat16)
    copy(4, sums.at[2, low], hop.at[0], right)
    copy(5, sums.at[2, high], hop.at[1], left)
    arrived(1, core_in.at[1])
    sums[1] = core_sum(1).astype(jnp.bfloat16)
    copy(6, sums.at[1, high], final.at[0, high], right)
    arrived(2, core_in.at[3])
    sums[3] = core_sum(3).astype(jnp.bfloat16)
    copy(7, sums.at[3, low], final.at[1, low], left)
    yield
    arrived(3, core_in.at[0])
    out[...] = core_sum(0)
    arrived(4, hop.at[0])
    sums[1, :half] = (sums[1, :half].astype(jnp.float32) + hop[0].astype(jnp.float32)).astype(
        jnp.bfloat16
    )
    copy(8, sums.at[1, low], final.at[0, low], right)
    arrived(5, hop.at[1])
    sums[3, half:] = (sums[3, half:].astype(jnp.float32) + hop[1].astype(jnp.float32)).astype(
        jnp.bfloat16
    )
    copy(9, sums.at[3, high], final.at[1, high], left)
    yield
    arrived(6, final.at[0, high])
    arrived(7, final.at[1, low])
    yield
    arrived(8, final.at[0, low])
    arrived(9, final.at[1, high])
    out[...] += final[0].astype(jnp.float32) + final[1].astype(jnp.float32)
    for item in started:
        item.wait_send()


def spread_scratch():
    half = ROWS // 2
    return [
        pltpu.VMEM((4, ROWS, D), jnp.bfloat16),
        pltpu.VMEM((4, ROWS, D), jnp.bfloat16),
        pltpu.VMEM((2, half, D), jnp.bfloat16),
        pltpu.VMEM((2, ROWS, D), jnp.bfloat16),
        pltpu.SemaphoreType.DMA((10,)),
        pltpu.SemaphoreType.DMA((10,)),
    ]


def gather_ring(where, own, slot, send, recv):
    h, x, zl, y, c = where
    home = lax.rem(h + c, 2) == 0
    above = device(h, x, zl, turn(y, 1, 4), c)
    below = device(h, x, zl, turn(y, 3, 4), c)
    beside = device(h, x, 1 - zl, y, c)

    def piece(p, step):
        return slot(turn(zl, p, 2), turn(y, step, 4), 0, 2, c)

    def ring(index, view, target):
        push(view, view, send.at[index], recv.at[index], target).start()

    def arrived(index, view):
        landed(view, send.at[index], recv.at[index])

    for d in range(2):
        target = device(turn(h, d, 2), x, zl, y, h)
        args = (own, slot(zl, y, c, 1, h), send.at[d], recv.at[c], target)
        if d == 0:
            move(*args, home)
        else:
            push(*args).start()
    yield
    for d in range(2):
        cc = turn(c, d, 2)
        args = (slot(zl, y, cc, 1, c), send.at[d], recv.at[cc])
        if d == 0:
            moved_in(*args, home)
        else:
            landed(*args)
    ring(2, piece(0, 0), beside)
    ring(3, piece(0, 0), above)
    ring(5, piece(0, 0), below)
    yield
    arrived(2, piece(1, 0))
    ring(4, piece(1, 0), above)
    ring(6, piece(1, 0), below)
    yield
    arrived(3, piece(0, 3))
    ring(7, piece(0, 3), above)
    arrived(6, piece(1, 1))
    ring(8, piece(1, 1), below)
    yield
    arrived(4, piece(1, 3))
    arrived(5, piece(0, 1))
    arrived(7, piece(0, 2))
    arrived(8, piece(1, 2))
    moved_out(own, send.at[0], recv.at[0], beside, home)
    push(own, own, send.at[1], recv.at[1], beside).wait_send()
    for index in range(2, 9):
        push(piece(0, 0), piece(0, 0), send.at[index], recv.at[index], beside).wait_send()


def gather_parts(where, block, send, recv):
    h, x, zl, y, c = where
    pairs = [(j, d) for j in range(4) for d in range(2) if j or d]
    mine = c * 4 + x
    started = []
    for index, (j, d) in enumerate(pairs):
        target = device(h, turn(x, j, 4), zl, y, turn(c, d, 2))
        item = push(block(mine), block(mine), send.at[index], recv.at[mine], target)
        item.start()
        started.append(item)
    yield
    for index, (j, d) in enumerate(pairs):
        other = turn(c, d, 2) * 4 + turn(x, j, 4)
        landed(block(other), send.at[index], recv.at[other])
    for item in started:
        item.wait_send()


def one_after_other(*parts):
    for part in parts:
        yield from part


def swap_in(where, pairs, send, recv):
    h, x, zl, y, c = where
    home = lax.rem(h + c, 2) == 0
    mine = h * 4 + x
    for item, (src, dst) in enumerate(pairs):
        for j in range(4):
            for d in range(2):
                xx, cc = turn(x, j, 4), turn(c, d, 2)
                args = (
                    src.at[rows_at((cc * 4 + xx) * ROWS, ROWS)],
                    dst.at[:, rows_at(mine * 128, 128)],
                    send.at[item, j * 2 + d],
                    recv.at[item, mine],
                    device(c, xx, zl, y, cc),
                )
                if j or d:
                    push(*args).start()
                else:
                    move(*args, home)
    yield
    for item, (src, dst) in enumerate(pairs):
        for j in range(4):
            for d in range(2):
                k = turn(h, d, 2) * 4 + turn(x, j, 4)
                view = dst.at[:, rows_at(k * 128, 128)]
                sems = (send.at[item, j * 2 + d], recv.at[item, k])
                gone = src.at[pl.ds(0, ROWS)]
                other = device(h, x, 1 - zl, y, c)
                if j or d:
                    landed(view, *sems)
                    push(gone, gone, *sems, other).wait_send()
                else:
                    moved_in(view, *sems, home)
                    moved_out(gone, *sems, other, home)


def swap_out(where, pairs, send, recv):
    h, x, zl, y, c = where
    home = lax.rem(h + c, 2) == 0
    mine = c * 4 + x
    for item, (src, dst) in enumerate(pairs):
        for j in range(4):
            for d in range(2):
                hh, xx = turn(h, d, 2), turn(x, j, 4)
                args = (
                    src.at[:, rows_at((hh * 4 + xx) * 128, 128)],
                    dst.at[rows_at(mine * ROWS, ROWS)],
                    send.at[item, j * 2 + d],
                    recv.at[item, mine],
                    device(hh, xx, zl, y, h),
                )
                if j or d:
                    push(*args).start()
                else:
                    move(*args, home)
    yield
    for item, (src, dst) in enumerate(pairs):
        for j in range(4):
            for d in range(2):
                part = turn(c, d, 2) * 4 + turn(x, j, 4)
                view = dst.at[rows_at(part * ROWS, ROWS)]
                sems = (send.at[item, j * 2 + d], recv.at[item, part])
                gone = src.at[:, pl.ds(0, 128)]
                other = device(h, x, 1 - zl, y, c)
                if j or d:
                    landed(view, *sems)
                    push(gone, gone, *sems, other).wait_send()
                else:
                    moved_in(view, *sems, home)
                    moved_out(gone, *sems, other, home)


def scatter_ring(where, rows, depth, out, hop, final, sums, kept, across, pair, last, send, recv):
    h, x, zl, y, c = where
    home = lax.rem(h + c, 2) == 0
    above = device(h, x, zl, turn(y, 1, 4), c)
    below = device(h, x, zl, turn(y, 3, 4), c)
    beside = device(h, x, 1 - zl, y, c)
    kind = hop.dtype

    def piece(p, step):
        return rows((turn(zl, p, 2) * 8 + turn(y, step, 4) * 2) * depth, 2 * depth)

    def wide(value):
        return value.astype(jnp.float32)

    def go(index, src, dst, target):
        push(src, dst, send.at[index], recv.at[index], target).start()

    def come(index, dst):
        landed(dst, send.at[index], recv.at[index])

    go(0, piece(0, 2), hop.at[0], above)
    go(1, piece(1, 2), hop.at[1], below)
    go(2, piece(1, 1), final.at[0, 1], above)
    go(3, piece(0, 3), final.at[1, 0], below)
    yield
    come(0, hop.at[0])
    sums[0] = (wide(piece(0, 1)[...]) + wide(hop[0])).astype(kind)
    go(4, sums.at[0], final.at[0, 0], above)
    come(1, hop.at[1])
    sums[1] = (wide(piece(1, 3)[...]) + wide(hop[1])).astype(kind)
    go(5, sums.at[1], final.at[1, 1], below)
    yield
    come(2, final.at[0, 1])
    come(5, final.at[1, 1])
    across[0] = (wide(piece(1, 0)[...]) + wide(final[0, 1]) + wide(final[1, 1])).astype(kind)
    go(6, across.at[0], across.at[1], beside)
    come(3, final.at[1, 0])
    come(4, final.at[0, 0])
    kept[...] = wide(piece(0, 0)[...]) + wide(final[0, 0]) + wide(final[1, 0])
    yield
    come(6, across.at[1])
    pair[...] = (kept[...] + wide(across[1])).astype(kind)
    for d in range(2):
        cc = turn(c, d, 2)
        args = (
            pair.at[rows_at(cc * depth, depth)],
            last.at[h],
            send.at[7 + d],
            recv.at[7 + h],
            device(c, x, zl, y, cc),
        )
        if d == 0:
            move(*args, home)
        else:
            push(*args).start()
    yield
    for d in range(2):
        hh = turn(h, d, 2)
        args = (last.at[hh], send.at[7 + d], recv.at[7 + hh])
        if d == 0:
            moved_in(*args, home)
        else:
            landed(*args)
    out[...] = wide(last[0]) + wide(last[1])
    for index in range(7):
        push(piece(0, 0), piece(0, 0), send.at[index], recv.at[index], beside).wait_send()
    gone = pair.at[pl.ds(0, depth)]
    moved_out(gone, send.at[7], recv.at[7], beside, home)
    push(gone, gone, send.at[8], recv.at[8], beside).wait_send()


def scatter_scratch(depth, rest, kind):
    both = (2 * depth,) + rest
    return [
        pltpu.VMEM((2,) + both, kind),
        pltpu.VMEM((2, 2) + both, kind),
        pltpu.VMEM((2,) + both, kind),
        pltpu.VMEM(both, jnp.float32),
        pltpu.VMEM((2,) + both, kind),
        pltpu.VMEM(both, kind),
        pltpu.VMEM((2, depth) + rest, kind),
    ] + RING_SEMS


def rows_of(full, depth):
    def slot(zz, yy, cc, count, core):
        return full.at[rows_at((zz * 8 + yy * 2 + cc) * depth, depth * count)]

    return slot


def rows_view(ref):
    return lambda start, count: ref.at[rows_at(start, count)]


ANYWHERE = pl.BlockSpec(memory_space=pl.ANY)
INSIDE = pl.BlockSpec(memory_space=pltpu.VMEM)
DEPTH = D // 16
CHUNK = 512


def call(body, name, number, ins, outs, scratch, args):
    result = pl.pallas_call(
        body,
        out_shape=tuple(shape for shape, _ in outs),
        in_specs=ins,
        out_specs=tuple(spec for _, spec in outs),
        scratch_shapes=scratch,
        compiler_params=pltpu.CompilerParams(
            collective_id=number, has_side_effects=True, vmem_limit_bytes=40 * 2**20
        ),
        name=name,
    )(*args)
    return result


FULL_ROWS = jax.ShapeDtypeStruct((CAP, D), jnp.bfloat16)
FULL_CHUNK = jax.ShapeDtypeStruct((D, CHUNK), jnp.bfloat16)
OWN_CHUNK = jax.ShapeDtypeStruct((DEPTH, CHUNK), jnp.float32)
OWN_ROWS = jax.ShapeDtypeStruct((ROWS, D), jnp.float32)


def gather_rows(rows, weights=None, grads=None):
    if weights is not None:

        def body(src, own, out, full, *sems):
            where = place()
            await_greetings(greet_line(where) + greet_ring(where, True))
            together(
                gather_line(where, src, out, *sems[:3]),
                gather_ring(where, own, rows_of(full, DEPTH), *sems[3:]),
            )

        return call(
            body,
            "gather_rows_weights",
            1,
            [ANYWHERE] * 2,
            [(FULL_ROWS, ANYWHERE), (FULL_CHUNK, ANYWHERE)],
            LINE_SEMS + RING_SEMS,
            (rows, weights),
        )
    if grads is not None:

        def body(src, part, out, own, *scratch):
            where = place()
            await_greetings(greet_line(where) + greet_ring(where, False))
            together(
                scatter_ring(where, rows_view(part), DEPTH, own, *scratch[3:]),
                gather_line(where, src, out, *scratch[:3]),
            )

        return call(
            body,
            "gather_rows_grads",
            2,
            [ANYWHERE, INSIDE],
            [(FULL_ROWS, ANYWHERE), (OWN_CHUNK, INSIDE)],
            LINE_SEMS + scatter_scratch(DEPTH, (CHUNK,), jnp.bfloat16),
            (rows, grads),
        )

    def body(src, out, *sems):
        where = place()
        await_greetings(greet_line(where))
        together(gather_line(where, src, out, *sems))

    return call(body, "gather_rows", 3, [ANYWHERE], [(FULL_ROWS, ANYWHERE)], LINE_SEMS, (rows,))[0]


def spread_rows(part, weights=None, grads=None):
    count = len(spread_scratch())
    if weights is not None:

        def body(part, own, out, full, *scratch):
            where = place()
            await_greetings(greet_line(where) + greet_ring(where, True))
            together(
                spread_line(where, part, out, *scratch[:count]),
                gather_ring(where, own, rows_of(full, DEPTH), *scratch[count:]),
            )

        return call(
            body,
            "spread_rows_weights",
            4,
            [INSIDE, ANYWHERE],
            [(OWN_ROWS, INSIDE), (FULL_CHUNK, ANYWHERE)],
            spread_scratch() + RING_SEMS,
            (part, weights),
        )
    if grads is not None:

        def body(part, grads, out, own, *scratch):
            where = place()
            await_greetings(greet_line(where) + greet_ring(where, False))
            together(
                spread_line(where, part, out, *scratch[:count]),
                scatter_ring(where, rows_view(grads), DEPTH, own, *scratch[count:]),
            )

        return call(
            body,
            "spread_rows_grads",
            5,
            [INSIDE, INSIDE],
            [(OWN_ROWS, INSIDE), (OWN_CHUNK, INSIDE)],
            spread_scratch() + scatter_scratch(DEPTH, (CHUNK,), jnp.bfloat16),
            (part, grads),
        )

    def body(part, out, *scratch):
        where = place()
        await_greetings(greet_line(where))
        together(spread_line(where, part, out, *scratch))

    return call(
        body, "spread_rows", 6, [INSIDE], [(OWN_ROWS, INSIDE)], spread_scratch(), (part,)
    )[0]


def enter_body(
    hid, cot, weights, pack, hid_out, cot_out, full, packs,
    ring_send, ring_recv, pack_send, pack_recv, part_send, part_recv, swap_send, swap_recv,
):
    where = place()
    h, x, zl, y, c = where
    await_greetings(greet_swap(where, True) + greet_ring(where, True) + greet_parts(where))

    def pack_slot(zz, yy, cc, count, core):
        return packs.at[core * 4 + x, pl.ds(zz * 8 + yy * 2 + cc, count)]

    together(
        one_after_other(
            gather_ring(where, pack, pack_slot, pack_send, pack_recv),
            gather_parts(where, lambda part: packs.at[part], part_send, part_recv),
        ),
        gather_ring(where, weights, rows_of(full, DEPTH), ring_send, ring_recv),
        swap_in(where, ((hid, hid_out), (cot, cot_out)), swap_send, swap_recv),
    )


def enter(hidden, cotangent, weights, pack):
    return call(
        enter_body,
        "enter",
        0,
        [ANYWHERE] * 4,
        [
            (OWN_ROWS, ANYWHERE),
            (OWN_ROWS, ANYWHERE),
            (FULL_CHUNK, ANYWHERE),
            (jax.ShapeDtypeStruct((8, 16, 1, 256), jnp.float32), ANYWHERE),
        ],
        RING_SEMS + RING_SEMS
        + [pltpu.SemaphoreType.DMA((7,)), pltpu.SemaphoreType.DMA((8,))]
        + [pltpu.SemaphoreType.DMA((2, 8)), pltpu.SemaphoreType.DMA((2, 8))],
        (hidden, cotangent, weights, pack),
    )


def leave_body(hid, cot, grads, vectors, hid_out, cot_out, out, vector_out, *scratch):
    where = place()
    h, x, zl, y, c = where
    await_greetings(greet_swap(where, False) + greet_ring(where, False) + greet_parts(where))
    ring, rest = scratch[:9], scratch[9:]
    vector_ring, rest = rest[:9], rest[9:]
    taken, total, part_send, part_recv, swap_send, swap_recv = rest

    def vector_parts():
        pairs = [(j, d) for j in range(4) for d in range(2) if j or d]
        mine = c * 4 + x
        started = []
        for index, (j, d) in enumerate(pairs):
            xx, cc = turn(x, j, 4), turn(c, d, 2)
            item = push(
                vectors.at[cc * 4 + xx],
                taken.at[index],
                part_send.at[index],
                part_recv.at[index],
                device(h, xx, zl, y, cc),
            )
            item.start()
            started.append(item)
        yield
        value = vectors[mine]
        for index in range(7):
            landed(taken.at[index], part_send.at[index], part_recv.at[index])
            value = value + taken[index]
        total[...] = value
        for item in started:
            item.wait_send()
        yield from scatter_ring(
            where, lambda start, count: total.at[pl.ds(start, count)], 1, vector_out, *vector_ring
        )

    together(
        scatter_ring(where, rows_view(grads), DEPTH, out, *ring),
        vector_parts(),
        swap_out(where, ((hid, hid_out), (cot, cot_out)), swap_send, swap_recv),
    )


def leave(hidden, grad_hidden, grads, vectors):
    columns = jax.ShapeDtypeStruct((CAP, 128), jnp.float32)
    return call(
        leave_body,
        "leave",
        7,
        [ANYWHERE, ANYWHERE, INSIDE, INSIDE],
        [
            (columns, ANYWHERE),
            (columns, ANYWHERE),
            (OWN_CHUNK, INSIDE),
            (jax.ShapeDtypeStruct((1, 1, 256), jnp.float32), INSIDE),
        ],
        scatter_scratch(DEPTH, (CHUNK,), jnp.bfloat16)
        + scatter_scratch(1, (1, 256), jnp.float32)
        + [
            pltpu.VMEM((7, 16, 1, 256), jnp.float32),
            pltpu.VMEM((16, 1, 256), jnp.float32),
            pltpu.SemaphoreType.DMA((7,)),
            pltpu.SemaphoreType.DMA((7,)),
            pltpu.SemaphoreType.DMA((2, 8)),
            pltpu.SemaphoreType.DMA((2, 8)),
        ],
        (hidden, grad_hidden, grads, vectors),
    )


def gelu_tanh(values):
    return (
        0.5
        * values
        * (1.0 + jnp.tanh(0.7978845608028654 * (values + 0.044715 * values * values * values)))
    )


def dot(left, right):
    return jnp.dot(left, right, preferred_element_type=jnp.float32)


def dot_t(left, right):
    return lax.dot_general(left, right, (((1,), (1,)), ((), ())), preferred_element_type=jnp.float32)


def t_dot(left, right):
    return lax.dot_general(left, right, (((0,), (0,)), ((), ())), preferred_element_type=jnp.float32)


def norm_forward(hidden, gain, shift):
    centred = hidden - jnp.mean(hidden, axis=1, keepdims=True)
    inverse = lax.rsqrt(jnp.mean(centred * centred, axis=1, keepdims=True) + EPS)
    normed = centred * inverse
    return (normed, inverse, (normed * gain + shift).astype(jnp.bfloat16))


def norm_backward(grad_rows, normed, inverse, gain):
    grad_gain = jnp.sum(grad_rows * normed, axis=0)
    grad_shift = jnp.sum(grad_rows, axis=0)
    scaled = grad_rows * gain
    mean_one = jnp.mean(scaled, axis=1, keepdims=True)
    mean_two = jnp.mean(scaled * normed, axis=1, keepdims=True)
    return (inverse * (scaled - mean_one - normed * mean_two), grad_gain, grad_shift)


def block_scores(query_block, key_rows, first_row, segment, slopes, score_scale):
    block_rows = query_block.shape[0]
    row_index = first_row + jnp.arange(block_rows, dtype=jnp.int32)
    columns = jnp.arange(key_rows.shape[0], dtype=jnp.int32)
    offset = (columns[None, :] - row_index[:, None]).astype(jnp.float32)
    scores = (
        jnp.einsum("qhd,khd->hqk", query_block, key_rows, preferred_element_type=jnp.float32)
        * score_scale
    )
    scores = scores + slopes[:, None, None] * offset[None]
    row_segment = lax.dynamic_slice_in_dim(segment, first_row, block_rows)
    allowed = (row_segment[:, None] == segment[None, :]) & (columns[None, :] <= row_index[:, None])
    return jnp.where(allowed[None], scores, NEG)


def attend_forward(query_rows, key_rows, value_rows, segment, slopes, score_scale, block_rows):
    block_count = query_rows.shape[0] // block_rows

    def one_block(block_index):
        first_row = block_index * block_rows
        query_block = lax.dynamic_slice_in_dim(query_rows, first_row, block_rows)
        scores = block_scores(query_block, key_rows, first_row, segment, slopes, score_scale)
        row_max = jnp.max(scores, axis=-1, keepdims=True)
        shifted = jnp.exp(scores - row_max)
        row_total = jnp.sum(shifted, axis=-1, keepdims=True)
        soft_probs = (shifted / row_total).astype(jnp.bfloat16)
        mixed_block = jnp.einsum(
            "hqk,khd->qhd", soft_probs, value_rows, preferred_element_type=jnp.float32
        )
        return (mixed_block.astype(jnp.bfloat16), (row_max + jnp.log(row_total))[..., 0])

    mixed_heads, log_totals = lax.map(one_block, jnp.arange(block_count, dtype=jnp.int32))
    return (mixed_heads.reshape(query_rows.shape), log_totals)


def attend_backward(
    query_rows,
    key_rows,
    value_rows,
    grad_heads,
    log_totals,
    segment,
    slopes,
    score_scale,
    block_rows,
):
    block_count = query_rows.shape[0] // block_rows

    def one_block(carried, block_index):
        grad_keys, grad_values = carried
        first_row = block_index * block_rows
        query_block = lax.dynamic_slice_in_dim(query_rows, first_row, block_rows)
        grad_block = lax.dynamic_slice_in_dim(grad_heads, first_row, block_rows)
        scores = block_scores(query_block, key_rows, first_row, segment, slopes, score_scale)
        soft_probs = jnp.exp(scores - log_totals[block_index][..., None])
        grad_probs = jnp.einsum(
            "qhd,khd->hqk", grad_block, value_rows, preferred_element_type=jnp.float32
        )
        inner_sum = jnp.sum(soft_probs * grad_probs, axis=-1, keepdims=True)
        grad_scores = (soft_probs * (grad_probs - inner_sum)).astype(jnp.bfloat16)
        grad_query = (
            jnp.einsum("hqk,khd->qhd", grad_scores, key_rows, preferred_element_type=jnp.float32)
            * score_scale
        )
        grad_keys = (
            grad_keys
            + jnp.einsum(
                "hqk,qhd->khd", grad_scores, query_block, preferred_element_type=jnp.float32
            )
            * score_scale
        )
        grad_values = grad_values + jnp.einsum(
            "hqk,qhd->khd",
            soft_probs.astype(jnp.bfloat16),
            grad_block,
            preferred_element_type=jnp.float32,
        )
        return ((grad_keys, grad_values), grad_query)

    zero_rows = jnp.zeros(key_rows.shape, jnp.float32)
    (grad_keys, grad_values), grad_queries = lax.scan(
        one_block, (zero_rows, zero_rows), jnp.arange(block_count, dtype=jnp.int32)
    )
    return (grad_queries.reshape(query_rows.shape), grad_keys, grad_values)


def layer_forward(hidden, weights, vectors, segment, slopes, part, cargo):
    (first_gain, first_shift, query_bias, value_bias, out_bias, second_gain, second_shift, down_bias, up_bias) = vectors
    joined_out = weights["joined_out"]
    normed_one, inverse_one, first_rows = norm_forward(hidden, first_gain, first_shift)
    first_full = carry(gather_rows, first_rows, cargo[0])
    joined_rows = dot(first_full, joined_out[:, :384]).reshape(CAP, LOCAL_HEADS, 3, HDIM)
    query_rows = (joined_rows[:, :, 0] + query_bias.reshape(LOCAL_HEADS, HDIM)).astype(jnp.bfloat16)
    key_rows = joined_rows[:, :, 1].astype(jnp.bfloat16)
    value_rows = (joined_rows[:, :, 2] + value_bias.reshape(LOCAL_HEADS, HDIM)).astype(jnp.bfloat16)
    mixed_heads, log_totals = attend_forward(
        query_rows, key_rows, value_rows, segment, slopes, HDIM ** (-0.5), 512
    )
    heads_flat = mixed_heads.reshape(CAP, -1)
    branch = carry(spread_rows, dot_t(heads_flat, joined_out[:, 384:]).astype(jnp.bfloat16), cargo[1])
    middle = hidden + branch + out_bias
    normed_two, inverse_two, second_rows = norm_forward(middle, second_gain, second_shift)
    second_full = carry(gather_rows, second_rows, cargo[2])
    up_rows = dot(second_full, weights["up"]) + up_bias
    activated = gelu_tanh(up_rows).astype(jnp.bfloat16)
    down_rows = carry(spread_rows, dot_t(activated, weights["down"]).astype(jnp.bfloat16), cargo[3])
    saved_rows = (
        normed_one,
        inverse_one,
        first_full,
        query_rows,
        key_rows,
        value_rows,
        log_totals,
        heads_flat,
        normed_two,
        inverse_two,
        second_full,
        up_rows,
        activated,
    )
    return (middle + down_rows + down_bias, saved_rows)


def carry(transfer, rows, cargo):
    if cargo is None:
        return transfer(rows)
    chunk, kept, name = cargo
    result, kept[name] = transfer(rows, weights=chunk)
    return result


def layer_backward(grad_next, weights, vectors, saved_rows, segment, slopes, part, waiting):
    (first_gain, first_shift, query_bias, value_bias, out_bias, second_gain, second_shift, down_bias, up_bias) = vectors
    (
        normed_one,
        inverse_one,
        first_full,
        query_rows,
        key_rows,
        value_rows,
        log_totals,
        heads_flat,
        normed_two,
        inverse_two,
        second_full,
        up_rows,
        activated,
    ) = saved_rows
    joined_out = weights["joined_out"]
    grad_down = grad_next.astype(jnp.bfloat16)
    down_bias_grad = jnp.sum(grad_down.astype(jnp.float32), axis=0)
    if waiting is None:
        grad_down_full, finished = gather_rows(grad_down), None
    else:
        grad_down_full, finished = gather_rows(grad_down, grads=waiting)
    grad_act = dot(grad_down_full, weights["down"])
    down_grad = t_dot(grad_down_full, activated).astype(jnp.bfloat16)
    _, gelu_pull = jax.vjp(gelu_tanh, up_rows)
    grad_up = gelu_pull(grad_act)[0].astype(jnp.bfloat16)
    up_bias_grad = jnp.sum(grad_up.astype(jnp.float32), axis=0)
    up_grad = t_dot(second_full, grad_up).astype(jnp.bfloat16)
    grad_second, down_sum = spread_rows(
        dot_t(grad_up, weights["up"]).astype(jnp.bfloat16), grads=down_grad
    )
    grad_norm_two, second_gain_grad, second_shift_grad = norm_backward(
        grad_second, normed_two, inverse_two, second_gain
    )
    grad_middle = grad_next + grad_norm_two
    grad_branch = grad_middle.astype(jnp.bfloat16)
    out_bias_grad = jnp.sum(grad_branch.astype(jnp.float32), axis=0)
    grad_branch_full, up_sum = gather_rows(grad_branch, grads=up_grad)
    out_grad = t_dot(grad_branch_full, heads_flat).astype(jnp.bfloat16)
    grad_heads = dot(grad_branch_full, joined_out[:, 384:]).astype(jnp.bfloat16)
    grad_heads = grad_heads.reshape(query_rows.shape)
    grad_query, grad_keys, grad_values = attend_backward(
        query_rows,
        key_rows,
        value_rows,
        grad_heads,
        log_totals,
        segment,
        slopes,
        HDIM ** (-0.5),
        512,
    )
    query_low = grad_query.astype(jnp.bfloat16)
    key_low = grad_keys.astype(jnp.bfloat16)
    value_low = grad_values.astype(jnp.bfloat16)
    query_bias_grad = jnp.sum(query_low.astype(jnp.float32), axis=0).reshape(-1)
    value_bias_grad = jnp.sum(value_low.astype(jnp.float32), axis=0).reshape(-1)
    grad_joined = jnp.stack([query_low, key_low, value_low], axis=2).reshape(CAP, -1)
    joined_grad = t_dot(first_full, grad_joined).astype(jnp.bfloat16)
    grad_first = spread_rows(dot_t(grad_joined, joined_out[:, :384]).astype(jnp.bfloat16))
    grad_norm_one, first_gain_grad, first_shift_grad = norm_backward(
        grad_first, normed_one, inverse_one, first_gain
    )
    grad_hidden = grad_middle + grad_norm_one

    def lay(piece, size):
        return lax.dynamic_update_slice(
            jnp.zeros((size,), jnp.float32), piece, (part * piece.shape[0],)
        )

    small = jnp.stack(
        [
            first_gain_grad,
            first_shift_grad,
            lay(query_bias_grad, D),
            lay(value_bias_grad, D),
            out_bias_grad,
            second_gain_grad,
            second_shift_grad,
            down_bias_grad,
        ]
    )
    sums = {"down": down_sum, "up": up_sum}
    return (
        grad_hidden,
        sums,
        jnp.concatenate([joined_grad, out_grad], axis=1),
        finished,
        small,
        lay(up_bias_grad, FF),
    )


def shards(
    hidden_in,
    joined_weight,
    query_bias,
    value_bias,
    out_weight,
    out_bias,
    first_gain,
    first_shift,
    up_weight,
    up_bias,
    down_weight,
    down_bias,
    second_gain,
    second_shift,
    seq_lengths,
    cotangent,
):
    h, x, zl, y, c = place()
    part = c * 4 + x
    small = jnp.stack(
        [
            first_gain,
            first_shift,
            query_bias,
            value_bias,
            out_bias,
            second_gain,
            second_shift,
            down_bias,
        ],
        axis=1,
    )
    pack = jnp.concatenate(
        [
            small.reshape(-1).astype(jnp.float32),
            up_bias.reshape(-1).astype(jnp.float32),
            seq_lengths[0].astype(jnp.float32),
            jnp.zeros((60,), jnp.float32),
        ]
    )
    joined_out = jnp.concatenate([joined_weight, jnp.swapaxes(out_weight, 1, 2)], axis=2)
    down_turned = jnp.swapaxes(down_weight, 1, 2)
    weights = [{} for _ in range(LAYERS)]
    hidden, grad_hidden, weights[0]["joined_out"], packs = enter(
        hidden_in, cotangent, joined_out[0], pack.reshape(1, 1, 256)
    )
    packs = packs.reshape(8, 16, 256)
    small_full = (
        packs[:, :, :128].reshape(8, 16, LAYERS, 8, 8).transpose(2, 3, 0, 1, 4).reshape(LAYERS, 8, D)
    )
    up_full = packs[:, :, 128:192].reshape(8, 16, LAYERS, 32).transpose(2, 0, 1, 3).reshape(LAYERS, FF)
    group_pack = lax.dynamic_index_in_dim(packs[0], zl * 8 + y * 2 + h, 0, keepdims=False)
    seq_ends = jnp.cumsum(group_pack[192:196].astype(jnp.int32))
    positions = jnp.arange(CAP, dtype=jnp.int32)
    segment = jnp.sum((positions[:, None] >= seq_ends[None, :]).astype(jnp.int32), axis=1)
    head_numbers = (part * LOCAL_HEADS + jnp.arange(LOCAL_HEADS, dtype=jnp.int32)).astype(jnp.float32)
    slopes = jnp.exp2(-8.0 * (head_numbers + 1.0) / HEADS)

    def vectors_of(layer):
        def own(vector, size):
            return lax.dynamic_slice_in_dim(vector, part * size, size)

        member = small_full[layer]
        return (
            member[0],
            member[1],
            own(member[2], D // PARTS),
            own(member[3], D // PARTS),
            member[4],
            member[5],
            member[6],
            member[7],
            own(up_full[layer], FF // PARTS),
        )

    to_fetch = [
        [
            (up_weight[0], weights[0], "up"),
            (down_turned[0], weights[0], "down"),
            (joined_out[1], weights[1], "joined_out"),
            (up_weight[1], weights[1], "up"),
        ],
        [(down_turned[1], weights[1], "down"), None, None, None],
    ]
    kept_rows = []
    for layer in range(LAYERS):
        hidden, saved_rows = layer_forward(
            hidden, weights[layer], vectors_of(layer), segment, slopes, part, to_fetch[layer]
        )
        kept_rows.append(saved_rows)
    sums = [None] * LAYERS
    small_grads = [None] * LAYERS
    up_bias_grads = [None] * LAYERS
    waiting = None
    for layer in range(LAYERS - 1, -1, -1):
        grad_hidden, sums[layer], left_over, finished, small_grads[layer], up_bias_grads[layer] = (
            layer_backward(
                grad_hidden,
                weights[layer],
                vectors_of(layer),
                kept_rows[layer],
                segment,
                slopes,
                part,
                waiting,
            )
        )
        if finished is not None:
            sums[layer + 1]["joined_out"] = finished
        waiting = left_over
    small_stack = (
        jnp.stack(small_grads)
        .reshape(LAYERS, 8, 8, 16, 8)
        .transpose(2, 3, 0, 1, 4)
        .reshape(8, 16, 128)
    )
    up_stack = (
        jnp.stack(up_bias_grads)
        .reshape(LAYERS, 8, 16, 32)
        .transpose(1, 2, 0, 3)
        .reshape(8, 16, 64)
    )
    vectors = jnp.concatenate(
        [small_stack, up_stack, jnp.zeros((8, 16, 64), jnp.float32)], axis=2
    ).reshape(8, 16, 1, 256)
    hidden_out, grad_out, sums[0]["joined_out"], vector_sums = leave(
        hidden, grad_hidden, waiting, vectors
    )
    small_sums = vector_sums[0, 0, :128].reshape(LAYERS, 8, 8)
    up_sums = vector_sums[0, 0, 128:192].reshape(LAYERS, 32)
    joined_sums = jnp.stack([sums[layer]["joined_out"] for layer in range(LAYERS)])
    up_weight_sums = jnp.stack([sums[layer]["up"] for layer in range(LAYERS)])
    down_sums = jnp.stack([sums[layer]["down"] for layer in range(LAYERS)])
    return (
        hidden_out,
        grad_out,
        joined_sums[:, :, :384],
        small_sums[:, 2],
        small_sums[:, 3],
        jnp.swapaxes(joined_sums[:, :, 384:], 1, 2),
        small_sums[:, 4],
        small_sums[:, 0],
        small_sums[:, 1],
        up_weight_sums,
        up_sums,
        jnp.swapaxes(down_sums, 1, 2),
        small_sums[:, 7],
        small_sums[:, 5],
        small_sums[:, 6],
    )


def solution(mesh):
    vector = P(None, ("col", "row"))
    return jax.shard_map(
        shards,
        mesh=mesh,
        in_specs=(
            P("row", "col"),
            P(None, "row", "col"),
            vector,
            vector,
            P(None, "col", "row"),
            vector,
            vector,
            vector,
            P(None, "row", "col"),
            vector,
            P(None, "col", "row"),
            vector,
            vector,
            vector,
            P("row", None),
            P("row", "col"),
        ),
        out_specs=(
            P("row", "col"),
            P("row", "col"),
            P(None, "row", "col"),
            vector,
            vector,
            P(None, "col", "row"),
            vector,
            vector,
            vector,
            P(None, "row", "col"),
            vector,
            P(None, "col", "row"),
            vector,
            vector,
            vector,
        ),
        check_vma=False,
    )
```

```python
import functools

import jax
import jax.numpy as jnp
from jax import lax
from jax.experimental import pallas as pl
from jax.experimental.pallas import tpu as pltpu
from jax.sharding import PartitionSpec as P

D = 1024
HEADS = 16
HDIM = 64
FF = 4096
LAYERS = 2
CAP = 1024
PARTS = 8
ROWS = CAP // PARTS
LOCAL_HEADS = HEADS // PARTS
EPS = 1e-05
NEG = -1000000000.0
MESH = pl.DeviceIdType.MESH


def place():
    row = lax.axis_index("row")
    col = lax.axis_index("col")
    return (
        lax.div(col, 4),
        lax.rem(col, 4),
        lax.div(row, 8),
        lax.div(lax.rem(row, 8), 2),
        lax.rem(row, 2),
    )


def device(h, x, zl, y, c):
    return (zl * 8 + y * 2 + c, h * 4 + x)


def turn(value, by, size):
    return lax.rem(value + by, size)


def rows_at(start, size):
    return pl.ds(pl.multiple_of(start, size), size)


def push(src, dst, send_sem, recv_sem, target):
    return pltpu.make_async_remote_copy(
        src_ref=src,
        dst_ref=dst,
        send_sem=send_sem,
        recv_sem=recv_sem,
        device_id=target,
        device_id_type=MESH,
    )


def greet(target):
    pl.semaphore_signal(
        pltpu.get_barrier_semaphore(), inc=1, device_id=target, device_id_type=MESH
    )


def await_greetings(count):
    pl.semaphore_wait(pltpu.get_barrier_semaphore(), count)


def unless(flag, run):
    pl.when(jnp.logical_not(flag))(run)


def together(*parts):
    alive = list(parts)
    while alive:
        alive = [part for part in alive if next(part, alive) is not alive]


def weave(main, *planned):
    count = 0
    waiting = [[part, list(plan)] for part, plan in planned]

    def advance():
        for part, plan in waiting:
            while plan and plan[0] <= count:
                next(part, None)
                plan.pop(0)

    advance()
    for _ in main:
        count += 1
        advance()
    for part, _ in waiting:
        for _ in part:
            pass


def landed(view, send_sem, recv_sem):
    row, col = lax.axis_index("row"), lax.axis_index("col")
    push(view, view, send_sem, recv_sem, (row, lax.rem(col + 1, 8))).wait_recv()


def neighbours(where):
    h, x, zl, y, c = where
    return (
        device(h, turn(x, 1, 4), zl, y, c),
        device(h, turn(x, 3, 4), zl, y, c),
        device(h, x, zl, y, 1 - c),
    )


def greet_line(where):
    for other in neighbours(where):
        greet(other)
    return 3


def greet_ring(where, inward):
    h, x, zl, y, c = where
    home = lax.rem(h + c, 2) == 0
    for d in range(2):
        if inward:
            source = device(c, x, zl, y, turn(c, d, 2))
        else:
            source = device(turn(h, d, 2), x, zl, y, h)
        if d == 0:
            unless(home, functools.partial(greet, source))
        else:
            greet(source)
    for step in (1, 3):
        greet(device(h, x, zl, turn(y, step, 4), c))
    greet(device(h, x, 1 - zl, y, c))
    return 4 + lax.rem(h + c, 2)


def greet_swap(where, inward):
    h, x, zl, y, c = where
    home = lax.rem(h + c, 2) == 0
    for j in range(4):
        for d in range(2):
            if inward:
                source = device(turn(h, d, 2), turn(x, j, 4), zl, y, h)
            else:
                source = device(c, turn(x, j, 4), zl, y, turn(c, d, 2))
            if j == 0 and d == 0:
                unless(home, functools.partial(greet, source))
            else:
                greet(source)
    return 7 + lax.rem(h + c, 2)


def greet_parts(where):
    h, x, zl, y, c = where
    for j in range(4):
        for d in range(2):
            if j or d:
                greet(device(h, turn(x, j, 4), zl, y, turn(c, d, 2)))
    return 7


def move(src, dst, send_sem, recv_sem, target, home):
    unless(home, push(src, dst, send_sem, recv_sem, target).start)
    pl.when(home)(lambda: pltpu.make_async_copy(src, dst, recv_sem).start())


def moved_in(dst, send_sem, recv_sem, home):
    unless(home, functools.partial(landed, dst, send_sem, recv_sem))
    pl.when(home)(lambda: pltpu.make_async_copy(dst, dst, recv_sem).wait())


def moved_out(src, send_sem, recv_sem, target, home):
    unless(home, push(src, src, send_sem, recv_sem, target).wait_send)


def gather_line(where, src, out, own_sem, send, recv, ready):
    h, x, zl, y, c = where
    right, left, mate = neighbours(where)
    half = ROWS // 2

    def span(core, step, first=0, size=ROWS):
        return rows_at((core * 4 + turn(x, step, 4)) * ROWS + first, size)

    def block(*args):
        return out.at[span(*args)]

    started = []

    def copy(index, view, target, source=None):
        source = view if source is None else source
        item = push(source, view, send.at[index], recv.at[index], target)
        item.start()
        started.append(item)

    def arrived(index, view):
        landed(view, send.at[index], recv.at[index])

    low, high = src.at[pl.ds(0, half)], src.at[pl.ds(half, half)]
    copy(0, block(c, 0, 0, half), right, low)
    copy(2, block(c, 0, half, half), left, high)
    copy(1, block(c, 0, half, half), right, high)
    copy(3, block(c, 0, 0, half), left, low)
    copy(4, block(c, 0), mate, src)
    own = pltpu.make_async_copy(src, block(c, 0), own_sem)
    own.start()
    yield
    own.wait()
    ready(span(c, 0))
    arrived(0, block(c, 3, 0, half))
    copy(5, block(c, 3, 0, half), right)
    arrived(2, block(c, 1, half, half))
    copy(6, block(c, 1, half, half), left)
    yield
    arrived(4, block(1 - c, 0))
    ready(span(1 - c, 0))
    arrived(1, block(c, 3, half, half))
    copy(7, block(c, 3), mate)
    arrived(3, block(c, 1, 0, half))
    copy(8, block(c, 1), mate)
    ready(span(c, 3))
    yield
    arrived(5, block(c, 2, 0, half))
    copy(9, block(c, 2, 0, half), mate)
    arrived(6, block(c, 2, half, half))
    copy(10, block(c, 2, half, half), mate)
    ready(span(c, 1))
    ready(span(c, 2))
    yield
    arrived(7, block(1 - c, 3))
    ready(span(1 - c, 3))
    arrived(8, block(1 - c, 1))
    ready(span(1 - c, 1))
    arrived(9, block(1 - c, 2, 0, half))
    arrived(10, block(1 - c, 2, half, half))
    ready(span(1 - c, 2))
    for item in started:
        item.wait_send()


LINE_SEMS = [
    pltpu.SemaphoreType.DMA,
    pltpu.SemaphoreType.DMA((11,)),
    pltpu.SemaphoreType.DMA((11,)),
]
RING_SEMS = [pltpu.SemaphoreType.DMA((9,)), pltpu.SemaphoreType.DMA((9,))]


def spread_line(where, part, out, core_in, sums, hop, final, send, recv):
    h, x, zl, y, c = where
    right, left, mate = neighbours(where)
    half = ROWS // 2
    low, high = pl.ds(0, half), pl.ds(half, half)

    def mine(core, step):
        return part.at[rows_at((core * 4 + turn(x, step, 4)) * ROWS, ROWS)]

    started = []

    def copy(index, source, view, target):
        item = push(source, view, send.at[index], recv.at[index], target)
        item.start()
        started.append(item)

    def arrived(index, view):
        landed(view, send.at[index], recv.at[index])

    for index, step in enumerate((2, 1, 3, 0)):
        copy(index, mine(1 - c, step), core_in.at[step], mate)
    yield

    def core_sum(step):
        return mine(c, step)[...].astype(jnp.float32) + core_in[step].astype(jnp.float32)

    arrived(0, core_in.at[2])
    sums[2] = core_sum(2).astype(jnp.bfloat16)
    copy(4, sums.at[2, low], hop.at[0], right)
    copy(5, sums.at[2, high], hop.at[1], left)
    arrived(1, core_in.at[1])
    sums[1] = core_sum(1).astype(jnp.bfloat16)
    copy(6, sums.at[1, high], final.at[0, high], right)
    arrived(2, core_in.at[3])
    sums[3] = core_sum(3).astype(jnp.bfloat16)
    copy(7, sums.at[3, low], final.at[1, low], left)
    yield
    arrived(3, core_in.at[0])
    out[...] = core_sum(0)
    arrived(4, hop.at[0])
    sums[1, :half] = (sums[1, :half].astype(jnp.float32) + hop[0].astype(jnp.float32)).astype(
        jnp.bfloat16
    )
    copy(8, sums.at[1, low], final.at[0, low], right)
    arrived(5, hop.at[1])
    sums[3, half:] = (sums[3, half:].astype(jnp.float32) + hop[1].astype(jnp.float32)).astype(
        jnp.bfloat16
    )
    copy(9, sums.at[3, high], final.at[1, high], left)
    yield
    arrived(6, final.at[0, high])
    arrived(7, final.at[1, low])
    yield
    arrived(8, final.at[0, low])
    arrived(9, final.at[1, high])
    out[...] += final[0].astype(jnp.float32) + final[1].astype(jnp.float32)
    for item in started:
        item.wait_send()


def spread_scratch():
    half = ROWS // 2
    return [
        pltpu.VMEM((4, ROWS, D), jnp.bfloat16),
        pltpu.VMEM((4, ROWS, D), jnp.bfloat16),
        pltpu.VMEM((2, half, D), jnp.bfloat16),
        pltpu.VMEM((2, ROWS, D), jnp.bfloat16),
        pltpu.SemaphoreType.DMA((10,)),
        pltpu.SemaphoreType.DMA((10,)),
    ]


def gather_ring(where, own, slot, send, recv):
    h, x, zl, y, c = where
    home = lax.rem(h + c, 2) == 0
    above = device(h, x, zl, turn(y, 1, 4), c)
    below = device(h, x, zl, turn(y, 3, 4), c)
    beside = device(h, x, 1 - zl, y, c)

    def piece(p, step):
        return slot(turn(zl, p, 2), turn(y, step, 4), 0, 2, c)

    def ring(index, view, target):
        push(view, view, send.at[index], recv.at[index], target).start()

    def arrived(index, view):
        landed(view, send.at[index], recv.at[index])

    for d in range(2):
        target = device(turn(h, d, 2), x, zl, y, h)
        args = (own, slot(zl, y, c, 1, h), send.at[d], recv.at[c], target)
        if d == 0:
            move(*args, home)
        else:
            push(*args).start()
    yield
    for d in range(2):
        cc = turn(c, d, 2)
        args = (slot(zl, y, cc, 1, c), send.at[d], recv.at[cc])
        if d == 0:
            moved_in(*args, home)
        else:
            landed(*args)
    ring(2, piece(0, 0), beside)
    ring(3, piece(0, 0), above)
    ring(5, piece(0, 0), below)
    yield
    arrived(2, piece(1, 0))
    ring(4, piece(1, 0), above)
    ring(6, piece(1, 0), below)
    yield
    arrived(3, piece(0, 3))
    ring(7, piece(0, 3), above)
    arrived(6, piece(1, 1))
    ring(8, piece(1, 1), below)
    yield
    arrived(4, piece(1, 3))
    arrived(5, piece(0, 1))
    arrived(7, piece(0, 2))
    arrived(8, piece(1, 2))
    moved_out(own, send.at[0], recv.at[0], beside, home)
    push(own, own, send.at[1], recv.at[1], beside).wait_send()
    for index in range(2, 9):
        push(piece(0, 0), piece(0, 0), send.at[index], recv.at[index], beside).wait_send()


def finish(part):
    for _ in part:
        pass


def gather_vectors(where, pack, vectors, ends, taken, mine, near, send, recv, part_send, part_recv):
    h, x, zl, y, c = where
    home = lax.rem(h + c, 2) == 0
    beside = device(h, x, 1 - zl, y, c)
    started = []

    def go(*args):
        item = push(*args)
        item.start()
        started.append(item)

    for d in range(2):
        args = (pack, taken.at[c], send.at[d], recv.at[c], device(turn(h, d, 2), x, zl, y, h))
        if d == 0:
            move(*args, home)
        else:
            go(*args)
    yield
    for d in range(2):
        cc = turn(c, d, 2)
        args = (taken.at[cc], send.at[d], recv.at[cc])
        if d == 0:
            moved_in(*args, home)
        else:
            landed(*args)
    mine[...] = taken[0] + taken[1]
    ends[...] = taken[h, 24:32, :]
    for index in range(1, 8):
        dz, dy = divmod(index, 4)
        other = device(h, x, turn(zl, dz, 2), turn(y, dy, 4), c)
        go(mine, near.at[index - 1], send.at[1 + index], recv.at[1 + index], other)
    yield
    value = mine[...]
    for index in range(1, 8):
        landed(near.at[index - 1], send.at[1 + index], recv.at[1 + index])
        value = value + near[index - 1]

    def block(part):
        return vectors.at[:, rows_at(part * 128, 128)]

    part = c * 4 + x
    vectors[:, rows_at(part * 128, 128)] = value
    pairs = [(j, d) for j in range(4) for d in range(2) if j or d]
    for index, (j, d) in enumerate(pairs):
        other = device(h, turn(x, j, 4), zl, y, turn(c, d, 2))
        go(block(part), block(part), part_send.at[index], part_recv.at[part], other)
    yield
    for index, (j, d) in enumerate(pairs):
        other = turn(c, d, 2) * 4 + turn(x, j, 4)
        landed(block(other), part_send.at[index], part_recv.at[other])
    for item in started:
        item.wait_send()
    moved_out(pack, send.at[0], recv.at[0], beside, home)


def greet_near(where):
    h, x, zl, y, c = where
    greet(device(h, x, zl, turn(y, 2, 4), c))
    for step in (1, 2, 3):
        greet(device(h, x, 1 - zl, turn(y, step, 4), c))
    return 4


def swap_in(where, pairs, send, recv):
    h, x, zl, y, c = where
    home = lax.rem(h + c, 2) == 0
    mine = h * 4 + x
    for item, (src, dst) in enumerate(pairs):
        for j in range(4):
            for d in range(2):
                xx, cc = turn(x, j, 4), turn(c, d, 2)
                args = (
                    src.at[rows_at((cc * 4 + xx) * ROWS, ROWS)],
                    dst.at[:, rows_at(mine * 128, 128)],
                    send.at[item, j * 2 + d],
                    recv.at[item, mine],
                    device(c, xx, zl, y, cc),
                )
                if j or d:
                    push(*args).start()
                else:
                    move(*args, home)
    yield
    for item, (src, dst) in enumerate(pairs):
        for j in range(4):
            for d in range(2):
                k = turn(h, d, 2) * 4 + turn(x, j, 4)
                view = dst.at[:, rows_at(k * 128, 128)]
                sems = (send.at[item, j * 2 + d], recv.at[item, k])
                gone = src.at[pl.ds(0, ROWS)]
                other = device(h, x, 1 - zl, y, c)
                if j or d:
                    landed(view, *sems)
                    push(gone, gone, *sems, other).wait_send()
                else:
                    moved_in(view, *sems, home)
                    moved_out(gone, *sems, other, home)


def swap_out(where, pairs, send, recv):
    h, x, zl, y, c = where
    home = lax.rem(h + c, 2) == 0
    mine = c * 4 + x
    for item, (src, dst) in enumerate(pairs):
        for j in range(4):
            for d in range(2):
                hh, xx = turn(h, d, 2), turn(x, j, 4)
                args = (
                    src.at[:, rows_at((hh * 4 + xx) * 128, 128)],
                    dst.at[rows_at(mine * ROWS, ROWS)],
                    send.at[item, j * 2 + d],
                    recv.at[item, mine],
                    device(hh, xx, zl, y, h),
                )
                if j or d:
                    push(*args).start()
                else:
                    move(*args, home)
    yield
    for item, (src, dst) in enumerate(pairs):
        for j in range(4):
            for d in range(2):
                part = turn(c, d, 2) * 4 + turn(x, j, 4)
                view = dst.at[rows_at(part * ROWS, ROWS)]
                sems = (send.at[item, j * 2 + d], recv.at[item, part])
                gone = src.at[:, pl.ds(0, 128)]
                other = device(h, x, 1 - zl, y, c)
                if j or d:
                    landed(view, *sems)
                    push(gone, gone, *sems, other).wait_send()
                else:
                    moved_in(view, *sems, home)
                    moved_out(gone, *sems, other, home)


def scatter_ring(where, rows, depth, out, hop, final, sums, kept, across, pair, last, send, recv):
    h, x, zl, y, c = where
    home = lax.rem(h + c, 2) == 0
    above = device(h, x, zl, turn(y, 1, 4), c)
    below = device(h, x, zl, turn(y, 3, 4), c)
    beside = device(h, x, 1 - zl, y, c)
    kind = hop.dtype

    def piece(p, step):
        return rows((turn(zl, p, 2) * 8 + turn(y, step, 4) * 2) * depth, 2 * depth)

    def wide(value):
        return value.astype(jnp.float32)

    def go(index, src, dst, target):
        push(src, dst, send.at[index], recv.at[index], target).start()

    def come(index, dst):
        landed(dst, send.at[index], recv.at[index])

    go(0, piece(0, 2), hop.at[0], above)
    go(1, piece(1, 2), hop.at[1], below)
    go(2, piece(1, 1), final.at[0, 1], above)
    go(3, piece(0, 3), final.at[1, 0], below)
    yield
    come(0, hop.at[0])
    sums[0] = (wide(piece(0, 1)[...]) + wide(hop[0])).astype(kind)
    go(4, sums.at[0], final.at[0, 0], above)
    come(1, hop.at[1])
    sums[1] = (wide(piece(1, 3)[...]) + wide(hop[1])).astype(kind)
    go(5, sums.at[1], final.at[1, 1], below)
    yield
    come(2, final.at[0, 1])
    come(5, final.at[1, 1])
    across[0] = (wide(piece(1, 0)[...]) + wide(final[0, 1]) + wide(final[1, 1])).astype(kind)
    go(6, across.at[0], across.at[1], beside)
    come(3, final.at[1, 0])
    come(4, final.at[0, 0])
    kept[...] = wide(piece(0, 0)[...]) + wide(final[0, 0]) + wide(final[1, 0])
    yield
    come(6, across.at[1])
    pair[...] = (kept[...] + wide(across[1])).astype(kind)
    for d in range(2):
        cc = turn(c, d, 2)
        args = (
            pair.at[rows_at(cc * depth, depth)],
            last.at[h],
            send.at[7 + d],
            recv.at[7 + h],
            device(c, x, zl, y, cc),
        )
        if d == 0:
            move(*args, home)
        else:
            push(*args).start()
    yield
    for d in range(2):
        hh = turn(h, d, 2)
        args = (last.at[hh], send.at[7 + d], recv.at[7 + hh])
        if d == 0:
            moved_in(*args, home)
        else:
            landed(*args)
    out[...] = wide(last[0]) + wide(last[1])
    for index in range(7):
        push(piece(0, 0), piece(0, 0), send.at[index], recv.at[index], beside).wait_send()
    gone = pair.at[pl.ds(0, depth)]
    moved_out(gone, send.at[7], recv.at[7], beside, home)
    push(gone, gone, send.at[8], recv.at[8], beside).wait_send()


def scatter_scratch(depth, rest, kind):
    both = (2 * depth,) + rest
    return [
        pltpu.VMEM((2,) + both, kind),
        pltpu.VMEM((2, 2) + both, kind),
        pltpu.VMEM((2,) + both, kind),
        pltpu.VMEM(both, jnp.float32),
        pltpu.VMEM((2,) + both, kind),
        pltpu.VMEM(both, kind),
        pltpu.VMEM((2, depth) + rest, kind),
    ] + RING_SEMS


def rows_of(full, depth):
    def slot(zz, yy, cc, count, core):
        return full.at[rows_at((zz * 8 + yy * 2 + cc) * depth, depth * count)]

    return slot


def rows_view(ref):
    return lambda start, count: ref.at[rows_at(start, count)]


ANYWHERE = pl.BlockSpec(memory_space=pl.ANY)
INSIDE = pl.BlockSpec(memory_space=pltpu.VMEM)
DEPTH = D // 16
CHUNK = 512
PAIR = 2 * HDIM
TILE = 256
VMEM_BYTES = 24 * 2**20

ROWS_LOW = jax.ShapeDtypeStruct((ROWS, D), jnp.bfloat16)
ROWS_WIDE = jax.ShapeDtypeStruct((ROWS, D), jnp.float32)
FULL_ROWS = jax.ShapeDtypeStruct((CAP, D), jnp.bfloat16)
FULL_CHUNK = jax.ShapeDtypeStruct((D, CHUNK), jnp.bfloat16)
OWN_CHUNK = jax.ShapeDtypeStruct((DEPTH, CHUNK), jnp.float32)
SMALL = jax.ShapeDtypeStruct((8, D), jnp.float32)
SMALL_OWN = jax.ShapeDtypeStruct((8, 128), jnp.float32)


def of(shape, kind=jnp.bfloat16):
    return jax.ShapeDtypeStruct(shape, kind)


def call(body, name, number, ins, outs, scratch, args):
    return pl.pallas_call(
        body,
        out_shape=tuple(shape for shape, _ in outs),
        in_specs=ins,
        out_specs=tuple(spec for _, spec in outs),
        scratch_shapes=scratch,
        compiler_params=pltpu.CompilerParams(
            collective_id=number, has_side_effects=True, vmem_limit_bytes=VMEM_BYTES
        ),
        name=name,
    )(*args)


def dot(left, right):
    return jnp.dot(left, right, preferred_element_type=jnp.float32)


def dot_t(left, right):
    return lax.dot_general(left, right, (((1,), (1,)), ((), ())), preferred_element_type=jnp.float32)


def t_dot(left, right):
    return lax.dot_general(left, right, (((0,), (0,)), ((), ())), preferred_element_type=jnp.float32)


def low(value):
    return value.astype(jnp.bfloat16)


def wide(value):
    return value.astype(jnp.float32)


def normed_of(values):
    centred = values - jnp.mean(values, axis=1, keepdims=True)
    inverse = lax.rsqrt(jnp.mean(centred * centred, axis=1, keepdims=True) + EPS)
    return centred * inverse, inverse


def norm_back(grad_rows, values, gain):
    normed, inverse = normed_of(values)
    grad_gain = jnp.sum(grad_rows * normed, axis=0, keepdims=True)
    grad_shift = jnp.sum(grad_rows, axis=0, keepdims=True)
    scaled = grad_rows * gain
    mean_one = jnp.mean(scaled, axis=1, keepdims=True)
    mean_two = jnp.mean(scaled * normed, axis=1, keepdims=True)
    return grad_gain, grad_shift, inverse * (scaled - mean_one - normed * mean_two)


def head_masks():
    first = lax.broadcasted_iota(jnp.int32, (1, PAIR), 1) < HDIM
    one = first.astype(jnp.float32)
    return one, 1.0 - one


def side_by_side(*parts):
    alive = list(parts)
    while alive:
        alive = [part for part in alive if next(part, alive) is not alive]
        yield


def weights_cargo(where, count, owns, fulls, sems, plan):
    return [
        (gather_ring(where, owns[i], rows_of(fulls[i], DEPTH), *sems[2 * i : 2 * i + 2]), plan)
        for i in range(count)
    ]


def grads_cargo(where, count, parts, owns, scratch, plan):
    return [
        (scatter_ring(where, rows_view(parts[i]), DEPTH, owns[i], *scratch[9 * i : 9 * i + 9]), plan)
        for i in range(count)
    ]


SWAP_SEMS = [pltpu.SemaphoreType.DMA((1, 8)), pltpu.SemaphoreType.DMA((1, 8))]
COLUMNS = jax.ShapeDtypeStruct((CAP, 128), jnp.float32)
ROW_SCRATCH = pltpu.VMEM((ROWS, D), jnp.bfloat16)
COLUMN_SCRATCH = pltpu.VMEM((CAP, 128), jnp.bfloat16)


PROBS = (2, TILE, TILE * 10)


def probs_at(tile):
    first = TILE * tile * (tile + 1) // 2
    return slice(first, first + TILE * (tile + 1))


def vector_of(vectors, layer, index):
    return vectors[8 * layer + index : 8 * layer + index + 1, :]


def own_vector(vectors, row, part):
    return vectors[row : row + 1, rows_at(part * 128, 128)]


def up_bias_of(vectors, layer, part):
    first = 16 + 4 * layer
    return jnp.concatenate([own_vector(vectors, first + i, part) for i in range(4)], axis=1)


def join_rows(rows, full, weights, qkv, vectors, layer, part):
    joined = dot(full[rows, :], weights[:, : 3 * PAIR])
    query_bias = own_vector(vectors, 8 * layer + 2, part)
    value_bias = own_vector(vectors, 8 * layer + 3, part)
    qkv[rows, :PAIR] = low((joined[:, :PAIR] + query_bias) * HDIM ** (-0.5))
    qkv[rows, PAIR : 2 * PAIR] = low(joined[:, PAIR : 2 * PAIR])
    qkv[rows, 2 * PAIR :] = low(joined[:, 2 * PAIR :] + value_bias)


def segments(ends, places):
    bound = 0.0
    found = jnp.zeros(places.shape, jnp.int32)
    for slot in range(4):
        bound = bound + ends[0:1, slot : slot + 1]
        found = found + (places >= bound).astype(jnp.int32)
    return found


def attend_tile(tile, qkv, ends, part, probs):
    masks = head_masks()
    rows, keys = slice(tile * TILE, (tile + 1) * TILE), (tile + 1) * TILE
    query = wide(qkv[rows, :PAIR])
    key, value = qkv[:keys, PAIR : 2 * PAIR], qkv[:keys, 2 * PAIR :]
    row_places = wide(tile * TILE + lax.broadcasted_iota(jnp.int32, (TILE, 1), 0))
    key_places = wide(lax.broadcasted_iota(jnp.int32, (1, keys), 1))
    offset = key_places - row_places
    allowed = (segments(ends, row_places) == segments(ends, key_places)) & (offset <= 0.0)
    mixed = 0.0
    for head in range(2):
        number = wide(jnp.full((1, 128), part * LOCAL_HEADS + head, jnp.int32))
        slope = jnp.exp2(-8.0 * (number + 1.0) / HEADS)
        scores = dot_t(low(query * masks[head]), key)
        scores = scores + slope[:, :1] * offset
        scores = jnp.where(allowed, scores, NEG)
        shifted = jnp.exp(scores - jnp.max(scores, axis=1, keepdims=True))
        soft = low(shifted / jnp.sum(shifted, axis=1, keepdims=True))
        probs[head, :, probs_at(tile)] = soft
        mixed = mixed + dot(soft, value) * masks[head]
    return low(mixed)


VECTORS = jax.ShapeDtypeStruct((32, D), jnp.float32)
ENDS = jax.ShapeDtypeStruct((8, 128), jnp.float32)
ATTEND_OUTS = [
    (FULL_ROWS, INSIDE),
    (of((CAP, 3 * PAIR)), INSIDE),
    (of(PROBS), INSIDE),
    (of((CAP, PAIR)), INSIDE),
    (ROWS_WIDE, INSIDE),
]


def enter_attend(columns, pack, joined, chunks):
    n = len(chunks)

    def body(columns, pack, joined, *rest):
        owns, rest = rest[:n], rest[n:]
        (vectors, ends, hidden, weights, full, qkv, probs, heads, middle), rest = rest[:9], rest[9:]
        fulls, rest = rest[:n], rest[n:]
        (columns_low, rows_low, first, part, taken, mine, near), rest = rest[:7], rest[7:]
        line, rest = rest[:3], rest[3:]
        spread, rest = rest[:6], rest[6:]
        swap_sems, rest = rest[:2], rest[2:]
        ring_sems, rest = rest[:2], rest[2:]
        sems, pack_sems = rest[: 2 * n], rest[2 * n :]
        where = place()
        h, x, zl, y, c = where
        await_greetings(
            greet_ring(where, True) + greet_parts(where) + greet_swap(where, True) + greet_near(where)
        )
        number = c * 4 + x
        columns_low[...] = low(columns[...])
        packs = gather_vectors(where, pack, vectors, ends, taken, mine, near, *pack_sems)
        swap = swap_in(where, ((columns_low, rows_low),), *swap_sems)
        ring = gather_ring(where, joined, rows_of(weights, DEPTH), *ring_sems)
        next(packs)
        next(swap)
        next(ring)
        next(packs)
        next(ring)
        next(packs)
        next(ring)
        finish(packs)
        finish(swap)
        hidden[...] = wide(rows_low[...])

        def main():
            normed, _ = normed_of(hidden[...])
            first[...] = low(normed * vector_of(vectors, 0, 0) + vector_of(vectors, 0, 1))
            yield from gather_line(where, first, full, *line, lambda rows: None)
            finish(ring)
            for tile in range(CAP // TILE):
                join_rows(slice(tile * TILE, (tile + 1) * TILE), full, weights, qkv, vectors, 0, number)
            for tile in range(CAP // TILE):
                rows = slice(tile * TILE, (tile + 1) * TILE)
                heads[rows, :] = attend_tile(tile, qkv, ends, number, probs)
                part[rows, :] = low(dot_t(heads[rows, :], weights[:, 3 * PAIR :]))
                yield
            yield from spread_line(where, part, middle, *spread)
            middle[...] = middle[...] + hidden[...] + vector_of(vectors, 0, 4)

        weave(main(), (ring, (2,)), *weights_cargo(where, n, owns, fulls, sems, (1, 4, 6, 10)))

    tile = (32, 128)
    return call(
        body,
        "enter_attend",
        0,
        [INSIDE] * (3 + n),
        [(VECTORS, INSIDE), (ENDS, INSIDE), (ROWS_WIDE, INSIDE), (FULL_CHUNK, INSIDE)]
        + ATTEND_OUTS
        + [(FULL_CHUNK, INSIDE)] * n,
        [
            COLUMN_SCRATCH,
            ROW_SCRATCH,
            ROW_SCRATCH,
            pltpu.VMEM((CAP, D), jnp.bfloat16),
            pltpu.VMEM((2,) + tile, jnp.float32),
            pltpu.VMEM(tile, jnp.float32),
            pltpu.VMEM((7,) + tile, jnp.float32),
        ]
        + LINE_SEMS
        + spread_scratch()
        + SWAP_SEMS
        + RING_SEMS * (1 + n)
        + [
            pltpu.SemaphoreType.DMA((9,)),
            pltpu.SemaphoreType.DMA((9,)),
            pltpu.SemaphoreType.DMA((7,)),
            pltpu.SemaphoreType.DMA((8,)),
        ],
        (columns, pack, joined, *chunks),
    )


def attend_forward(layer, number, hidden, vectors, ends, weights, chunks, columns):
    n = len(chunks)

    def body(hidden, vectors, ends, weights, *rest):
        owns, rest = rest[:n], rest[n:]
        (columns, full, qkv, probs, heads, middle), rest = rest[:6], rest[6:]
        fulls, rest = rest[:n], rest[n:]
        (swapped, first, part), rest = rest[:3], rest[3:]
        line, rest = rest[:3], rest[3:]
        spread, rest = rest[:6], rest[6:]
        sems, rest = rest[: 2 * n], rest[2 * n :]
        columns_low, *swap_sems = rest
        where = place()
        h, x, zl, y, c = where
        await_greetings(greet_line(where) + greet_ring(where, True) + greet_swap(where, True))
        part_number = c * 4 + x
        columns_low[...] = low(columns[...])

        def ready(rows):
            join_rows(rows, full, weights, qkv, vectors, layer, part_number)

        def main():
            normed, _ = normed_of(hidden[...])
            first[...] = low(normed * vector_of(vectors, layer, 0) + vector_of(vectors, layer, 1))
            yield from gather_line(where, first, full, *line, ready)
            for tile in range(CAP // TILE):
                rows = slice(tile * TILE, (tile + 1) * TILE)
                heads[rows, :] = attend_tile(tile, qkv, ends, part_number, probs)
                part[rows, :] = low(dot_t(heads[rows, :], weights[:, 3 * PAIR :]))
                yield
            yield from spread_line(where, part, middle, *spread)
            middle[...] = middle[...] + hidden[...] + vector_of(vectors, layer, 4)

        weave(
            main(),
            *weights_cargo(where, n, owns, fulls, sems, (0, 2, 4, 8)),
            (swap_in(where, ((columns_low, swapped),), *swap_sems), (4,)),
        )

    return call(
        body,
        "attend_forward",
        number,
        [INSIDE] * (5 + n),
        ATTEND_OUTS + [(FULL_CHUNK, INSIDE)] * n + [(ROWS_LOW, INSIDE)],
        [ROW_SCRATCH, pltpu.VMEM((CAP, D), jnp.bfloat16)]
        + LINE_SEMS
        + spread_scratch()
        + RING_SEMS * n
        + [COLUMN_SCRATCH]
        + SWAP_SEMS,
        (hidden, vectors, ends, weights, *chunks, columns),
    )


def gelu_pair(values):
    square = values * values
    bent = jnp.tanh(0.7978845608028654 * values * (1.0 + 0.044715 * square))
    half = 0.5 * (1.0 + bent)
    bend = 0.7978845608028654 * (1.0 + 3.0 * 0.044715 * square)
    return low(values * half), low(half + 0.5 * values * (1.0 - bent * bent) * bend)


def feed_forward(layer, number, middle, vectors, up, down, chunks):
    n = len(chunks)

    def body(middle, vectors, up, down, *rest):
        owns, rest = rest[:n], rest[n:]
        (full, activated, slope, hidden), rest = rest[:4], rest[4:]
        fulls, rest = rest[:n], rest[n:]
        (second, part), rest = rest[:2], rest[2:]
        line, rest = rest[:3], rest[3:]
        spread, sems = rest[:6], rest[6:]
        where = place()
        h, x, zl, y, c = where
        count = greet_line(where)
        if n:
            count = count + greet_ring(where, True)
        await_greetings(count)
        bias = up_bias_of(vectors, layer, c * 4 + x)

        def vector(index):
            return vector_of(vectors, layer, index)

        def ready(rows):
            values = dot(full[rows, :], up[...]) + bias
            active, slope[rows, :] = gelu_pair(values)
            activated[rows, :] = active
            part[rows, :] = low(dot_t(active, down[...]))

        def main():
            normed, _ = normed_of(middle[...])
            second[...] = low(normed * vector(5) + vector(6))
            yield from gather_line(where, second, full, *line, ready)
            yield from spread_line(where, part, hidden, *spread)
            hidden[...] = hidden[...] + middle[...] + vector(7)

        weave(main(), *weights_cargo(where, n, owns, fulls, sems, (0, 2, 5, 7)))

    return call(
        body,
        "feed_forward",
        number,
        [INSIDE] * (4 + n),
        [
            (FULL_ROWS, INSIDE),
            (of((CAP, CHUNK)), INSIDE),
            (of((CAP, CHUNK)), INSIDE),
            (ROWS_WIDE, INSIDE),
        ]
        + [(FULL_CHUNK, INSIDE)] * n,
        [pltpu.VMEM((ROWS, D), jnp.bfloat16), pltpu.VMEM((CAP, D), jnp.bfloat16)]
        + LINE_SEMS
        + spread_scratch()
        + RING_SEMS * n,
        (middle, vectors, up, down, *chunks),
    )


def feed_both(layer, number, middle, vectors, up, down, cotangent):
    def body(
        middle, vectors, up, down, cotangent,
        hidden, grad_middle, down_grad, up_grad, small, small_own,
        second, second_full, activated, slope, part, full, grad_up, grad_part, *rest,
    ):
        line, rest = rest[:3], rest[3:]
        grad_line, rest = rest[:3], rest[3:]
        spread, grad_spread = rest[:6], rest[6:]
        where = place()
        h, x, zl, y, c = where
        await_greetings(greet_line(where))
        bias = up_bias_of(vectors, layer, c * 4 + x)

        def vector(index):
            return vector_of(vectors, layer, index)

        def ready(rows):
            values = dot(second_full[rows, :], up[...]) + bias
            activated[rows, :], slope[rows, :] = gelu_pair(values)
            part[rows, :] = low(dot_t(activated[rows, :], down[...]))

        def ready_back(rows):
            grad_low = low(dot(full[rows, :], down[...]) * wide(slope[rows, :]))
            grad_up[rows, :] = grad_low
            grad_part[rows, :] = low(dot_t(grad_low, up[...]))

        def weight_grads():
            for tile in range(D // TILE):
                columns = slice(tile * TILE, (tile + 1) * TILE)
                down_grad[columns, :] = low(t_dot(full[:, columns], activated[...]))
                up_grad[columns, :] = low(t_dot(second_full[:, columns], grad_up[...]))
                if tile % 2:
                    yield
            total = jnp.sum(wide(grad_up[...]), axis=0, keepdims=True)
            small_own[...] = jnp.zeros_like(small_own)
            for index in range(CHUNK // 128):
                small_own[index : index + 1, :] = total[:, index * 128 : (index + 1) * 128]

        normed, _ = normed_of(middle[...])
        second[...] = low(normed * vector(5) + vector(6))
        forth = gather_line(where, second, second_full, *line, ready)
        back = gather_line(where, cotangent, full, *grad_line, ready_back)
        next(forth)
        next(forth)
        next(back)
        finish(forth)
        spread_forth = spread_line(where, part, hidden, *spread)
        next(spread_forth)
        next(back)
        next(spread_forth)
        finish(back)
        spread_back = spread_line(where, grad_part, grad_middle, *grad_spread)
        next(spread_back)
        next(spread_forth)
        next(spread_back)
        finish(spread_forth)
        hidden[...] = hidden[...] + middle[...] + vector(7)
        finish(side_by_side(spread_back, weight_grads()))
        grad_next = wide(cotangent[...])
        gain, shift, grad = norm_back(grad_middle[...], middle[...], vector(5))
        small[...] = jnp.zeros_like(small)
        small[0:1, :] = gain
        small[1:2, :] = shift
        small[2:3, :] = jnp.sum(grad_next, axis=0, keepdims=True)
        grad_middle[...] = grad_next + grad

    return call(
        body,
        "feed_both",
        number,
        [INSIDE] * 5,
        [
            (ROWS_WIDE, INSIDE),
            (ROWS_WIDE, INSIDE),
            (FULL_CHUNK, INSIDE),
            (FULL_CHUNK, INSIDE),
            (SMALL, INSIDE),
            (SMALL_OWN, INSIDE),
        ],
        [
            ROW_SCRATCH,
            pltpu.VMEM((CAP, D), jnp.bfloat16),
            pltpu.VMEM((CAP, CHUNK), jnp.bfloat16),
            pltpu.VMEM((CAP, CHUNK), jnp.bfloat16),
            pltpu.VMEM((CAP, D), jnp.bfloat16),
            pltpu.VMEM((CAP, D), jnp.bfloat16),
            pltpu.VMEM((CAP, CHUNK), jnp.bfloat16),
            pltpu.VMEM((CAP, D), jnp.bfloat16),
        ]
        + LINE_SEMS * 2
        + spread_scratch() * 2,
        (middle, vectors, up, down, cotangent),
    )


def feed_backward(layer, number, grad_next, vectors, middle, up, down, second_full, activated, slope, chunks):
    n = len(chunks)

    def body(grad_next, vectors, middle, up, down, second_full, activated, slope, *rest):
        parts, rest = rest[:n], rest[n:]
        (grad_middle, down_grad, up_grad, small, small_own), rest = rest[:5], rest[5:]
        owns, rest = rest[:n], rest[n:]
        (rows_low, full, grad_up, part), rest = rest[:4], rest[4:]
        line, rest = rest[:3], rest[3:]
        spread, rest = rest[:6], rest[6:]
        where = place()
        count = greet_line(where)
        if n:
            count = count + greet_ring(where, False)
        await_greetings(count)

        def ready(rows):
            grad_act = dot(full[rows, :], down[...])
            grad_low = low(grad_act * wide(slope[rows, :]))
            grad_up[rows, :] = grad_low
            part[rows, :] = low(dot_t(grad_low, up[...]))

        def weight_grads():
            for tile in range(D // TILE):
                columns = slice(tile * TILE, (tile + 1) * TILE)
                down_grad[columns, :] = low(t_dot(full[:, columns], activated[...]))
                up_grad[columns, :] = low(t_dot(second_full[:, columns], grad_up[...]))
                if tile % 2:
                    yield
            total = jnp.sum(wide(grad_up[...]), axis=0, keepdims=True)
            small_own[...] = jnp.zeros_like(small_own)
            for index in range(CHUNK // 128):
                small_own[index : index + 1, :] = total[:, index * 128 : (index + 1) * 128]

        def main():
            rows_low[...] = low(grad_next[...])
            yield from gather_line(where, rows_low, full, *line, ready)
            yield from side_by_side(
                spread_line(where, part, grad_middle, *spread), weight_grads()
            )
            gain, shift, grad = norm_back(
                grad_middle[...], middle[...], vectors[8 * layer + 5 : 8 * layer + 6, :]
            )
            small[...] = jnp.zeros_like(small)
            small[0:1, :] = gain
            small[1:2, :] = shift
            small[2:3, :] = jnp.sum(wide(rows_low[...]), axis=0, keepdims=True)
            grad_middle[...] = grad_next[...] + grad

        weave(main(), *grads_cargo(where, n, parts, owns, rest, (0, 2, 5, 7)))

    return call(
        body,
        "feed_backward",
        number,
        [INSIDE] * (8 + n),
        [
            (ROWS_WIDE, INSIDE),
            (FULL_CHUNK, INSIDE),
            (FULL_CHUNK, INSIDE),
            (SMALL, INSIDE),
            (SMALL_OWN, INSIDE),
        ]
        + [(OWN_CHUNK, INSIDE)] * n,
        [
            pltpu.VMEM((ROWS, D), jnp.bfloat16),
            pltpu.VMEM((CAP, D), jnp.bfloat16),
            pltpu.VMEM((CAP, CHUNK), jnp.bfloat16),
            pltpu.VMEM((CAP, D), jnp.bfloat16),
        ]
        + LINE_SEMS
        + spread_scratch()
        + scatter_scratch(DEPTH, (CHUNK,), jnp.bfloat16) * n,
        (grad_next, vectors, middle, up, down, second_full, activated, slope, *chunks),
    )


SUMS = 32


def sum_vectors(where, small, own, total, taken, turned, across, last, out, part_send, part_recv, send, recv):
    h, x, zl, y, c = where
    home = lax.rem(h + c, 2) == 0
    beside = device(h, x, 1 - zl, y, c)
    pairs = [(j, d) for j in range(4) for d in range(2) if j or d]
    started = []

    def go(*args):
        item = push(*args)
        item.start()
        started.append(item)

    for index, (j, d) in enumerate(pairs):
        xx, cc = turn(x, j, 4), turn(c, d, 2)
        go(
            small.at[:, rows_at((cc * 4 + xx) * 128, 128)],
            taken.at[index],
            part_send.at[index],
            part_recv.at[index],
            device(h, xx, zl, y, cc),
        )
    yield
    value = small[:, rows_at((c * 4 + x) * 128, 128)]
    for index in range(7):
        landed(taken.at[index], part_send.at[index], part_recv.at[index])
        value = value + taken[index]
    total[0, :SUMS] = value
    total[0, SUMS:] = own[...]
    for step in (1, 2, 3):
        go(
            total.at[0],
            turned.at[step - 1],
            send.at[step - 1],
            recv.at[step - 1],
            device(h, x, zl, turn(y, step, 4), c),
        )
    yield
    for step in (1, 2, 3):
        landed(turned.at[step - 1], send.at[step - 1], recv.at[step - 1])
    total[1] = total[0] + turned[0] + turned[1] + turned[2]
    go(total.at[1], across, send.at[3], recv.at[3], beside)
    yield
    landed(across, send.at[3], recv.at[3])
    total[2] = total[1] + across[...]
    for d in range(2):
        args = (
            total.at[2],
            last.at[h],
            send.at[4 + d],
            recv.at[4 + h],
            device(c, x, zl, y, turn(c, d, 2)),
        )
        if d == 0:
            move(*args, home)
        else:
            go(*args)
    yield
    for d in range(2):
        hh = turn(h, d, 2)
        args = (last.at[hh], send.at[4 + d], recv.at[4 + hh])
        if d == 0:
            moved_in(*args, home)
        else:
            landed(*args)
    out[...] = last[0] + last[1]
    for item in started:
        item.wait_send()
    moved_out(total.at[2], send.at[4], recv.at[4], beside, home)


def attend_backward(
    layer, number, grad_middle, vectors, hidden, weights, first_full, qkv, probs, heads, chunks,
    output=None, smalls=None,
):
    n = len(chunks)
    swaps = output is not None
    final = smalls is not None

    def body(grad_middle, vectors, hidden, weights, first_full, qkv, probs, heads, *rest):
        parts, rest = rest[:n], rest[n:]
        if swaps:
            output, rest = rest[0], rest[1:]
        if final:
            others, rest = rest[:6], rest[6:]
            (columns, weight_sum, totals), rest = rest[:3], rest[3:]
        else:
            (grad_hidden, weight_grad, small, small_own), rest = rest[:4], rest[4:]
        owns, rest = rest[:n], rest[n:]
        if swaps:
            columns, rest = rest[0], rest[1:]
        (rows_low, full, grad_heads, grad_joined, grad_key, grad_value, part), rest = rest[:7], rest[7:]
        line, rest = rest[:3], rest[3:]
        spread, rest = rest[:6], rest[6:]
        cargo, rest = rest[: 9 * n], rest[9 * n :]
        if final:
            (grad_hidden, weight_grad, small_all, own_all), rest = rest[:4], rest[4:]
            ring_scratch, rest = rest[:9], rest[9:]
            sum_scratch, rest = rest[:9], rest[9:]
            small, small_own = small_all.at[pl.ds(8, 8)], own_all.at[pl.ds(8, 8)]
        where = place()
        h, x, zl, y, c = where
        count = greet_ring(where, False)
        if final:
            greet(device(h, x, zl, turn(y, 2, 4), c))
            count = count + 1 + greet_parts(where)
        else:
            count = count + greet_line(where)
        if swaps or final:
            count = count + greet_swap(where, False)
            rows_out, columns_low, *swap_sems = rest
        await_greetings(count)
        planned = grads_cargo(where, n, parts, owns, cargo, (0, 3, 8, 10 if final else 11))
        if swaps:
            rows_out[...] = low(output[...])
            planned.append((swap_out(where, ((rows_out, columns_low),), *swap_sems), (4,)))

        def ready(rows):
            grad_heads[rows, :] = low(dot(full[rows, :], weights[:, 3 * PAIR :]))

        def weight_grads():
            for tile in range(D // TILE):
                features = slice(tile * TILE, (tile + 1) * TILE)
                weight_grad[features, : 3 * PAIR] = low(
                    t_dot(first_full[:, features], grad_joined[...])
                )
                weight_grad[features, 3 * PAIR :] = low(t_dot(full[:, features], heads[...]))
                if tile % 2:
                    yield
            total = jnp.sum(wide(grad_joined[...]), axis=0, keepdims=True)
            small_own[...] = jnp.zeros(small_own.shape, jnp.float32)
            small_own[0:1, :] = total[:, :PAIR]
            small_own[1:2, :] = total[:, 2 * PAIR :]

        def norm_end():
            gain, shift, grad = norm_back(grad_hidden[...], hidden[...], vector_of(vectors, layer, 0))
            small[...] = jnp.zeros(small.shape, jnp.float32)
            small[0:1, :] = gain
            small[1:2, :] = shift
            small[2:3, :] = jnp.sum(wide(rows_low[...]), axis=0, keepdims=True)
            grad_hidden[...] = grad_middle[...] + grad

        def last_steps():
            for index, first in enumerate((0, 16, 24)):
                small_all[first : first + 8, :] = others[2 * index][...]
                own_all[first : first + 8, :] = others[2 * index + 1][...]
            spreading = spread_line(where, part, grad_hidden, *spread)
            next(spreading)
            finish(weight_grads())
            ring = scatter_ring(where, rows_view(weight_grad), DEPTH, weight_sum, *ring_scratch)
            next(ring)
            yield
            next(spreading)
            yield
            next(spreading)
            next(ring)
            yield
            finish(spreading)
            norm_end()
            rows_out[...] = low(grad_hidden[...])
            swap = swap_out(where, ((rows_out, columns_low),), *swap_sems)
            next(swap)
            sums = sum_vectors(where, small_all, own_all, *sum_scratch[:5], totals, *sum_scratch[5:])
            next(sums)
            next(ring)
            next(sums)
            next(ring)
            next(sums)
            next(sums)
            finish(ring)
            finish(swap)
            columns[...] = wide(columns_low[...])
            finish(sums)

        def main():
            rows_low[...] = low(grad_middle[...])
            yield from gather_line(where, rows_low, full, *line, ready)
            masks = head_masks()
            grad_key[...] = jnp.zeros_like(grad_key)
            grad_value[...] = jnp.zeros_like(grad_value)
            for tile in range(CAP // TILE):
                rows, keys = slice(tile * TILE, (tile + 1) * TILE), (tile + 1) * TILE
                query, grad = wide(qkv[rows, :PAIR]), wide(grad_heads[rows, :])
                key, value = qkv[:keys, PAIR : 2 * PAIR], qkv[:keys, 2 * PAIR :]
                grad_query = 0.0
                for head in range(2):
                    grad_one = low(grad * masks[head])
                    soft_low = probs[head, :, probs_at(tile)]
                    soft = wide(soft_low)
                    grad_probs = dot_t(grad_one, value)
                    inner = jnp.sum(soft * grad_probs, axis=1, keepdims=True)
                    grad_scores = low(soft * (grad_probs - inner))
                    grad_query = grad_query + dot(grad_scores, key) * masks[head]
                    grad_key[:keys, :] += t_dot(grad_scores, low(query * masks[head]))
                    grad_value[:keys, :] += t_dot(soft_low, grad_one)
                grad_joined[rows, :PAIR] = low(grad_query * HDIM ** (-0.5))
                yield
            for tile in range(CAP // TILE):
                rows = slice(tile * TILE, (tile + 1) * TILE)
                grad_joined[rows, PAIR : 2 * PAIR] = low(grad_key[rows, :])
                grad_joined[rows, 2 * PAIR :] = low(grad_value[rows, :])
                part[rows, :] = low(dot_t(grad_joined[rows, :], weights[:, : 3 * PAIR]))
            if final:
                yield from last_steps()
                return
            yield from side_by_side(
                spread_line(where, part, grad_hidden, *spread), weight_grads()
            )
            norm_end()

        weave(main(), *planned)
        if swaps:
            columns[...] = wide(columns_low[...])

    rows = (2 * SUMS, 128)
    scatter = scatter_scratch(DEPTH, (CHUNK,), jnp.bfloat16)
    if final:
        outs = [(COLUMNS, INSIDE), (OWN_CHUNK, INSIDE), (of(rows, jnp.float32), INSIDE)]
        extra = (
            [
                pltpu.VMEM((ROWS, D), jnp.float32),
                pltpu.VMEM((D, CHUNK), jnp.bfloat16),
                pltpu.VMEM((SUMS, D), jnp.float32),
                pltpu.VMEM((SUMS, 128), jnp.float32),
            ]
            + scatter
            + [
                pltpu.VMEM((3,) + rows, jnp.float32),
                pltpu.VMEM((7, SUMS, 128), jnp.float32),
                pltpu.VMEM((3,) + rows, jnp.float32),
                pltpu.VMEM(rows, jnp.float32),
                pltpu.VMEM((2,) + rows, jnp.float32),
                pltpu.SemaphoreType.DMA((7,)),
                pltpu.SemaphoreType.DMA((7,)),
                pltpu.SemaphoreType.DMA((6,)),
                pltpu.SemaphoreType.DMA((6,)),
            ]
        )
    else:
        outs = [(ROWS_WIDE, INSIDE), (FULL_CHUNK, INSIDE), (SMALL, INSIDE), (SMALL_OWN, INSIDE)]
        extra = []
    return call(
        body,
        "attend_backward_last" if final else "attend_backward",
        number,
        [INSIDE] * (8 + n + swaps + 6 * final),
        outs + [(OWN_CHUNK, INSIDE)] * n + [(COLUMNS, INSIDE)] * swaps,
        [
            ROW_SCRATCH,
            pltpu.VMEM((CAP, D), jnp.bfloat16),
            pltpu.VMEM((CAP, PAIR), jnp.bfloat16),
            pltpu.VMEM((CAP, 3 * PAIR), jnp.bfloat16),
            pltpu.VMEM((CAP, PAIR), jnp.float32),
            pltpu.VMEM((CAP, PAIR), jnp.float32),
            pltpu.VMEM((CAP, D), jnp.bfloat16),
        ]
        + LINE_SEMS
        + spread_scratch()
        + scatter * n
        + extra
        + ([ROW_SCRATCH, COLUMN_SCRATCH] + SWAP_SEMS) * (swaps or final),
        (
            grad_middle, vectors, hidden, weights, first_full, qkv, probs, heads, *chunks,
            *([output] if swaps else []), *(smalls if final else []),
        ),
    )


def head_pairs(joined):
    shape = joined.shape[:-1]
    return jnp.swapaxes(joined.reshape(shape + (LOCAL_HEADS, 3, HDIM)), -3, -2).reshape(joined.shape)


def heads_apart(joined):
    shape = joined.shape[:-1]
    return jnp.swapaxes(joined.reshape(shape + (3, LOCAL_HEADS, HDIM)), -3, -2).reshape(joined.shape)


def shards(
    hidden_in,
    joined_weight,
    query_bias,
    value_bias,
    out_weight,
    out_bias,
    first_gain,
    first_shift,
    up_weight,
    up_bias,
    down_weight,
    down_bias,
    second_gain,
    second_shift,
    seq_lengths,
    cotangent,
):
    row = lax.axis_index("row")
    small = jnp.concatenate(
        [
            first_gain,
            first_shift,
            query_bias,
            value_bias,
            out_bias,
            second_gain,
            second_shift,
            down_bias,
        ],
        axis=1,
    ).reshape(LAYERS * 8, 8)
    lanes = jnp.arange(128, dtype=jnp.int32)[None, :]
    small_tile = jnp.where(lax.div(lanes, 8) == row, jnp.tile(small, (1, 16)), 0)
    quarter = jnp.arange(4 * LAYERS, dtype=jnp.int32)[:, None] % 4
    up_tile = jnp.where(
        quarter * 4 + lax.div(lanes, 32) == row, jnp.tile(jnp.repeat(up_bias, 4, axis=0), (1, 4)), 0
    )
    lengths_tile = jnp.pad(seq_lengths.astype(jnp.float32), ((0, 7), (0, 124)))
    pack = jnp.concatenate(
        [small_tile.astype(jnp.float32), up_tile.astype(jnp.float32), lengths_tile]
    )
    joined_out = jnp.concatenate([head_pairs(joined_weight), jnp.swapaxes(out_weight, 1, 2)], axis=2)
    down_turned = jnp.swapaxes(down_weight, 1, 2)
    (
        vectors, ends, input_0, joined_0, full_10, qkv_0, probs_0, heads_0, middle_0, up_0, down_0,
    ) = enter_attend(hidden_in, pack, joined_out[0], [up_weight[0], down_turned[0]])
    full_20, active_0, slope_0, hidden, joined_1, up_1 = feed_forward(
        0, 2, middle_0, vectors, up_0, down_0, [joined_out[1], up_weight[1]]
    )
    input_1 = hidden
    full_11, qkv_1, probs_1, heads_1, middle_1, down_1, cotangent_rows = attend_forward(
        1, 3, hidden, vectors, ends, joined_1, [down_turned[1]], cotangent
    )
    hidden, grad_middle, down_part, up_part, feed_small_1, feed_own_1 = feed_both(
        1, 4, middle_1, vectors, up_1, down_1, cotangent_rows
    )
    (
        grad_hidden, joined_part, attend_small_1, attend_own_1, down_sum_1, up_sum_1, hidden_out,
    ) = attend_backward(
        1, 6, grad_middle, vectors, input_1, joined_1, full_11, qkv_1, probs_1, heads_1,
        [down_part, up_part], hidden,
    )
    grad_middle, down_part, up_part, feed_small_0, feed_own_0, joined_sum_1 = feed_backward(
        0, 7, grad_hidden, vectors, middle_0, up_0, down_0, full_20, active_0, slope_0, [joined_part]
    )
    grad_out, joined_sum_0, totals, down_sum_0, up_sum_0 = attend_backward(
        0, 8, grad_middle, vectors, input_0, joined_0, full_10, qkv_0, probs_0, heads_0,
        [down_part, up_part],
        smalls=[
            feed_small_0, feed_own_0, feed_small_1, feed_own_1, attend_small_1, attend_own_1,
        ],
    )
    narrow = lax.dynamic_slice_in_dim(totals, row * 8, 8, axis=1).reshape(2, LAYERS, 2, 8, 8)
    ups = totals[SUMS:].reshape(LAYERS, 2, 8, 128)[:, 0, :4].reshape(LAYERS, CHUNK)
    joined_sums = jnp.stack([joined_sum_0, joined_sum_1])
    return (
        hidden_out,
        grad_out,
        heads_apart(joined_sums[:, :, : 3 * PAIR]),
        narrow[1, :, 1, 0],
        narrow[1, :, 1, 1],
        jnp.swapaxes(joined_sums[:, :, 3 * PAIR :], 1, 2),
        narrow[0, :, 1, 2],
        narrow[0, :, 1, 0],
        narrow[0, :, 1, 1],
        jnp.stack([up_sum_0, up_sum_1]),
        lax.dynamic_slice_in_dim(ups, row * 32, 32, axis=1),
        jnp.swapaxes(jnp.stack([down_sum_0, down_sum_1]), 1, 2),
        narrow[0, :, 0, 2],
        narrow[0, :, 0, 0],
        narrow[0, :, 0, 1],
    )


def solution(mesh):
    vector = P(None, ("col", "row"))
    return jax.shard_map(
        shards,
        mesh=mesh,
        in_specs=(
            P("row", "col"),
            P(None, "row", "col"),
            vector,
            vector,
            P(None, "col", "row"),
            vector,
            vector,
            vector,
            P(None, "row", "col"),
            vector,
            P(None, "col", "row"),
            vector,
            vector,
            vector,
            P("row", None),
            P("row", "col"),
        ),
        out_specs=(
            P("row", "col"),
            P("row", "col"),
            P(None, "row", "col"),
            vector,
            vector,
            P(None, "col", "row"),
            vector,
            vector,
            vector,
            P(None, "row", "col"),
            vector,
            P(None, "col", "row"),
            vector,
            vector,
            vector,
        ),
        check_vma=False,
    )
```

```python
import functools

import jax
import jax.numpy as jnp
from jax import lax
from jax.experimental import pallas as pl
from jax.experimental.pallas import tpu as pltpu
from jax.sharding import PartitionSpec as P

D = 1024
HEADS = 16
HDIM = 64
FF = 4096
LAYERS = 2
CAP = 1024
PARTS = 8
ROWS = CAP // PARTS
LOCAL_HEADS = HEADS // PARTS
EPS = 1e-05
NEG = -1000000000.0
MESH = pl.DeviceIdType.MESH


def place():
    row = lax.axis_index("row")
    col = lax.axis_index("col")
    return (
        lax.div(col, 4),
        lax.rem(col, 4),
        lax.div(row, 8),
        lax.div(lax.rem(row, 8), 2),
        lax.rem(row, 2),
    )


def device(h, x, zl, y, c):
    return (zl * 8 + y * 2 + c, h * 4 + x)


def turn(value, by, size):
    return lax.rem(value + by, size)


def rows_at(start, size):
    return pl.ds(pl.multiple_of(start, size), size)


def push(src, dst, send_sem, recv_sem, target):
    return pltpu.make_async_remote_copy(
        src_ref=src,
        dst_ref=dst,
        send_sem=send_sem,
        recv_sem=recv_sem,
        device_id=target,
        device_id_type=MESH,
    )


def greet(target):
    pl.semaphore_signal(
        pltpu.get_barrier_semaphore(), inc=1, device_id=target, device_id_type=MESH
    )


def await_greetings(count):
    pl.semaphore_wait(pltpu.get_barrier_semaphore(), count)


def unless(flag, run):
    pl.when(jnp.logical_not(flag))(run)


def together(*parts):
    alive = list(parts)
    while alive:
        alive = [part for part in alive if next(part, alive) is not alive]


def weave(main, *planned):
    count = 0
    waiting = [[part, list(plan)] for part, plan in planned]

    def advance():
        for part, plan in waiting:
            while plan and plan[0] <= count:
                next(part, None)
                plan.pop(0)

    advance()
    for _ in main:
        count += 1
        advance()
    for part, _ in waiting:
        for _ in part:
            pass


def landed(view, send_sem, recv_sem):
    row, col = lax.axis_index("row"), lax.axis_index("col")
    push(view, view, send_sem, recv_sem, (row, lax.rem(col + 1, 8))).wait_recv()


def neighbours(where):
    h, x, zl, y, c = where
    return (
        device(h, turn(x, 1, 4), zl, y, c),
        device(h, turn(x, 3, 4), zl, y, c),
        device(h, x, zl, y, 1 - c),
    )


def greet_line(where):
    for other in neighbours(where):
        greet(other)
    return 3


def greet_ring(where, inward):
    h, x, zl, y, c = where
    home = lax.rem(h + c, 2) == 0
    for d in range(2):
        if inward:
            source = device(c, x, zl, y, turn(c, d, 2))
        else:
            source = device(turn(h, d, 2), x, zl, y, h)
        if d == 0:
            unless(home, functools.partial(greet, source))
        else:
            greet(source)
    for step in (1, 3):
        greet(device(h, x, zl, turn(y, step, 4), c))
    greet(device(h, x, 1 - zl, y, c))
    return 4 + lax.rem(h + c, 2)


def greet_swap(where, inward):
    h, x, zl, y, c = where
    home = lax.rem(h + c, 2) == 0
    for j in range(4):
        for d in range(2):
            if inward:
                source = device(turn(h, d, 2), turn(x, j, 4), zl, y, h)
            else:
                source = device(c, turn(x, j, 4), zl, y, turn(c, d, 2))
            if j == 0 and d == 0:
                unless(home, functools.partial(greet, source))
            else:
                greet(source)
    return 7 + lax.rem(h + c, 2)


def greet_parts(where):
    h, x, zl, y, c = where
    for j in range(4):
        for d in range(2):
            if j or d:
                greet(device(h, turn(x, j, 4), zl, y, turn(c, d, 2)))
    return 7


def move(src, dst, send_sem, recv_sem, target, home):
    unless(home, push(src, dst, send_sem, recv_sem, target).start)
    pl.when(home)(lambda: pltpu.make_async_copy(src, dst, recv_sem).start())


def moved_in(dst, send_sem, recv_sem, home):
    unless(home, functools.partial(landed, dst, send_sem, recv_sem))
    pl.when(home)(lambda: pltpu.make_async_copy(dst, dst, recv_sem).wait())


def moved_out(src, send_sem, recv_sem, target, home):
    unless(home, push(src, src, send_sem, recv_sem, target).wait_send)


def gather_line(where, src, out, own_sem, send, recv, ready):
    h, x, zl, y, c = where
    right, left, mate = neighbours(where)
    half = ROWS // 2

    def span(core, step, first=0, size=ROWS):
        return rows_at((core * 4 + turn(x, step, 4)) * ROWS + first, size)

    def block(*args):
        return out.at[span(*args)]

    started = []

    def copy(index, view, target, source=None):
        source = view if source is None else source
        item = push(source, view, send.at[index], recv.at[index], target)
        item.start()
        started.append(item)

    def arrived(index, view):
        landed(view, send.at[index], recv.at[index])

    low, high = src.at[pl.ds(0, half)], src.at[pl.ds(half, half)]
    copy(0, block(c, 0, 0, half), right, low)
    copy(2, block(c, 0, half, half), left, high)
    copy(1, block(c, 0, half, half), right, high)
    copy(3, block(c, 0, 0, half), left, low)
    copy(4, block(c, 0), mate, src)
    own = pltpu.make_async_copy(src, block(c, 0), own_sem)
    own.start()
    yield
    own.wait()
    ready(span(c, 0))
    arrived(0, block(c, 3, 0, half))
    copy(5, block(c, 3, 0, half), right)
    arrived(2, block(c, 1, half, half))
    copy(6, block(c, 1, half, half), left)
    yield
    arrived(4, block(1 - c, 0))
    ready(span(1 - c, 0))
    arrived(1, block(c, 3, half, half))
    copy(7, block(c, 3), mate)
    arrived(3, block(c, 1, 0, half))
    copy(8, block(c, 1), mate)
    ready(span(c, 3))
    yield
    arrived(5, block(c, 2, 0, half))
    copy(9, block(c, 2, 0, half), mate)
    arrived(6, block(c, 2, half, half))
    copy(10, block(c, 2, half, half), mate)
    ready(span(c, 1))
    ready(span(c, 2))
    yield
    arrived(7, block(1 - c, 3))
    ready(span(1 - c, 3))
    arrived(8, block(1 - c, 1))
    ready(span(1 - c, 1))
    arrived(9, block(1 - c, 2, 0, half))
    arrived(10, block(1 - c, 2, half, half))
    ready(span(1 - c, 2))
    for item in started:
        item.wait_send()


LINE_SEMS = [
    pltpu.SemaphoreType.DMA,
    pltpu.SemaphoreType.DMA((11,)),
    pltpu.SemaphoreType.DMA((11,)),
]
RING_SEMS = [pltpu.SemaphoreType.DMA((9,)), pltpu.SemaphoreType.DMA((9,))]


def spread_line(where, part, out, core_in, sums, hop, final, send, recv):
    h, x, zl, y, c = where
    right, left, mate = neighbours(where)
    half, quarter = ROWS // 2, ROWS // 4

    def mine(core, step, first=0, size=ROWS):
        return part.at[rows_at((core * 4 + turn(x, step, 4)) * ROWS + first, size)]

    started = []

    def copy(index, source, view, target):
        item = push(source, view, send.at[index], recv.at[index], target)
        item.start()
        started.append(item)

    def arrived(index, view):
        landed(view, send.at[index], recv.at[index])

    def add(left_ref, right_ref):
        return wide(left_ref[...]) + wide(right_ref[...])

    for first in (0, half):
        rows = pl.ds(first, half)
        copy(1 if first else 0, mine(1 - c, 2, first, half), core_in.at[2, rows], mate)
    copy(2, mine(1 - c, 1), core_in.at[1], mate)
    copy(3, mine(1 - c, 3), core_in.at[3], mate)
    copy(4, mine(1 - c, 0), core_in.at[0], mate)
    yield
    for side, (first, target) in enumerate(((0, right), (half, left))):
        rows = pl.ds(first, half)
        arrived(side, core_in.at[2, rows])
        sums[2, first : first + half] = low(add(mine(c, 2, first, half), core_in.at[2, rows]))
        for piece in range(2):
            copy(
                5 + 2 * side + piece,
                sums.at[2, pl.ds(first + piece * quarter, quarter)],
                hop.at[side, pl.ds(piece * quarter, quarter)],
                target,
            )
    arrived(2, core_in.at[1])
    sums[1] = low(add(mine(c, 1), core_in.at[1]))
    copy(9, sums.at[1, pl.ds(half, half)], final.at[0, pl.ds(half, half)], right)
    arrived(3, core_in.at[3])
    sums[3] = low(add(mine(c, 3), core_in.at[3]))
    copy(10, sums.at[3, pl.ds(0, half)], final.at[1, pl.ds(0, half)], left)
    yield
    arrived(4, core_in.at[0])
    out[...] = add(mine(c, 0), core_in.at[0])
    for piece in range(2):
        for side, (block, first, target) in enumerate(((1, 0, right), (3, half, left))):
            taken = hop.at[side, pl.ds(piece * quarter, quarter)]
            start = first + piece * quarter
            rows = pl.ds(start, quarter)
            arrived(5 + 2 * side + piece, taken)
            sums[block, start : start + quarter] = low(add(sums.at[block, rows], taken))
            copy(11 + 2 * side + piece, sums.at[block, rows], final.at[side, rows], target)
    yield
    arrived(9, final.at[0, pl.ds(half, half)])
    arrived(10, final.at[1, pl.ds(0, half)])
    yield
    for piece in range(2):
        arrived(11 + piece, final.at[0, pl.ds(piece * quarter, quarter)])
        arrived(13 + piece, final.at[1, pl.ds(half + piece * quarter, quarter)])
    out[...] += wide(final[0]) + wide(final[1])
    for item in started:
        item.wait_send()


def spread_scratch():
    half = ROWS // 2
    return [
        pltpu.VMEM((4, ROWS, D), jnp.bfloat16),
        pltpu.VMEM((4, ROWS, D), jnp.bfloat16),
        pltpu.VMEM((2, half, D), jnp.bfloat16),
        pltpu.VMEM((2, ROWS, D), jnp.bfloat16),
        pltpu.SemaphoreType.DMA((15,)),
        pltpu.SemaphoreType.DMA((15,)),
    ]


def gather_ring(where, own, slot, send, recv):
    h, x, zl, y, c = where
    home = lax.rem(h + c, 2) == 0
    above = device(h, x, zl, turn(y, 1, 4), c)
    below = device(h, x, zl, turn(y, 3, 4), c)
    beside = device(h, x, 1 - zl, y, c)

    def piece(p, step):
        return slot(turn(zl, p, 2), turn(y, step, 4), 0, 2, c)

    def ring(index, view, target):
        push(view, view, send.at[index], recv.at[index], target).start()

    def arrived(index, view):
        landed(view, send.at[index], recv.at[index])

    for d in range(2):
        target = device(turn(h, d, 2), x, zl, y, h)
        args = (own, slot(zl, y, c, 1, h), send.at[d], recv.at[c], target)
        if d == 0:
            move(*args, home)
        else:
            push(*args).start()
    yield
    for d in range(2):
        cc = turn(c, d, 2)
        args = (slot(zl, y, cc, 1, c), send.at[d], recv.at[cc])
        if d == 0:
            moved_in(*args, home)
        else:
            landed(*args)
    ring(2, piece(0, 0), beside)
    ring(3, piece(0, 0), above)
    ring(5, piece(0, 0), below)
    yield
    arrived(2, piece(1, 0))
    ring(4, piece(1, 0), above)
    ring(6, piece(1, 0), below)
    yield
    arrived(3, piece(0, 3))
    ring(7, piece(0, 3), above)
    arrived(6, piece(1, 1))
    ring(8, piece(1, 1), below)
    yield
    arrived(4, piece(1, 3))
    arrived(5, piece(0, 1))
    arrived(7, piece(0, 2))
    arrived(8, piece(1, 2))
    moved_out(own, send.at[0], recv.at[0], beside, home)
    push(own, own, send.at[1], recv.at[1], beside).wait_send()
    for index in range(2, 9):
        push(piece(0, 0), piece(0, 0), send.at[index], recv.at[index], beside).wait_send()


def finish(part):
    for _ in part:
        pass


def gather_vectors(where, pack, vectors, ends, taken, mine, near, send, recv, part_send, part_recv):
    h, x, zl, y, c = where
    home = lax.rem(h + c, 2) == 0
    beside = device(h, x, 1 - zl, y, c)
    started = []

    def go(*args):
        item = push(*args)
        item.start()
        started.append(item)

    for d in range(2):
        args = (pack, taken.at[c], send.at[d], recv.at[c], device(turn(h, d, 2), x, zl, y, h))
        if d == 0:
            move(*args, home)
        else:
            go(*args)
    yield
    for d in range(2):
        cc = turn(c, d, 2)
        args = (taken.at[cc], send.at[d], recv.at[cc])
        if d == 0:
            moved_in(*args, home)
        else:
            landed(*args)
    mine[...] = taken[0] + taken[1]
    ends[...] = taken[h, 24:32, :]
    for index in range(1, 8):
        dz, dy = divmod(index, 4)
        other = device(h, x, turn(zl, dz, 2), turn(y, dy, 4), c)
        go(mine, near.at[index - 1], send.at[1 + index], recv.at[1 + index], other)
    yield
    value = mine[...]
    for index in range(1, 8):
        landed(near.at[index - 1], send.at[1 + index], recv.at[1 + index])
        value = value + near[index - 1]

    def block(part):
        return vectors.at[:, rows_at(part * 128, 128)]

    part = c * 4 + x
    vectors[:, rows_at(part * 128, 128)] = value
    pairs = [(j, d) for j in range(4) for d in range(2) if j or d]
    for index, (j, d) in enumerate(pairs):
        other = device(h, turn(x, j, 4), zl, y, turn(c, d, 2))
        go(block(part), block(part), part_send.at[index], part_recv.at[part], other)
    yield
    for index, (j, d) in enumerate(pairs):
        other = turn(c, d, 2) * 4 + turn(x, j, 4)
        landed(block(other), part_send.at[index], part_recv.at[other])
    for item in started:
        item.wait_send()
    moved_out(pack, send.at[0], recv.at[0], beside, home)


def greet_near(where):
    h, x, zl, y, c = where
    greet(device(h, x, zl, turn(y, 2, 4), c))
    for step in (1, 2, 3):
        greet(device(h, x, 1 - zl, turn(y, step, 4), c))
    return 4


def swap_in(where, pairs, send, recv):
    h, x, zl, y, c = where
    home = lax.rem(h + c, 2) == 0
    mine = h * 4 + x
    for item, (src, dst) in enumerate(pairs):
        for j in range(4):
            for d in range(2):
                xx, cc = turn(x, j, 4), turn(c, d, 2)
                args = (
                    src.at[rows_at((cc * 4 + xx) * ROWS, ROWS)],
                    dst.at[:, rows_at(mine * 128, 128)],
                    send.at[item, j * 2 + d],
                    recv.at[item, mine],
                    device(c, xx, zl, y, cc),
                )
                if j or d:
                    push(*args).start()
                else:
                    move(*args, home)
    yield
    for item, (src, dst) in enumerate(pairs):
        for j in range(4):
            for d in range(2):
                k = turn(h, d, 2) * 4 + turn(x, j, 4)
                view = dst.at[:, rows_at(k * 128, 128)]
                sems = (send.at[item, j * 2 + d], recv.at[item, k])
                gone = src.at[pl.ds(0, ROWS)]
                other = device(h, x, 1 - zl, y, c)
                if j or d:
                    landed(view, *sems)
                    push(gone, gone, *sems, other).wait_send()
                else:
                    moved_in(view, *sems, home)
                    moved_out(gone, *sems, other, home)


def swap_out(where, pairs, send, recv):
    h, x, zl, y, c = where
    home = lax.rem(h + c, 2) == 0
    mine = c * 4 + x
    for item, (src, dst) in enumerate(pairs):
        for j in range(4):
            for d in range(2):
                hh, xx = turn(h, d, 2), turn(x, j, 4)
                args = (
                    src.at[:, rows_at((hh * 4 + xx) * 128, 128)],
                    dst.at[rows_at(mine * ROWS, ROWS)],
                    send.at[item, j * 2 + d],
                    recv.at[item, mine],
                    device(hh, xx, zl, y, h),
                )
                if j or d:
                    push(*args).start()
                else:
                    move(*args, home)
    yield
    for item, (src, dst) in enumerate(pairs):
        for j in range(4):
            for d in range(2):
                part = turn(c, d, 2) * 4 + turn(x, j, 4)
                view = dst.at[rows_at(part * ROWS, ROWS)]
                sems = (send.at[item, j * 2 + d], recv.at[item, part])
                gone = src.at[:, pl.ds(0, 128)]
                other = device(h, x, 1 - zl, y, c)
                if j or d:
                    landed(view, *sems)
                    push(gone, gone, *sems, other).wait_send()
                else:
                    moved_in(view, *sems, home)
                    moved_out(gone, *sems, other, home)


def scatter_ring(where, rows, depth, out, hop, final, sums, kept, across, pair, last, send, recv):
    h, x, zl, y, c = where
    home = lax.rem(h + c, 2) == 0
    above = device(h, x, zl, turn(y, 1, 4), c)
    below = device(h, x, zl, turn(y, 3, 4), c)
    beside = device(h, x, 1 - zl, y, c)
    kind = hop.dtype

    def piece(p, step):
        return rows((turn(zl, p, 2) * 8 + turn(y, step, 4) * 2) * depth, 2 * depth)

    def wide(value):
        return value.astype(jnp.float32)

    def go(index, src, dst, target):
        push(src, dst, send.at[index], recv.at[index], target).start()

    def come(index, dst):
        landed(dst, send.at[index], recv.at[index])

    go(0, piece(0, 2), hop.at[0], above)
    go(1, piece(1, 2), hop.at[1], below)
    go(2, piece(1, 1), final.at[0, 1], above)
    go(3, piece(0, 3), final.at[1, 0], below)
    yield
    come(0, hop.at[0])
    sums[0] = (wide(piece(0, 1)[...]) + wide(hop[0])).astype(kind)
    go(4, sums.at[0], final.at[0, 0], above)
    come(1, hop.at[1])
    sums[1] = (wide(piece(1, 3)[...]) + wide(hop[1])).astype(kind)
    go(5, sums.at[1], final.at[1, 1], below)
    yield
    come(2, final.at[0, 1])
    come(5, final.at[1, 1])
    across[0] = (wide(piece(1, 0)[...]) + wide(final[0, 1]) + wide(final[1, 1])).astype(kind)
    go(6, across.at[0], across.at[1], beside)
    come(3, final.at[1, 0])
    come(4, final.at[0, 0])
    kept[...] = wide(piece(0, 0)[...]) + wide(final[0, 0]) + wide(final[1, 0])
    yield
    come(6, across.at[1])
    pair[...] = (kept[...] + wide(across[1])).astype(kind)
    for d in range(2):
        cc = turn(c, d, 2)
        args = (
            pair.at[rows_at(cc * depth, depth)],
            last.at[h],
            send.at[7 + d],
            recv.at[7 + h],
            device(c, x, zl, y, cc),
        )
        if d == 0:
            move(*args, home)
        else:
            push(*args).start()
    yield
    for d in range(2):
        hh = turn(h, d, 2)
        args = (last.at[hh], send.at[7 + d], recv.at[7 + hh])
        if d == 0:
            moved_in(*args, home)
        else:
            landed(*args)
    out[...] = wide(last[0]) + wide(last[1])
    for index in range(7):
        push(piece(0, 0), piece(0, 0), send.at[index], recv.at[index], beside).wait_send()
    gone = pair.at[pl.ds(0, depth)]
    moved_out(gone, send.at[7], recv.at[7], beside, home)
    push(gone, gone, send.at[8], recv.at[8], beside).wait_send()


def scatter_scratch(depth, rest, kind):
    both = (2 * depth,) + rest
    return [
        pltpu.VMEM((2,) + both, kind),
        pltpu.VMEM((2, 2) + both, kind),
        pltpu.VMEM((2,) + both, kind),
        pltpu.VMEM(both, jnp.float32),
        pltpu.VMEM((2,) + both, kind),
        pltpu.VMEM(both, kind),
        pltpu.VMEM((2, depth) + rest, kind),
    ] + RING_SEMS


def rows_of(full, depth):
    def slot(zz, yy, cc, count, core):
        return full.at[rows_at((zz * 8 + yy * 2 + cc) * depth, depth * count)]

    return slot


def rows_view(ref):
    return lambda start, count: ref.at[rows_at(start, count)]


ANYWHERE = pl.BlockSpec(memory_space=pl.ANY)
INSIDE = pl.BlockSpec(memory_space=pltpu.VMEM)
DEPTH = D // 16
CHUNK = 512
PAIR = 2 * HDIM
TILE = 256
VMEM_BYTES = 24 * 2**20

ROWS_LOW = jax.ShapeDtypeStruct((ROWS, D), jnp.bfloat16)
ROWS_WIDE = jax.ShapeDtypeStruct((ROWS, D), jnp.float32)
FULL_ROWS = jax.ShapeDtypeStruct((CAP, D), jnp.bfloat16)
FULL_CHUNK = jax.ShapeDtypeStruct((D, CHUNK), jnp.bfloat16)
OWN_CHUNK = jax.ShapeDtypeStruct((DEPTH, CHUNK), jnp.float32)
SMALL = jax.ShapeDtypeStruct((8, D), jnp.float32)
SMALL_OWN = jax.ShapeDtypeStruct((8, 128), jnp.float32)


def of(shape, kind=jnp.bfloat16):
    return jax.ShapeDtypeStruct(shape, kind)


def call(body, name, number, ins, outs, scratch, args):
    return pl.pallas_call(
        body,
        out_shape=tuple(shape for shape, _ in outs),
        in_specs=ins,
        out_specs=tuple(spec for _, spec in outs),
        scratch_shapes=scratch,
        compiler_params=pltpu.CompilerParams(
            collective_id=number, has_side_effects=True, vmem_limit_bytes=VMEM_BYTES
        ),
        name=name,
    )(*args)


def dot(left, right):
    return jnp.dot(left, right, preferred_element_type=jnp.float32)


def dot_t(left, right):
    return lax.dot_general(left, right, (((1,), (1,)), ((), ())), preferred_element_type=jnp.float32)


def t_dot(left, right):
    return lax.dot_general(left, right, (((0,), (0,)), ((), ())), preferred_element_type=jnp.float32)


def low(value):
    return value.astype(jnp.bfloat16)


def wide(value):
    return value.astype(jnp.float32)


def normed_of(values):
    centred = values - jnp.mean(values, axis=1, keepdims=True)
    inverse = lax.rsqrt(jnp.mean(centred * centred, axis=1, keepdims=True) + EPS)
    return centred * inverse, inverse


def norm_back(grad_rows, values, gain):
    normed, inverse = normed_of(values)
    grad_gain = jnp.sum(grad_rows * normed, axis=0, keepdims=True)
    grad_shift = jnp.sum(grad_rows, axis=0, keepdims=True)
    scaled = grad_rows * gain
    mean_one = jnp.mean(scaled, axis=1, keepdims=True)
    mean_two = jnp.mean(scaled * normed, axis=1, keepdims=True)
    return grad_gain, grad_shift, inverse * (scaled - mean_one - normed * mean_two)


def head_masks():
    first = lax.broadcasted_iota(jnp.int32, (1, PAIR), 1) < HDIM
    one = first.astype(jnp.float32)
    return one, 1.0 - one


def side_by_side(*parts):
    alive = list(parts)
    while alive:
        alive = [part for part in alive if next(part, alive) is not alive]
        yield


def weights_cargo(where, count, owns, fulls, sems, *plans):
    return [
        (gather_ring(where, owns[i], rows_of(fulls[i], DEPTH), *sems[2 * i : 2 * i + 2]), plans[i])
        for i in range(count)
    ]


def grads_cargo(where, count, parts, owns, scratch, *plans):
    return [
        (scatter_ring(where, rows_view(parts[i]), DEPTH, owns[i], *scratch[9 * i : 9 * i + 9]), plans[i])
        for i in range(count)
    ]


SWAP_SEMS = [pltpu.SemaphoreType.DMA((1, 8)), pltpu.SemaphoreType.DMA((1, 8))]
COLUMNS = jax.ShapeDtypeStruct((CAP, 128), jnp.float32)
ROW_SCRATCH = pltpu.VMEM((ROWS, D), jnp.bfloat16)
COLUMN_SCRATCH = pltpu.VMEM((CAP, 128), jnp.bfloat16)


PROBS = (2, TILE, TILE * 10)


def probs_at(tile):
    first = TILE * tile * (tile + 1) // 2
    return slice(first, first + TILE * (tile + 1))


def vector_of(vectors, layer, index):
    return vectors[8 * layer + index : 8 * layer + index + 1, :]


def own_vector(vectors, row, part):
    return vectors[row : row + 1, rows_at(part * 128, 128)]


def up_bias_of(vectors, layer, part):
    first = 16 + 4 * layer
    return jnp.concatenate([own_vector(vectors, first + i, part) for i in range(4)], axis=1)


def join_rows(rows, full, weights, qkv, vectors, layer, part):
    joined = dot(full[rows, :], weights[:, : 3 * PAIR])
    query_bias = own_vector(vectors, 8 * layer + 2, part)
    value_bias = own_vector(vectors, 8 * layer + 3, part)
    qkv[rows, :PAIR] = low((joined[:, :PAIR] + query_bias) * HDIM ** (-0.5))
    qkv[rows, PAIR : 2 * PAIR] = low(joined[:, PAIR : 2 * PAIR])
    qkv[rows, 2 * PAIR :] = low(joined[:, 2 * PAIR :] + value_bias)


def segments(ends, places):
    bound = 0.0
    found = jnp.zeros(places.shape, jnp.int32)
    for slot in range(4):
        bound = bound + ends[0:1, slot : slot + 1]
        found = found + (places >= bound).astype(jnp.int32)
    return found


def attend_tile(tile, qkv, ends, part, probs):
    masks = head_masks()
    rows, keys = slice(tile * TILE, (tile + 1) * TILE), (tile + 1) * TILE
    query = wide(qkv[rows, :PAIR])
    key, value = qkv[:keys, PAIR : 2 * PAIR], qkv[:keys, 2 * PAIR :]
    row_places = wide(tile * TILE + lax.broadcasted_iota(jnp.int32, (TILE, 1), 0))
    key_places = wide(lax.broadcasted_iota(jnp.int32, (1, keys), 1))
    offset = key_places - row_places
    allowed = (segments(ends, row_places) == segments(ends, key_places)) & (offset <= 0.0)
    mixed = 0.0
    for head in range(2):
        number = wide(jnp.full((1, 128), part * LOCAL_HEADS + head, jnp.int32))
        slope = jnp.exp2(-8.0 * (number + 1.0) / HEADS)
        scores = dot_t(low(query * masks[head]), key)
        scores = scores + slope[:, :1] * offset
        scores = jnp.where(allowed, scores, NEG)
        shifted = jnp.exp(scores - jnp.max(scores, axis=1, keepdims=True))
        soft = low(shifted / jnp.sum(shifted, axis=1, keepdims=True))
        probs[head, :, probs_at(tile)] = soft
        mixed = mixed + dot(soft, value) * masks[head]
    return low(mixed)


def attend_rows(core, qkv, ends, number, probs, heads, part, weights, spreading):
    def two_tiles(first):
        for tile in (first, first + 1):
            rows = slice(tile * TILE, (tile + 1) * TILE)
            mixed = attend_tile(tile, qkv, ends, number, probs)
            heads[rows, :] = mixed
            part[rows, :] = low(dot_t(mixed, weights[:, 3 * PAIR :]))

    pl.when(core == 0)(functools.partial(two_tiles, 2))
    pl.when(core == 1)(functools.partial(two_tiles, 0))
    yield
    next(spreading)
    yield
    pl.when(core == 0)(functools.partial(two_tiles, 0))
    pl.when(core == 1)(functools.partial(two_tiles, 2))
    yield


VECTORS = jax.ShapeDtypeStruct((32, D), jnp.float32)
ENDS = jax.ShapeDtypeStruct((8, 128), jnp.float32)
ATTEND_OUTS = [
    (FULL_ROWS, INSIDE),
    (of((CAP, 3 * PAIR)), INSIDE),
    (of(PROBS), INSIDE),
    (of((CAP, PAIR)), INSIDE),
    (ROWS_WIDE, INSIDE),
]


def enter_attend(columns, pack, joined, chunks):
    n = len(chunks)

    def body(columns, pack, joined, *rest):
        owns, rest = rest[:n], rest[n:]
        (vectors, ends, hidden, weights, full, qkv, probs, heads, middle), rest = rest[:9], rest[9:]
        fulls, rest = rest[:n], rest[n:]
        (columns_in, columns_sem), rest = rest[:2], rest[2:]
        (columns_low, rows_low, first, part, taken, mine, near), rest = rest[:7], rest[7:]
        line, rest = rest[:3], rest[3:]
        spread, rest = rest[:6], rest[6:]
        swap_sems, rest = rest[:2], rest[2:]
        ring_sems, rest = rest[:2], rest[2:]
        sems, pack_sems = rest[: 2 * n], rest[2 * n :]
        where = place()
        h, x, zl, y, c = where
        count = (
            greet_ring(where, True) + greet_parts(where) + greet_swap(where, True) + greet_near(where)
        )
        number = c * 4 + x
        fetch = pltpu.make_async_copy(columns, columns_in, columns_sem)
        fetch.start()
        fetch.wait()
        columns_low[...] = low(columns_in[...])
        await_greetings(count)
        packs = gather_vectors(where, pack, vectors, ends, taken, mine, near, *pack_sems)
        swap = swap_in(where, ((columns_low, rows_low),), *swap_sems)
        ring = gather_ring(where, joined, rows_of(weights, DEPTH), *ring_sems)
        next(packs)
        next(swap)
        next(ring)
        next(packs)
        next(ring)
        next(packs)
        next(ring)
        finish(packs)
        finish(swap)
        hidden[...] = wide(rows_low[...])

        def main():
            normed, _ = normed_of(hidden[...])
            first[...] = low(normed * vector_of(vectors, 0, 0) + vector_of(vectors, 0, 1))
            yield from gather_line(where, first, full, *line, lambda rows: None)
            finish(ring)
            for tile in range(CAP // TILE):
                join_rows(slice(tile * TILE, (tile + 1) * TILE), full, weights, qkv, vectors, 0, number)
            spreading = spread_line(where, part, middle, *spread)
            yield from attend_rows(c, qkv, ends, number, probs, heads, part, weights, spreading)
            yield from spreading
            middle[...] = middle[...] + hidden[...] + vector_of(vectors, 0, 4)

        weave(main(), (ring, (2,)), *weights_cargo(where, n, owns, fulls, sems, (1, 3, 5, 9), (1, 3, 5, 9)))

    tile = (32, 128)
    return call(
        body,
        "enter_attend",
        0,
        [pl.BlockSpec(memory_space=pltpu.HBM)] + [INSIDE] * (2 + n),
        [(VECTORS, INSIDE), (ENDS, INSIDE), (ROWS_WIDE, INSIDE), (FULL_CHUNK, INSIDE)]
        + ATTEND_OUTS
        + [(FULL_CHUNK, INSIDE)] * n,
        [
            pltpu.VMEM((CAP, 128), jnp.float32),
            pltpu.SemaphoreType.DMA,
            COLUMN_SCRATCH,
            ROW_SCRATCH,
            ROW_SCRATCH,
            pltpu.VMEM((CAP, D), jnp.bfloat16),
            pltpu.VMEM((2,) + tile, jnp.float32),
            pltpu.VMEM(tile, jnp.float32),
            pltpu.VMEM((7,) + tile, jnp.float32),
        ]
        + LINE_SEMS
        + spread_scratch()
        + SWAP_SEMS
        + RING_SEMS * (1 + n)
        + [
            pltpu.SemaphoreType.DMA((9,)),
            pltpu.SemaphoreType.DMA((9,)),
            pltpu.SemaphoreType.DMA((7,)),
            pltpu.SemaphoreType.DMA((8,)),
        ],
        (columns, pack, joined, *chunks),
    )


def attend_forward(layer, number, hidden, vectors, ends, weights, chunks, columns):
    n = len(chunks)

    def body(hidden, vectors, ends, weights, *rest):
        owns, rest = rest[:n], rest[n:]
        (columns, full, qkv, probs, heads, middle), rest = rest[:6], rest[6:]
        fulls, rest = rest[:n], rest[n:]
        (swapped, first, part), rest = rest[:3], rest[3:]
        line, rest = rest[:3], rest[3:]
        spread, rest = rest[:6], rest[6:]
        sems, rest = rest[: 2 * n], rest[2 * n :]
        columns_low, *swap_sems = rest
        where = place()
        h, x, zl, y, c = where
        count = greet_line(where) + greet_ring(where, True) + greet_swap(where, True)
        part_number = c * 4 + x
        columns_low[...] = low(columns[...])
        normed, _ = normed_of(hidden[...])
        first[...] = low(normed * vector_of(vectors, layer, 0) + vector_of(vectors, layer, 1))
        await_greetings(count)

        def ready(rows):
            join_rows(rows, full, weights, qkv, vectors, layer, part_number)

        def main():
            yield from gather_line(where, first, full, *line, ready)
            spreading = spread_line(where, part, middle, *spread)
            yield from attend_rows(c, qkv, ends, part_number, probs, heads, part, weights, spreading)
            yield from spreading
            middle[...] = middle[...] + hidden[...] + vector_of(vectors, layer, 4)

        weave(
            main(),
            *weights_cargo(where, n, owns, fulls, sems, (0, 2, 4, 8), (0, 2, 5, 9)),
            (swap_in(where, ((columns_low, swapped),), *swap_sems), (4,)),
        )

    return call(
        body,
        "attend_forward",
        number,
        [INSIDE] * (5 + n),
        ATTEND_OUTS + [(FULL_CHUNK, INSIDE)] * n + [(ROWS_LOW, INSIDE)],
        [ROW_SCRATCH, pltpu.VMEM((CAP, D), jnp.bfloat16)]
        + LINE_SEMS
        + spread_scratch()
        + RING_SEMS * n
        + [COLUMN_SCRATCH]
        + SWAP_SEMS,
        (hidden, vectors, ends, weights, *chunks, columns),
    )


def gelu_pair(values):
    square = values * values
    bent = jnp.tanh(0.7978845608028654 * values * (1.0 + 0.044715 * square))
    half = 0.5 * (1.0 + bent)
    bend = 0.7978845608028654 * (1.0 + 3.0 * 0.044715 * square)
    return low(values * half), low(half + 0.5 * values * (1.0 - bent * bent) * bend)


def feed_forward(layer, number, middle, vectors, up, down, chunks):
    n = len(chunks)

    def body(middle, vectors, up, down, *rest):
        owns, rest = rest[:n], rest[n:]
        (full, activated, slope, hidden), rest = rest[:4], rest[4:]
        fulls, rest = rest[:n], rest[n:]
        (second, part), rest = rest[:2], rest[2:]
        line, rest = rest[:3], rest[3:]
        spread, sems = rest[:6], rest[6:]
        where = place()
        h, x, zl, y, c = where
        count = greet_line(where)
        if n:
            count = count + greet_ring(where, True)
        normed, _ = normed_of(middle[...])
        second[...] = low(normed * vector_of(vectors, layer, 5) + vector_of(vectors, layer, 6))
        await_greetings(count)
        bias = up_bias_of(vectors, layer, c * 4 + x)

        def vector(index):
            return vector_of(vectors, layer, index)

        def ready(rows):
            values = dot(full[rows, :], up[...]) + bias
            active, slope[rows, :] = gelu_pair(values)
            activated[rows, :] = active
            part[rows, :] = low(dot_t(active, down[...]))

        def main():
            spreading = spread_line(where, part, hidden, *spread)
            yield from gather_line(where, second, full, *line, ready)
            yield from spreading
            hidden[...] = hidden[...] + middle[...] + vector(7)

        weave(main(), *weights_cargo(where, n, owns, fulls, sems, (0, 2, 5, 6)))

    return call(
        body,
        "feed_forward",
        number,
        [INSIDE] * (4 + n),
        [
            (FULL_ROWS, INSIDE),
            (of((CAP, CHUNK)), INSIDE),
            (of((CAP, CHUNK)), INSIDE),
            (ROWS_WIDE, INSIDE),
        ]
        + [(FULL_CHUNK, INSIDE)] * n,
        [pltpu.VMEM((ROWS, D), jnp.bfloat16), pltpu.VMEM((CAP, D), jnp.bfloat16)]
        + LINE_SEMS
        + spread_scratch()
        + RING_SEMS * n,
        (middle, vectors, up, down, *chunks),
    )


def feed_both(layer, number, middle, vectors, up, down, cotangent):
    def body(
        middle, vectors, up, down, cotangent,
        hidden, grad_middle, down_grad, up_grad, small, small_own,
        second, second_full, activated, slope, part, full, grad_up, grad_part, *rest,
    ):
        line, rest = rest[:3], rest[3:]
        grad_line, rest = rest[:3], rest[3:]
        spread, grad_spread = rest[:6], rest[6:]
        where = place()
        h, x, zl, y, c = where
        count = greet_line(where)
        normed, _ = normed_of(middle[...])
        second[...] = low(normed * vector_of(vectors, layer, 5) + vector_of(vectors, layer, 6))
        await_greetings(count)
        bias = up_bias_of(vectors, layer, c * 4 + x)

        def vector(index):
            return vector_of(vectors, layer, index)

        def ready(rows):
            values = dot(second_full[rows, :], up[...]) + bias
            activated[rows, :], slope[rows, :] = gelu_pair(values)
            part[rows, :] = low(dot_t(activated[rows, :], down[...]))

        def ready_back(rows):
            grad_low = low(dot(full[rows, :], down[...]) * wide(slope[rows, :]))
            grad_up[rows, :] = grad_low
            grad_part[rows, :] = low(dot_t(grad_low, up[...]))

        def weight_grads():
            for tile in range(D // TILE):
                columns = slice(tile * TILE, (tile + 1) * TILE)
                down_grad[columns, :] = low(t_dot(full[:, columns], activated[...]))
                up_grad[columns, :] = low(t_dot(second_full[:, columns], grad_up[...]))
                if tile % 2:
                    yield
            total = jnp.sum(wide(grad_up[...]), axis=0, keepdims=True)
            small_own[...] = jnp.zeros_like(small_own)
            for index in range(CHUNK // 128):
                small_own[index : index + 1, :] = total[:, index * 128 : (index + 1) * 128]

        spread_forth = spread_line(where, part, hidden, *spread)
        spread_back = spread_line(where, grad_part, grad_middle, *grad_spread)
        forth = gather_line(where, second, second_full, *line, ready)
        back = gather_line(where, cotangent, full, *grad_line, ready_back)
        next(forth)
        next(forth)
        next(back)
        finish(forth)
        next(spread_forth)
        next(back)
        next(spread_forth)
        finish(back)
        next(spread_back)
        next(spread_forth)
        next(spread_back)
        finish(spread_forth)
        hidden[...] = hidden[...] + middle[...] + vector(7)
        finish(side_by_side(spread_back, weight_grads()))
        grad_next = wide(cotangent[...])
        gain, shift, grad = norm_back(grad_middle[...], middle[...], vector(5))
        small[...] = jnp.zeros_like(small)
        small[0:1, :] = gain
        small[1:2, :] = shift
        small[2:3, :] = jnp.sum(grad_next, axis=0, keepdims=True)
        grad_middle[...] = grad_next + grad

    return call(
        body,
        "feed_both",
        number,
        [INSIDE] * 5,
        [
            (ROWS_WIDE, INSIDE),
            (ROWS_WIDE, INSIDE),
            (FULL_CHUNK, INSIDE),
            (FULL_CHUNK, INSIDE),
            (SMALL, INSIDE),
            (SMALL_OWN, INSIDE),
        ],
        [
            ROW_SCRATCH,
            pltpu.VMEM((CAP, D), jnp.bfloat16),
            pltpu.VMEM((CAP, CHUNK), jnp.bfloat16),
            pltpu.VMEM((CAP, CHUNK), jnp.bfloat16),
            pltpu.VMEM((CAP, D), jnp.bfloat16),
            pltpu.VMEM((CAP, D), jnp.bfloat16),
            pltpu.VMEM((CAP, CHUNK), jnp.bfloat16),
            pltpu.VMEM((CAP, D), jnp.bfloat16),
        ]
        + LINE_SEMS * 2
        + spread_scratch() * 2,
        (middle, vectors, up, down, cotangent),
    )


def feed_backward(layer, number, grad_next, vectors, middle, up, down, second_full, activated, slope, chunks):
    n = len(chunks)

    def body(grad_next, vectors, middle, up, down, second_full, activated, slope, *rest):
        parts, rest = rest[:n], rest[n:]
        (grad_middle, down_grad, up_grad, small, small_own), rest = rest[:5], rest[5:]
        owns, rest = rest[:n], rest[n:]
        (rows_low, full, grad_up, part), rest = rest[:4], rest[4:]
        line, rest = rest[:3], rest[3:]
        spread, rest = rest[:6], rest[6:]
        where = place()
        count = greet_line(where)
        if n:
            count = count + greet_ring(where, False)
        rows_low[...] = low(grad_next[...])
        await_greetings(count)

        def ready(rows):
            grad_act = dot(full[rows, :], down[...])
            grad_low = low(grad_act * wide(slope[rows, :]))
            grad_up[rows, :] = grad_low
            part[rows, :] = low(dot_t(grad_low, up[...]))

        def weight_grads():
            for tile in range(D // TILE):
                columns = slice(tile * TILE, (tile + 1) * TILE)
                down_grad[columns, :] = low(t_dot(full[:, columns], activated[...]))
                up_grad[columns, :] = low(t_dot(second_full[:, columns], grad_up[...]))
                if tile % 2:
                    yield
            total = jnp.sum(wide(grad_up[...]), axis=0, keepdims=True)
            small_own[...] = jnp.zeros_like(small_own)
            for index in range(CHUNK // 128):
                small_own[index : index + 1, :] = total[:, index * 128 : (index + 1) * 128]

        def main():
            spreading = spread_line(where, part, grad_middle, *spread)
            yield from gather_line(where, rows_low, full, *line, ready)
            next(spreading)
            yield
            yield from side_by_side(spreading, weight_grads())
            gain, shift, grad = norm_back(
                grad_middle[...], middle[...], vectors[8 * layer + 5 : 8 * layer + 6, :]
            )
            small[...] = jnp.zeros_like(small)
            small[0:1, :] = gain
            small[1:2, :] = shift
            small[2:3, :] = jnp.sum(wide(rows_low[...]), axis=0, keepdims=True)
            grad_middle[...] = grad_next[...] + grad

        weave(main(), *grads_cargo(where, n, parts, owns, rest, (0, 2, 5, 7)))

    return call(
        body,
        "feed_backward",
        number,
        [INSIDE] * (8 + n),
        [
            (ROWS_WIDE, INSIDE),
            (FULL_CHUNK, INSIDE),
            (FULL_CHUNK, INSIDE),
            (SMALL, INSIDE),
            (SMALL_OWN, INSIDE),
        ]
        + [(OWN_CHUNK, INSIDE)] * n,
        [
            pltpu.VMEM((ROWS, D), jnp.bfloat16),
            pltpu.VMEM((CAP, D), jnp.bfloat16),
            pltpu.VMEM((CAP, CHUNK), jnp.bfloat16),
            pltpu.VMEM((CAP, D), jnp.bfloat16),
        ]
        + LINE_SEMS
        + spread_scratch()
        + scatter_scratch(DEPTH, (CHUNK,), jnp.bfloat16) * n,
        (grad_next, vectors, middle, up, down, second_full, activated, slope, *chunks),
    )


SUMS = 32


def sum_vectors(where, small, own, total, taken, turned, across, last, out, part_send, part_recv, send, recv):
    h, x, zl, y, c = where
    home = lax.rem(h + c, 2) == 0
    beside = device(h, x, 1 - zl, y, c)
    pairs = [(j, d) for j in range(4) for d in range(2) if j or d]
    started = []

    def go(*args):
        item = push(*args)
        item.start()
        started.append(item)

    for index, (j, d) in enumerate(pairs):
        xx, cc = turn(x, j, 4), turn(c, d, 2)
        go(
            small.at[:, rows_at((cc * 4 + xx) * 128, 128)],
            taken.at[index],
            part_send.at[index],
            part_recv.at[index],
            device(h, xx, zl, y, cc),
        )
    yield
    value = small[:, rows_at((c * 4 + x) * 128, 128)]
    for index in range(7):
        landed(taken.at[index], part_send.at[index], part_recv.at[index])
        value = value + taken[index]
    total[0, :SUMS] = value
    total[0, SUMS:] = own[...]
    for step in (1, 2, 3):
        go(
            total.at[0],
            turned.at[step - 1],
            send.at[step - 1],
            recv.at[step - 1],
            device(h, x, zl, turn(y, step, 4), c),
        )
    yield
    for step in (1, 2, 3):
        landed(turned.at[step - 1], send.at[step - 1], recv.at[step - 1])
    total[1] = total[0] + turned[0] + turned[1] + turned[2]
    go(total.at[1], across, send.at[3], recv.at[3], beside)
    yield
    landed(across, send.at[3], recv.at[3])
    total[2] = total[1] + across[...]
    for d in range(2):
        args = (
            total.at[2],
            last.at[h],
            send.at[4 + d],
            recv.at[4 + h],
            device(c, x, zl, y, turn(c, d, 2)),
        )
        if d == 0:
            move(*args, home)
        else:
            go(*args)
    yield
    for d in range(2):
        hh = turn(h, d, 2)
        args = (last.at[hh], send.at[4 + d], recv.at[4 + hh])
        if d == 0:
            moved_in(*args, home)
        else:
            landed(*args)
    out[...] = last[0] + last[1]
    for item in started:
        item.wait_send()
    moved_out(total.at[2], send.at[4], recv.at[4], beside, home)


def attend_backward(
    layer, number, grad_middle, vectors, hidden, weights, first_full, qkv, probs, heads, chunks,
    output=None, smalls=None,
):
    n = len(chunks)
    swaps = output is not None
    final = smalls is not None

    def body(grad_middle, vectors, hidden, weights, first_full, qkv, probs, heads, *rest):
        parts, rest = rest[:n], rest[n:]
        if swaps:
            output, rest = rest[0], rest[1:]
        if final:
            others, rest = rest[:6], rest[6:]
            (columns, weight_sum, totals), rest = rest[:3], rest[3:]
        else:
            (grad_hidden, weight_grad, small, small_own), rest = rest[:4], rest[4:]
        owns, rest = rest[:n], rest[n:]
        if swaps:
            columns, rest = rest[0], rest[1:]
        (rows_low, full, grad_heads, grad_joined, grad_key, grad_value, part), rest = rest[:7], rest[7:]
        line, rest = rest[:3], rest[3:]
        spread, rest = rest[:6], rest[6:]
        cargo, rest = rest[: 9 * n], rest[9 * n :]
        if final:
            (grad_hidden, weight_grad, small_all, own_all), rest = rest[:4], rest[4:]
            ring_scratch, rest = rest[:9], rest[9:]
            sum_scratch, rest = rest[:9], rest[9:]
            small, small_own = small_all.at[pl.ds(8, 8)], own_all.at[pl.ds(8, 8)]
        where = place()
        h, x, zl, y, c = where
        count = greet_ring(where, False)
        if final:
            greet(device(h, x, zl, turn(y, 2, 4), c))
            count = count + 1 + greet_parts(where)
        else:
            count = count + greet_line(where)
        if swaps or final:
            count = count + greet_swap(where, False)
            rows_out, columns_low, *swap_sems = rest
        rows_low[...] = low(grad_middle[...])
        await_greetings(count)
        planned = grads_cargo(where, n, parts, owns, cargo, (0, 2, 7, 10), (0, 3, 8, 11))
        if swaps:
            rows_out[...] = low(output[...])
            planned.append((swap_out(where, ((rows_out, columns_low),), *swap_sems), (4,)))

        def ready(rows):
            grad_heads[rows, :] = low(dot(full[rows, :], weights[:, 3 * PAIR :]))

        def weight_grads():
            for tile in range(D // TILE):
                features = slice(tile * TILE, (tile + 1) * TILE)
                weight_grad[features, : 3 * PAIR] = low(
                    t_dot(first_full[:, features], grad_joined[...])
                )
                weight_grad[features, 3 * PAIR :] = low(t_dot(full[:, features], heads[...]))
                if tile % 2:
                    yield
            total = jnp.sum(wide(grad_joined[...]), axis=0, keepdims=True)
            small_own[...] = jnp.zeros(small_own.shape, jnp.float32)
            small_own[0:1, :] = total[:, :PAIR]
            small_own[1:2, :] = total[:, 2 * PAIR :]

        def norm_end():
            gain, shift, grad = norm_back(grad_hidden[...], hidden[...], vector_of(vectors, layer, 0))
            small[...] = jnp.zeros(small.shape, jnp.float32)
            small[0:1, :] = gain
            small[1:2, :] = shift
            small[2:3, :] = jnp.sum(wide(rows_low[...]), axis=0, keepdims=True)
            grad_hidden[...] = grad_middle[...] + grad

        def last_steps(spreading):
            for index, first in enumerate((0, 16, 24)):
                small_all[first : first + 8, :] = others[2 * index][...]
                own_all[first : first + 8, :] = others[2 * index + 1][...]
            next(spreading)
            finish(weight_grads())
            ring = scatter_ring(where, rows_view(weight_grad), DEPTH, weight_sum, *ring_scratch)
            next(ring)
            yield
            next(spreading)
            yield
            next(ring)
            next(spreading)
            yield
            finish(spreading)
            norm_end()
            rows_out[...] = low(grad_hidden[...])
            sums = sum_vectors(where, small_all, own_all, *sum_scratch[:5], totals, *sum_scratch[5:])
            next(sums)
            swap = swap_out(where, ((rows_out, columns_low),), *swap_sems)
            next(swap)
            next(ring)
            next(sums)
            next(ring)
            next(sums)
            next(sums)
            finish(ring)
            finish(swap)
            columns[...] = wide(columns_low[...])
            finish(sums)

        def main():
            yield from gather_line(where, rows_low, full, *line, ready)
            masks = head_masks()
            grad_key[...] = jnp.zeros_like(grad_key)
            grad_value[...] = jnp.zeros_like(grad_value)
            for tile in range(CAP // TILE):
                rows, keys = slice(tile * TILE, (tile + 1) * TILE), (tile + 1) * TILE
                query, grad = wide(qkv[rows, :PAIR]), wide(grad_heads[rows, :])
                key, value = qkv[:keys, PAIR : 2 * PAIR], qkv[:keys, 2 * PAIR :]
                grad_query = 0.0
                for head in range(2):
                    grad_one = low(grad * masks[head])
                    soft_low = probs[head, :, probs_at(tile)]
                    soft = wide(soft_low)
                    grad_probs = dot_t(grad_one, value)
                    inner = jnp.sum(soft * grad_probs, axis=1, keepdims=True)
                    grad_scores = low(soft * (grad_probs - inner))
                    grad_query = grad_query + dot(grad_scores, key) * masks[head]
                    grad_key[:keys, :] += t_dot(grad_scores, low(query * masks[head]))
                    grad_value[:keys, :] += t_dot(soft_low, grad_one)
                grad_joined[rows, :PAIR] = low(grad_query * HDIM ** (-0.5))
                yield
            spreading = spread_line(where, part, grad_hidden, *spread)
            for step in range(CAP // TILE):
                rows = rows_at(turn((1 - c) * 2, step, 4) * TILE, TILE)
                grad_joined[rows, PAIR : 2 * PAIR] = low(grad_key[rows, :])
                grad_joined[rows, 2 * PAIR :] = low(grad_value[rows, :])
                part[rows, :] = low(dot_t(grad_joined[rows, :], weights[:, : 3 * PAIR]))
                if step == 1:
                    next(spreading)
            if final:
                yield from last_steps(spreading)
                return
            yield
            yield from side_by_side(spreading, weight_grads())
            norm_end()

        weave(main(), *planned)
        if swaps:
            columns[...] = wide(columns_low[...])

    rows = (2 * SUMS, 128)
    scatter = scatter_scratch(DEPTH, (CHUNK,), jnp.bfloat16)
    if final:
        outs = [(COLUMNS, INSIDE), (OWN_CHUNK, INSIDE), (of(rows, jnp.float32), INSIDE)]
        extra = (
            [
                pltpu.VMEM((ROWS, D), jnp.float32),
                pltpu.VMEM((D, CHUNK), jnp.bfloat16),
                pltpu.VMEM((SUMS, D), jnp.float32),
                pltpu.VMEM((SUMS, 128), jnp.float32),
            ]
            + scatter
            + [
                pltpu.VMEM((3,) + rows, jnp.float32),
                pltpu.VMEM((7, SUMS, 128), jnp.float32),
                pltpu.VMEM((3,) + rows, jnp.float32),
                pltpu.VMEM(rows, jnp.float32),
                pltpu.VMEM((2,) + rows, jnp.float32),
                pltpu.SemaphoreType.DMA((7,)),
                pltpu.SemaphoreType.DMA((7,)),
                pltpu.SemaphoreType.DMA((6,)),
                pltpu.SemaphoreType.DMA((6,)),
            ]
        )
    else:
        outs = [(ROWS_WIDE, INSIDE), (FULL_CHUNK, INSIDE), (SMALL, INSIDE), (SMALL_OWN, INSIDE)]
        extra = []
    return call(
        body,
        "attend_backward_last" if final else "attend_backward",
        number,
        [INSIDE] * (8 + n + swaps + 6 * final),
        outs + [(OWN_CHUNK, INSIDE)] * n + [(COLUMNS, INSIDE)] * swaps,
        [
            ROW_SCRATCH,
            pltpu.VMEM((CAP, D), jnp.bfloat16),
            pltpu.VMEM((CAP, PAIR), jnp.bfloat16),
            pltpu.VMEM((CAP, 3 * PAIR), jnp.bfloat16),
            pltpu.VMEM((CAP, PAIR), jnp.float32),
            pltpu.VMEM((CAP, PAIR), jnp.float32),
            pltpu.VMEM((CAP, D), jnp.bfloat16),
        ]
        + LINE_SEMS
        + spread_scratch()
        + scatter * n
        + extra
        + ([ROW_SCRATCH, COLUMN_SCRATCH] + SWAP_SEMS) * (swaps or final),
        (
            grad_middle, vectors, hidden, weights, first_full, qkv, probs, heads, *chunks,
            *([output] if swaps else []), *(smalls if final else []),
        ),
    )


def local_call(body, name, ins, outs, args):
    return pl.pallas_call(
        body,
        out_shape=tuple(outs),
        in_specs=ins,
        out_specs=tuple(INSIDE for _ in outs),
        compiler_params=pltpu.CompilerParams(vmem_limit_bytes=VMEM_BYTES),
        name=name,
    )(*args)


def reorder(value, order):
    return jnp.concatenate([value[:, i * HDIM : (i + 1) * HDIM] for i in order], axis=1)


def prepare(lengths, small, joined, out_turned):
    def body(lengths, small, joined, out_turned, pack, joined_out):
        row = lax.axis_index("row")
        values = wide(small[...])
        stacked = jnp.concatenate(
            [
                values[layer : layer + 1, 8 * i : 8 * i + 8]
                for layer in range(LAYERS)
                for i in range(8)
            ],
            axis=0,
        )
        lane = lax.broadcasted_iota(jnp.int32, (8, 128), 1)
        index = lax.broadcasted_iota(jnp.int32, (8, 128), 0)
        pack[0:16, :] = dot(low(stacked), low(wide(lane == row * 8 + index)))
        lane = lax.broadcasted_iota(jnp.int32, (32, 128), 1)
        index = lax.broadcasted_iota(jnp.int32, (32, 128), 0)
        placed = wide(lane == lax.rem(row, 4) * 32 + index)
        value = dot(low(values[:, 64:96]), low(placed))
        for quarter in range(4):
            here = wide(jnp.full((1, 128), quarter, jnp.int32) == lax.div(row, 4))
            for layer in range(LAYERS):
                at = 16 + 4 * layer + quarter
                pack[at : at + 1, :] = value[layer : layer + 1] * here
        lane = lax.broadcasted_iota(jnp.int32, (8, 128), 1)
        value = jnp.zeros((8, 128), jnp.float32)
        for slot in range(4):
            value = jnp.where(lane == slot, lengths[0, slot].astype(jnp.float32), value)
        pack[24:32, :] = value
        for layer in range(LAYERS):
            turned = reorder(wide(joined[layer]), (0, 3, 1, 4, 2, 5))
            joined_out[layer, :, : 3 * PAIR] = low(turned)
            joined_out[layer, :, 3 * PAIR :] = out_turned[layer]

    return local_call(
        body,
        "prepare",
        [pl.BlockSpec(memory_space=pltpu.SMEM)] + [INSIDE] * 3,
        [of((32, 128), jnp.float32), of((LAYERS, DEPTH, CHUNK))],
        (lengths, small, joined, out_turned),
    )


def settle(hidden, grad, joined, up, down, totals):
    def body(hidden, grad, joined_0, joined_1, up_0, up_1, down_0, down_1, totals, *outs):
        hidden_out, grad_out, joined_out, query, value, out_out, out_bias, first_gain, first_shift = outs[:9]
        up_out, up_bias, down_out, down_bias, second_gain, second_shift = outs[9:]
        row = lax.axis_index("row")
        hidden_out[...] = hidden[...]
        grad_out[...] = grad[...]
        for layer, ref in enumerate((joined_0, joined_1)):
            joined_out[layer] = reorder(ref[:, : 3 * PAIR], (0, 2, 4, 1, 3, 5))
            out_out[layer] = ref[:, 3 * PAIR :]
        for layer, ref in enumerate((up_0, up_1)):
            up_out[layer] = ref[...]
        for layer, ref in enumerate((down_0, down_1)):
            down_out[layer] = ref[...]
        turned = pltpu.roll(totals[...], lax.rem(128 - row * 8, 128), 1)
        places = (
            (second_gain, 0), (second_shift, 1), (down_bias, 2),
            (first_gain, 8), (first_shift, 9), (out_bias, 10),
            (query, SUMS + 8), (value, SUMS + 9),
        )
        for ref, at in places:
            for layer in range(LAYERS):
                ref[layer : layer + 1, :] = turned[at + 16 * layer : at + 16 * layer + 1, :8]
        for layer in range(LAYERS):
            block = totals[SUMS + 16 * layer : SUMS + 16 * layer + 8, :]
            index = lax.broadcasted_iota(jnp.int32, (8, 128), 0)
            line = jnp.sum(jnp.where(index == lax.div(row, 4), block, 0.0), axis=0, keepdims=True)
            line = pltpu.roll(jnp.broadcast_to(line, (8, 128)), lax.rem(128 - lax.rem(row, 4) * 32, 128), 1)
            up_bias[layer : layer + 1, :] = line[0:1, :32]

    vector = of((LAYERS, 8), jnp.float32)
    return local_call(
        body,
        "settle",
        [INSIDE] * 9,
        [
            COLUMNS,
            COLUMNS,
            of((LAYERS, DEPTH, 3 * PAIR), jnp.float32),
            vector,
            vector,
            of((LAYERS, DEPTH, PAIR), jnp.float32),
            vector,
            vector,
            vector,
            of((LAYERS, DEPTH, CHUNK), jnp.float32),
            of((LAYERS, 32), jnp.float32),
            of((LAYERS, DEPTH, CHUNK), jnp.float32),
            vector,
            vector,
            vector,
        ],
        (hidden, grad, *joined, *up, *down, totals),
    )


def shards(
    hidden_in,
    joined_weight,
    query_bias,
    value_bias,
    out_weight,
    out_bias,
    first_gain,
    first_shift,
    up_weight,
    up_bias,
    down_weight,
    down_bias,
    second_gain,
    second_shift,
    seq_lengths,
    cotangent,
):
    small = jnp.concatenate(
        [
            first_gain,
            first_shift,
            query_bias,
            value_bias,
            out_bias,
            second_gain,
            second_shift,
            down_bias,
            up_bias,
        ],
        axis=1,
    )
    pack, joined_out = prepare(seq_lengths, small, joined_weight, jnp.swapaxes(out_weight, 1, 2))
    down_turned = jnp.swapaxes(down_weight, 1, 2)
    (
        vectors, ends, input_0, joined_0, full_10, qkv_0, probs_0, heads_0, middle_0, up_0, down_0,
    ) = enter_attend(hidden_in, pack, joined_out[0], [up_weight[0], down_turned[0]])
    full_20, active_0, slope_0, hidden, joined_1 = feed_forward(
        0, 2, middle_0, vectors, up_0, down_0, [joined_out[1]]
    )
    input_1 = hidden
    full_11, qkv_1, probs_1, heads_1, middle_1, up_1, down_1, cotangent_rows = attend_forward(
        1, 3, hidden, vectors, ends, joined_1, [up_weight[1], down_turned[1]], cotangent
    )
    hidden, grad_middle, down_part, up_part, feed_small_1, feed_own_1 = feed_both(
        1, 4, middle_1, vectors, up_1, down_1, cotangent_rows
    )
    (
        grad_hidden, joined_part, attend_small_1, attend_own_1, down_sum_1, up_sum_1, hidden_out,
    ) = attend_backward(
        1, 6, grad_middle, vectors, input_1, joined_1, full_11, qkv_1, probs_1, heads_1,
        [down_part, up_part], hidden,
    )
    grad_middle, down_part, up_part, feed_small_0, feed_own_0, joined_sum_1 = feed_backward(
        0, 7, grad_hidden, vectors, middle_0, up_0, down_0, full_20, active_0, slope_0, [joined_part]
    )
    grad_out, joined_sum_0, totals, down_sum_0, up_sum_0 = attend_backward(
        0, 8, grad_middle, vectors, input_0, joined_0, full_10, qkv_0, probs_0, heads_0,
        [down_part, up_part],
        smalls=[
            feed_small_0, feed_own_0, feed_small_1, feed_own_1, attend_small_1, attend_own_1,
        ],
    )
    outs = list(
        settle(
            hidden_out,
            grad_out,
            (joined_sum_0, joined_sum_1),
            (up_sum_0, up_sum_1),
            (down_sum_0, down_sum_1),
            totals,
        )
    )
    outs[5] = jnp.swapaxes(outs[5], 1, 2)
    outs[11] = jnp.swapaxes(outs[11], 1, 2)
    return tuple(outs)


def solution(mesh):
    vector = P(None, ("col", "row"))
    return jax.shard_map(
        shards,
        mesh=mesh,
        in_specs=(
            P("row", "col"),
            P(None, "row", "col"),
            vector,
            vector,
            P(None, "col", "row"),
            vector,
            vector,
            vector,
            P(None, "row", "col"),
            vector,
            P(None, "col", "row"),
            vector,
            vector,
            vector,
            P("row", None),
            P("row", "col"),
        ),
        out_specs=(
            P("row", "col"),
            P("row", "col"),
            P(None, "row", "col"),
            vector,
            vector,
            P(None, "col", "row"),
            vector,
            vector,
            vector,
            P(None, "row", "col"),
            vector,
            P(None, "col", "row"),
            vector,
            vector,
            vector,
        ),
        check_vma=False,
    )
```

```python
import functools

import jax
import jax.numpy as jnp
from jax import lax
from jax.experimental import pallas as pl
from jax.experimental.pallas import tpu as pltpu
from jax.sharding import PartitionSpec as P

D = 1024
HEADS = 16
HDIM = 64
FF = 4096
LAYERS = 2
CAP = 1024
PARTS = 8
ROWS = CAP // PARTS
LOCAL_HEADS = HEADS // PARTS
EPS = 1e-05
NEG = -1000000000.0
MESH = pl.DeviceIdType.MESH


def place():
    row = lax.axis_index("row")
    col = lax.axis_index("col")
    return (
        lax.div(col, 4),
        lax.rem(col, 4),
        lax.div(row, 8),
        lax.div(lax.rem(row, 8), 2),
        lax.rem(row, 2),
    )


def device(h, x, zl, y, c):
    return (zl * 8 + y * 2 + c, h * 4 + x)


def turn(value, by, size):
    return lax.rem(value + by, size)


def rows_at(start, size):
    return pl.ds(pl.multiple_of(start, size), size)


def push(src, dst, send_sem, recv_sem, target):
    return pltpu.make_async_remote_copy(
        src_ref=src,
        dst_ref=dst,
        send_sem=send_sem,
        recv_sem=recv_sem,
        device_id=target,
        device_id_type=MESH,
    )


def greet(target):
    pl.semaphore_signal(
        pltpu.get_barrier_semaphore(), inc=1, device_id=target, device_id_type=MESH
    )


def await_greetings(count):
    pl.semaphore_wait(pltpu.get_barrier_semaphore(), count)


def unless(flag, run):
    pl.when(jnp.logical_not(flag))(run)


def together(*parts):
    alive = list(parts)
    while alive:
        alive = [part for part in alive if next(part, alive) is not alive]


def weave(main, *planned):
    count = 0
    waiting = [[part, list(plan)] for part, plan in planned]

    def advance():
        for part, plan in waiting:
            while plan and plan[0] <= count:
                next(part, None)
                plan.pop(0)

    advance()
    for _ in main:
        count += 1
        advance()
    for part, _ in waiting:
        for _ in part:
            pass


def landed(view, send_sem, recv_sem):
    row, col = lax.axis_index("row"), lax.axis_index("col")
    push(view, view, send_sem, recv_sem, (row, lax.rem(col + 1, 8))).wait_recv()


def neighbours(where):
    h, x, zl, y, c = where
    return (
        device(h, turn(x, 1, 4), zl, y, c),
        device(h, turn(x, 3, 4), zl, y, c),
        device(h, x, zl, y, 1 - c),
    )


def greet_line(where):
    for other in neighbours(where):
        greet(other)
    return 3


def greet_ring(where, inward):
    h, x, zl, y, c = where
    home = lax.rem(h + c, 2) == 0
    for d in range(2):
        if inward:
            source = device(c, x, zl, y, turn(c, d, 2))
        else:
            source = device(turn(h, d, 2), x, zl, y, h)
        if d == 0:
            unless(home, functools.partial(greet, source))
        else:
            greet(source)
    for step in (1, 3):
        greet(device(h, x, zl, turn(y, step, 4), c))
    greet(device(h, x, 1 - zl, y, c))
    return 4 + lax.rem(h + c, 2)


def greet_swap(where, inward):
    h, x, zl, y, c = where
    home = lax.rem(h + c, 2) == 0
    for j in range(4):
        for d in range(2):
            if inward:
                source = device(turn(h, d, 2), turn(x, j, 4), zl, y, h)
            else:
                source = device(c, turn(x, j, 4), zl, y, turn(c, d, 2))
            if j == 0 and d == 0:
                unless(home, functools.partial(greet, source))
            else:
                greet(source)
    return 7 + lax.rem(h + c, 2)


def greet_parts(where):
    h, x, zl, y, c = where
    for j in range(4):
        for d in range(2):
            if j or d:
                greet(device(h, turn(x, j, 4), zl, y, turn(c, d, 2)))
    return 7


def move(src, dst, send_sem, recv_sem, target, home):
    unless(home, push(src, dst, send_sem, recv_sem, target).start)
    pl.when(home)(lambda: pltpu.make_async_copy(src, dst, recv_sem).start())


def moved_in(dst, send_sem, recv_sem, home):
    unless(home, functools.partial(landed, dst, send_sem, recv_sem))
    pl.when(home)(lambda: pltpu.make_async_copy(dst, dst, recv_sem).wait())


def moved_out(src, send_sem, recv_sem, target, home):
    unless(home, push(src, src, send_sem, recv_sem, target).wait_send)


def gather_line(where, src, out, own_sem, send, recv, ready):
    h, x, zl, y, c = where
    right, left, mate = neighbours(where)
    half = ROWS // 2

    def span(core, step, first=0, size=ROWS):
        return rows_at((core * 4 + turn(x, step, 4)) * ROWS + first, size)

    def block(*args):
        return out.at[span(*args)]

    started = []

    def copy(index, view, target, source=None):
        source = view if source is None else source
        item = push(source, view, send.at[index], recv.at[index], target)
        item.start()
        started.append(item)

    def arrived(index, view):
        landed(view, send.at[index], recv.at[index])

    low, high = src.at[pl.ds(0, half)], src.at[pl.ds(half, half)]
    copy(0, block(c, 0, 0, half), right, low)
    copy(2, block(c, 0, half, half), left, high)
    copy(1, block(c, 0, half, half), right, high)
    copy(3, block(c, 0, 0, half), left, low)
    copy(4, block(c, 0), mate, src)
    own = pltpu.make_async_copy(src, block(c, 0), own_sem)
    own.start()
    yield
    own.wait()
    ready(span(c, 0))
    arrived(0, block(c, 3, 0, half))
    copy(5, block(c, 3, 0, half), right)
    arrived(2, block(c, 1, half, half))
    copy(6, block(c, 1, half, half), left)
    yield
    arrived(4, block(1 - c, 0))
    ready(span(1 - c, 0))
    arrived(1, block(c, 3, half, half))
    copy(7, block(c, 3), mate)
    arrived(3, block(c, 1, 0, half))
    copy(8, block(c, 1), mate)
    ready(span(c, 3))
    yield
    arrived(5, block(c, 2, 0, half))
    copy(9, block(c, 2, 0, half), mate)
    arrived(6, block(c, 2, half, half))
    copy(10, block(c, 2, half, half), mate)
    ready(span(c, 1))
    ready(span(c, 2))
    yield
    arrived(7, block(1 - c, 3))
    ready(span(1 - c, 3))
    arrived(8, block(1 - c, 1))
    ready(span(1 - c, 1))
    arrived(9, block(1 - c, 2, 0, half))
    arrived(10, block(1 - c, 2, half, half))
    ready(span(1 - c, 2))
    for item in started:
        item.wait_send()


LINE_SEMS = [
    pltpu.SemaphoreType.DMA,
    pltpu.SemaphoreType.DMA((11,)),
    pltpu.SemaphoreType.DMA((11,)),
]
RING_SEMS = [pltpu.SemaphoreType.DMA((9,)), pltpu.SemaphoreType.DMA((9,))]


def spread_line(where, part, out, core_in, sums, hop, final, send, recv):
    h, x, zl, y, c = where
    right, left, mate = neighbours(where)
    half, quarter = ROWS // 2, ROWS // 4

    def mine(core, step, first=0, size=ROWS):
        return part.at[rows_at((core * 4 + turn(x, step, 4)) * ROWS + first, size)]

    started = []

    def copy(index, source, view, target):
        item = push(source, view, send.at[index], recv.at[index], target)
        item.start()
        started.append(item)

    def arrived(index, view):
        landed(view, send.at[index], recv.at[index])

    def add(left_ref, right_ref):
        return wide(left_ref[...]) + wide(right_ref[...])

    for first in (0, half):
        rows = pl.ds(first, half)
        copy(1 if first else 0, mine(1 - c, 2, first, half), core_in.at[2, rows], mate)
    copy(2, mine(1 - c, 1), core_in.at[1], mate)
    copy(3, mine(1 - c, 3), core_in.at[3], mate)
    copy(4, mine(1 - c, 0), core_in.at[0], mate)
    yield
    for side, (first, target) in enumerate(((0, right), (half, left))):
        rows = pl.ds(first, half)
        arrived(side, core_in.at[2, rows])
        sums[2, first : first + half] = low(add(mine(c, 2, first, half), core_in.at[2, rows]))
        for piece in range(2):
            copy(
                5 + 2 * side + piece,
                sums.at[2, pl.ds(first + piece * quarter, quarter)],
                hop.at[side, pl.ds(piece * quarter, quarter)],
                target,
            )
    arrived(2, core_in.at[1])
    sums[1] = low(add(mine(c, 1), core_in.at[1]))
    copy(9, sums.at[1, pl.ds(half, half)], final.at[0, pl.ds(half, half)], right)
    arrived(3, core_in.at[3])
    sums[3] = low(add(mine(c, 3), core_in.at[3]))
    copy(10, sums.at[3, pl.ds(0, half)], final.at[1, pl.ds(0, half)], left)
    yield
    arrived(4, core_in.at[0])
    out[...] = add(mine(c, 0), core_in.at[0])
    for piece in range(2):
        for side, (block, first, target) in enumerate(((1, 0, right), (3, half, left))):
            taken = hop.at[side, pl.ds(piece * quarter, quarter)]
            start = first + piece * quarter
            rows = pl.ds(start, quarter)
            arrived(5 + 2 * side + piece, taken)
            sums[block, start : start + quarter] = low(add(sums.at[block, rows], taken))
            copy(11 + 2 * side + piece, sums.at[block, rows], final.at[side, rows], target)
    yield
    arrived(9, final.at[0, pl.ds(half, half)])
    arrived(10, final.at[1, pl.ds(0, half)])
    yield
    for piece in range(2):
        arrived(11 + piece, final.at[0, pl.ds(piece * quarter, quarter)])
        arrived(13 + piece, final.at[1, pl.ds(half + piece * quarter, quarter)])
    out[...] += wide(final[0]) + wide(final[1])
    for item in started:
        item.wait_send()


def spread_scratch():
    half = ROWS // 2
    return [
        pltpu.VMEM((4, ROWS, D), jnp.bfloat16),
        pltpu.VMEM((4, ROWS, D), jnp.bfloat16),
        pltpu.VMEM((2, half, D), jnp.bfloat16),
        pltpu.VMEM((2, ROWS, D), jnp.bfloat16),
        pltpu.SemaphoreType.DMA((15,)),
        pltpu.SemaphoreType.DMA((15,)),
    ]


def gather_ring(where, own, slot, send, recv):
    h, x, zl, y, c = where
    home = lax.rem(h + c, 2) == 0
    above = device(h, x, zl, turn(y, 1, 4), c)
    below = device(h, x, zl, turn(y, 3, 4), c)
    beside = device(h, x, 1 - zl, y, c)

    def piece(p, step):
        return slot(turn(zl, p, 2), turn(y, step, 4), 0, 2, c)

    def ring(index, view, target):
        push(view, view, send.at[index], recv.at[index], target).start()

    def arrived(index, view):
        landed(view, send.at[index], recv.at[index])

    for d in range(2):
        target = device(turn(h, d, 2), x, zl, y, h)
        args = (own, slot(zl, y, c, 1, h), send.at[d], recv.at[c], target)
        if d == 0:
            move(*args, home)
        else:
            push(*args).start()
    yield
    for d in range(2):
        cc = turn(c, d, 2)
        args = (slot(zl, y, cc, 1, c), send.at[d], recv.at[cc])
        if d == 0:
            moved_in(*args, home)
        else:
            landed(*args)
    ring(2, piece(0, 0), beside)
    ring(3, piece(0, 0), above)
    ring(5, piece(0, 0), below)
    yield
    arrived(2, piece(1, 0))
    ring(4, piece(1, 0), above)
    ring(6, piece(1, 0), below)
    yield
    arrived(3, piece(0, 3))
    ring(7, piece(0, 3), above)
    arrived(6, piece(1, 1))
    ring(8, piece(1, 1), below)
    yield
    arrived(4, piece(1, 3))
    arrived(5, piece(0, 1))
    arrived(7, piece(0, 2))
    arrived(8, piece(1, 2))
    moved_out(own, send.at[0], recv.at[0], beside, home)
    push(own, own, send.at[1], recv.at[1], beside).wait_send()
    for index in range(2, 9):
        push(piece(0, 0), piece(0, 0), send.at[index], recv.at[index], beside).wait_send()


def finish(part):
    for _ in part:
        pass


def gather_vectors(where, pack, vectors, ends, taken, mine, near, send, recv, part_send, part_recv):
    h, x, zl, y, c = where
    home = lax.rem(h + c, 2) == 0
    beside = device(h, x, 1 - zl, y, c)
    started = []

    def go(*args):
        item = push(*args)
        item.start()
        started.append(item)

    for d in range(2):
        args = (pack, taken.at[c], send.at[d], recv.at[c], device(turn(h, d, 2), x, zl, y, h))
        if d == 0:
            move(*args, home)
        else:
            go(*args)
    yield
    for d in range(2):
        cc = turn(c, d, 2)
        args = (taken.at[cc], send.at[d], recv.at[cc])
        if d == 0:
            moved_in(*args, home)
        else:
            landed(*args)
    mine[...] = taken[0] + taken[1]
    ends[...] = taken[h, 24:32, :]
    for index in range(1, 8):
        dz, dy = divmod(index, 4)
        other = device(h, x, turn(zl, dz, 2), turn(y, dy, 4), c)
        go(mine, near.at[index - 1], send.at[1 + index], recv.at[1 + index], other)
    yield
    value = mine[...]
    for index in range(1, 8):
        landed(near.at[index - 1], send.at[1 + index], recv.at[1 + index])
        value = value + near[index - 1]

    def block(part):
        return vectors.at[:, rows_at(part * 128, 128)]

    part = c * 4 + x
    vectors[:, rows_at(part * 128, 128)] = value
    pairs = [(j, d) for j in range(4) for d in range(2) if j or d]
    for index, (j, d) in enumerate(pairs):
        other = device(h, turn(x, j, 4), zl, y, turn(c, d, 2))
        go(block(part), block(part), part_send.at[index], part_recv.at[part], other)
    yield
    for index, (j, d) in enumerate(pairs):
        other = turn(c, d, 2) * 4 + turn(x, j, 4)
        landed(block(other), part_send.at[index], part_recv.at[other])
    for item in started:
        item.wait_send()
    moved_out(pack, send.at[0], recv.at[0], beside, home)


def greet_near(where):
    h, x, zl, y, c = where
    greet(device(h, x, zl, turn(y, 2, 4), c))
    for step in (1, 2, 3):
        greet(device(h, x, 1 - zl, turn(y, step, 4), c))
    return 4


def swap_in(where, pairs, send, recv):
    h, x, zl, y, c = where
    home = lax.rem(h + c, 2) == 0
    mine = h * 4 + x
    for item, (src, dst) in enumerate(pairs):
        for j in range(4):
            for d in range(2):
                xx, cc = turn(x, j, 4), turn(c, d, 2)
                args = (
                    src.at[rows_at((cc * 4 + xx) * ROWS, ROWS)],
                    dst.at[:, rows_at(mine * 128, 128)],
                    send.at[item, j * 2 + d],
                    recv.at[item, mine],
                    device(c, xx, zl, y, cc),
                )
                if j or d:
                    push(*args).start()
                else:
                    move(*args, home)
    yield
    for item, (src, dst) in enumerate(pairs):
        for j in range(4):
            for d in range(2):
                k = turn(h, d, 2) * 4 + turn(x, j, 4)
                view = dst.at[:, rows_at(k * 128, 128)]
                sems = (send.at[item, j * 2 + d], recv.at[item, k])
                gone = src.at[pl.ds(0, ROWS)]
                other = device(h, x, 1 - zl, y, c)
                if j or d:
                    landed(view, *sems)
                    push(gone, gone, *sems, other).wait_send()
                else:
                    moved_in(view, *sems, home)
                    moved_out(gone, *sems, other, home)


def swap_out(where, pairs, send, recv):
    h, x, zl, y, c = where
    home = lax.rem(h + c, 2) == 0
    mine = c * 4 + x
    for item, (src, dst) in enumerate(pairs):
        for j in range(4):
            for d in range(2):
                hh, xx = turn(h, d, 2), turn(x, j, 4)
                args = (
                    src.at[:, rows_at((hh * 4 + xx) * 128, 128)],
                    dst.at[rows_at(mine * ROWS, ROWS)],
                    send.at[item, j * 2 + d],
                    recv.at[item, mine],
                    device(hh, xx, zl, y, h),
                )
                if j or d:
                    push(*args).start()
                else:
                    move(*args, home)
    yield
    for item, (src, dst) in enumerate(pairs):
        for j in range(4):
            for d in range(2):
                part = turn(c, d, 2) * 4 + turn(x, j, 4)
                view = dst.at[rows_at(part * ROWS, ROWS)]
                sems = (send.at[item, j * 2 + d], recv.at[item, part])
                gone = src.at[:, pl.ds(0, 128)]
                other = device(h, x, 1 - zl, y, c)
                if j or d:
                    landed(view, *sems)
                    push(gone, gone, *sems, other).wait_send()
                else:
                    moved_in(view, *sems, home)
                    moved_out(gone, *sems, other, home)


def scatter_ring(where, rows, depth, out, hop, final, sums, kept, across, pair, last, send, recv):
    h, x, zl, y, c = where
    home = lax.rem(h + c, 2) == 0
    above = device(h, x, zl, turn(y, 1, 4), c)
    below = device(h, x, zl, turn(y, 3, 4), c)
    beside = device(h, x, 1 - zl, y, c)
    kind = hop.dtype

    def piece(p, step):
        return rows((turn(zl, p, 2) * 8 + turn(y, step, 4) * 2) * depth, 2 * depth)

    def wide(value):
        return value.astype(jnp.float32)

    def go(index, src, dst, target):
        push(src, dst, send.at[index], recv.at[index], target).start()

    def come(index, dst):
        landed(dst, send.at[index], recv.at[index])

    go(0, piece(0, 2), hop.at[0], above)
    go(1, piece(1, 2), hop.at[1], below)
    go(2, piece(1, 1), final.at[0, 1], above)
    go(3, piece(0, 3), final.at[1, 0], below)
    yield
    come(0, hop.at[0])
    sums[0] = (wide(piece(0, 1)[...]) + wide(hop[0])).astype(kind)
    go(4, sums.at[0], final.at[0, 0], above)
    come(1, hop.at[1])
    sums[1] = (wide(piece(1, 3)[...]) + wide(hop[1])).astype(kind)
    go(5, sums.at[1], final.at[1, 1], below)
    yield
    come(2, final.at[0, 1])
    come(5, final.at[1, 1])
    across[0] = (wide(piece(1, 0)[...]) + wide(final[0, 1]) + wide(final[1, 1])).astype(kind)
    go(6, across.at[0], across.at[1], beside)
    come(3, final.at[1, 0])
    come(4, final.at[0, 0])
    kept[...] = wide(piece(0, 0)[...]) + wide(final[0, 0]) + wide(final[1, 0])
    yield
    come(6, across.at[1])
    pair[...] = (kept[...] + wide(across[1])).astype(kind)
    for d in range(2):
        cc = turn(c, d, 2)
        args = (
            pair.at[rows_at(cc * depth, depth)],
            last.at[h],
            send.at[7 + d],
            recv.at[7 + h],
            device(c, x, zl, y, cc),
        )
        if d == 0:
            move(*args, home)
        else:
            push(*args).start()
    yield
    for d in range(2):
        hh = turn(h, d, 2)
        args = (last.at[hh], send.at[7 + d], recv.at[7 + hh])
        if d == 0:
            moved_in(*args, home)
        else:
            landed(*args)
    out[...] = wide(last[0]) + wide(last[1])
    for index in range(7):
        push(piece(0, 0), piece(0, 0), send.at[index], recv.at[index], beside).wait_send()
    gone = pair.at[pl.ds(0, depth)]
    moved_out(gone, send.at[7], recv.at[7], beside, home)
    push(gone, gone, send.at[8], recv.at[8], beside).wait_send()


def scatter_scratch(depth, rest, kind):
    both = (2 * depth,) + rest
    return [
        pltpu.VMEM((2,) + both, kind),
        pltpu.VMEM((2, 2) + both, kind),
        pltpu.VMEM((2,) + both, kind),
        pltpu.VMEM(both, jnp.float32),
        pltpu.VMEM((2,) + both, kind),
        pltpu.VMEM(both, kind),
        pltpu.VMEM((2, depth) + rest, kind),
    ] + RING_SEMS


def rows_of(full, depth):
    def slot(zz, yy, cc, count, core):
        return full.at[rows_at((zz * 8 + yy * 2 + cc) * depth, depth * count)]

    return slot


def rows_view(ref):
    return lambda start, count: ref.at[rows_at(start, count)]


ANYWHERE = pl.BlockSpec(memory_space=pl.ANY)
INSIDE = pl.BlockSpec(memory_space=pltpu.VMEM)
DEPTH = D // 16
CHUNK = 512
PAIR = 2 * HDIM
TILE = 256
VMEM_BYTES = 24 * 2**20

ROWS_LOW = jax.ShapeDtypeStruct((ROWS, D), jnp.bfloat16)
ROWS_WIDE = jax.ShapeDtypeStruct((ROWS, D), jnp.float32)
FULL_ROWS = jax.ShapeDtypeStruct((CAP, D), jnp.bfloat16)
FULL_CHUNK = jax.ShapeDtypeStruct((D, CHUNK), jnp.bfloat16)
OWN_CHUNK = jax.ShapeDtypeStruct((DEPTH, CHUNK), jnp.float32)
SMALL = jax.ShapeDtypeStruct((8, D), jnp.float32)
SMALL_OWN = jax.ShapeDtypeStruct((8, 128), jnp.float32)


def of(shape, kind=jnp.bfloat16):
    return jax.ShapeDtypeStruct(shape, kind)


def call(body, name, number, ins, outs, scratch, args):
    return pl.pallas_call(
        body,
        out_shape=tuple(shape for shape, _ in outs),
        in_specs=ins,
        out_specs=tuple(spec for _, spec in outs),
        scratch_shapes=scratch,
        compiler_params=pltpu.CompilerParams(
            collective_id=number, has_side_effects=True, vmem_limit_bytes=VMEM_BYTES
        ),
        name=name,
    )(*args)


def dot(left, right):
    return jnp.dot(left, right, preferred_element_type=jnp.float32)


def dot_t(left, right):
    return lax.dot_general(left, right, (((1,), (1,)), ((), ())), preferred_element_type=jnp.float32)


def t_dot(left, right):
    return lax.dot_general(left, right, (((0,), (0,)), ((), ())), preferred_element_type=jnp.float32)


def low(value):
    return value.astype(jnp.bfloat16)


def wide(value):
    return value.astype(jnp.float32)


def normed_of(values):
    centred = values - jnp.mean(values, axis=1, keepdims=True)
    inverse = lax.rsqrt(jnp.mean(centred * centred, axis=1, keepdims=True) + EPS)
    return centred * inverse, inverse


def norm_back(grad_rows, values, gain):
    normed, inverse = normed_of(values)
    grad_gain = jnp.sum(grad_rows * normed, axis=0, keepdims=True)
    grad_shift = jnp.sum(grad_rows, axis=0, keepdims=True)
    scaled = grad_rows * gain
    mean_one = jnp.mean(scaled, axis=1, keepdims=True)
    mean_two = jnp.mean(scaled * normed, axis=1, keepdims=True)
    return grad_gain, grad_shift, inverse * (scaled - mean_one - normed * mean_two)


def head_masks():
    first = lax.broadcasted_iota(jnp.int32, (1, PAIR), 1) < HDIM
    one = first.astype(jnp.float32)
    return one, 1.0 - one


def side_by_side(*parts):
    alive = list(parts)
    while alive:
        alive = [part for part in alive if next(part, alive) is not alive]
        yield


def weights_cargo(where, count, owns, fulls, sems, *plans):
    return [
        (gather_ring(where, owns[i], rows_of(fulls[i], DEPTH), *sems[2 * i : 2 * i + 2]), plans[i])
        for i in range(count)
    ]


def grads_cargo(where, count, parts, owns, scratch, *plans):
    return [
        (scatter_ring(where, rows_view(parts[i]), DEPTH, owns[i], *scratch[9 * i : 9 * i + 9]), plans[i])
        for i in range(count)
    ]


SWAP_SEMS = [pltpu.SemaphoreType.DMA((1, 8)), pltpu.SemaphoreType.DMA((1, 8))]
COLUMNS = jax.ShapeDtypeStruct((CAP, 128), jnp.float32)
ROW_SCRATCH = pltpu.VMEM((ROWS, D), jnp.bfloat16)
COLUMN_SCRATCH = pltpu.VMEM((CAP, 128), jnp.bfloat16)


PROBS = (2, TILE, TILE * 10)


def probs_at(tile):
    first = TILE * tile * (tile + 1) // 2
    return slice(first, first + TILE * (tile + 1))


def vector_of(vectors, layer, index):
    return vectors[8 * layer + index : 8 * layer + index + 1, :]


def own_vector(vectors, row, part):
    return vectors[row : row + 1, rows_at(part * 128, 128)]


def up_bias_of(vectors, layer, part):
    first = 16 + 4 * layer
    return jnp.concatenate([own_vector(vectors, first + i, part) for i in range(4)], axis=1)


def join_rows(rows, full, weights, qkv, vectors, layer, part):
    joined = dot(full[rows, :], weights[:, : 3 * PAIR])
    query_bias = own_vector(vectors, 8 * layer + 2, part)
    value_bias = own_vector(vectors, 8 * layer + 3, part)
    qkv[rows, :PAIR] = low((joined[:, :PAIR] + query_bias) * HDIM ** (-0.5))
    qkv[rows, PAIR : 2 * PAIR] = low(joined[:, PAIR : 2 * PAIR])
    qkv[rows, 2 * PAIR :] = low(joined[:, 2 * PAIR :] + value_bias)


def segments(ends, places):
    bound = 0.0
    found = jnp.zeros(places.shape, jnp.int32)
    for slot in range(4):
        bound = bound + ends[0:1, slot : slot + 1]
        found = found + (places >= bound).astype(jnp.int32)
    return found


def attend_tile(tile, qkv, ends, part, probs):
    masks = head_masks()
    rows, keys = slice(tile * TILE, (tile + 1) * TILE), (tile + 1) * TILE
    query = wide(qkv[rows, :PAIR])
    key, value = qkv[:keys, PAIR : 2 * PAIR], qkv[:keys, 2 * PAIR :]
    row_places = wide(tile * TILE + lax.broadcasted_iota(jnp.int32, (TILE, 1), 0))
    key_places = wide(lax.broadcasted_iota(jnp.int32, (1, keys), 1))
    offset = key_places - row_places
    allowed = (segments(ends, row_places) == segments(ends, key_places)) & (offset <= 0.0)
    mixed = 0.0
    for head in range(2):
        number = wide(jnp.full((1, 128), part * LOCAL_HEADS + head, jnp.int32))
        slope = jnp.exp2(-8.0 * (number + 1.0) / HEADS)
        scores = dot_t(low(query * masks[head]), key)
        scores = scores + slope[:, :1] * offset
        scores = jnp.where(allowed, scores, NEG)
        shifted = jnp.exp(scores - jnp.max(scores, axis=1, keepdims=True))
        soft = low(shifted / jnp.sum(shifted, axis=1, keepdims=True))
        probs[head, :, probs_at(tile)] = soft
        mixed = mixed + dot(soft, value) * masks[head]
    return low(mixed)


def attend_rows(core, qkv, ends, number, probs, heads, part, weights, spreading):
    def two_tiles(first):
        for tile in (first, first + 1):
            rows = slice(tile * TILE, (tile + 1) * TILE)
            mixed = attend_tile(tile, qkv, ends, number, probs)
            heads[rows, :] = mixed
            part[rows, :] = low(dot_t(mixed, weights[:, 3 * PAIR :]))

    pl.when(core == 0)(functools.partial(two_tiles, 2))
    pl.when(core == 1)(functools.partial(two_tiles, 0))
    yield
    next(spreading)
    yield
    pl.when(core == 0)(functools.partial(two_tiles, 0))
    pl.when(core == 1)(functools.partial(two_tiles, 2))
    yield


VECTORS = jax.ShapeDtypeStruct((32, D), jnp.float32)
ENDS = jax.ShapeDtypeStruct((8, 128), jnp.float32)
ATTEND_OUTS = [
    (FULL_ROWS, INSIDE),
    (of((CAP, 3 * PAIR)), INSIDE),
    (of(PROBS), INSIDE),
    (of((CAP, PAIR)), INSIDE),
    (ROWS_WIDE, INSIDE),
]


def enter_attend(columns, pack, joined, chunks):
    n = len(chunks)

    def body(columns, pack, joined, *rest):
        owns, rest = rest[:n], rest[n:]
        (vectors, ends, hidden, weights, full, qkv, probs, heads, middle), rest = rest[:9], rest[9:]
        fulls, rest = rest[:n], rest[n:]
        (columns_in, columns_sem), rest = rest[:2], rest[2:]
        (columns_low, rows_low, first, part, taken, mine, near), rest = rest[:7], rest[7:]
        line, rest = rest[:3], rest[3:]
        spread, rest = rest[:6], rest[6:]
        swap_sems, rest = rest[:2], rest[2:]
        ring_sems, rest = rest[:2], rest[2:]
        sems, pack_sems = rest[: 2 * n], rest[2 * n :]
        where = place()
        h, x, zl, y, c = where
        count = (
            greet_ring(where, True) + greet_parts(where) + greet_swap(where, True) + greet_near(where)
        )
        number = c * 4 + x
        fetch = pltpu.make_async_copy(columns, columns_in, columns_sem)
        fetch.start()
        fetch.wait()
        columns_low[...] = low(columns_in[...])
        await_greetings(count)
        packs = gather_vectors(where, pack, vectors, ends, taken, mine, near, *pack_sems)
        swap = swap_in(where, ((columns_low, rows_low),), *swap_sems)
        ring = gather_ring(where, joined, rows_of(weights, DEPTH), *ring_sems)
        gather = gather_line(where, first, part, *line, lambda rows: None)
        next(packs)
        next(swap)
        next(ring)
        finish(swap)
        hidden[...] = wide(rows_low[...])
        first[...] = low(normed_of(hidden[...])[0])
        next(gather)
        next(packs)
        next(ring)
        next(gather)
        next(packs)
        next(ring)
        next(gather)

        def main():
            yield
            next(gather)
            finish(packs)
            yield
            finish(gather)
            next(ring)
            for tile in range(CAP // TILE):
                rows = slice(tile * TILE, (tile + 1) * TILE)
                normed = wide(part[rows, :])
                full[rows, :] = low(normed * vector_of(vectors, 0, 0) + vector_of(vectors, 0, 1))
            yield
            finish(ring)
            for tile in range(CAP // TILE):
                join_rows(slice(tile * TILE, (tile + 1) * TILE), full, weights, qkv, vectors, 0, number)
            spreading = spread_line(where, part, middle, *spread)
            yield from attend_rows(c, qkv, ends, number, probs, heads, part, weights, spreading)
            yield from spreading
            middle[...] = middle[...] + hidden[...] + vector_of(vectors, 0, 4)

        weave(main(), *weights_cargo(where, n, owns, fulls, sems, (1, 3, 4, 8), (1, 3, 4, 8)))

    tile = (32, 128)
    return call(
        body,
        "enter_attend",
        0,
        [pl.BlockSpec(memory_space=pltpu.HBM)] + [INSIDE] * (2 + n),
        [(VECTORS, INSIDE), (ENDS, INSIDE), (ROWS_WIDE, INSIDE), (FULL_CHUNK, INSIDE)]
        + ATTEND_OUTS
        + [(FULL_CHUNK, INSIDE)] * n,
        [
            pltpu.VMEM((CAP, 128), jnp.float32),
            pltpu.SemaphoreType.DMA,
            COLUMN_SCRATCH,
            ROW_SCRATCH,
            ROW_SCRATCH,
            pltpu.VMEM((CAP, D), jnp.bfloat16),
            pltpu.VMEM((2,) + tile, jnp.float32),
            pltpu.VMEM(tile, jnp.float32),
            pltpu.VMEM((7,) + tile, jnp.float32),
        ]
        + LINE_SEMS
        + spread_scratch()
        + SWAP_SEMS
        + RING_SEMS * (1 + n)
        + [
            pltpu.SemaphoreType.DMA((9,)),
            pltpu.SemaphoreType.DMA((9,)),
            pltpu.SemaphoreType.DMA((7,)),
            pltpu.SemaphoreType.DMA((8,)),
        ],
        (columns, pack, joined, *chunks),
    )


def attend_forward(layer, number, hidden, vectors, ends, weights, chunks, columns):
    n = len(chunks)

    def body(hidden, vectors, ends, weights, *rest):
        owns, rest = rest[:n], rest[n:]
        (columns, full, qkv, probs, heads, middle), rest = rest[:6], rest[6:]
        fulls, rest = rest[:n], rest[n:]
        (swapped, first, part), rest = rest[:3], rest[3:]
        line, rest = rest[:3], rest[3:]
        spread, rest = rest[:6], rest[6:]
        sems, rest = rest[: 2 * n], rest[2 * n :]
        columns_low, *swap_sems = rest
        where = place()
        h, x, zl, y, c = where
        count = greet_line(where) + greet_ring(where, True) + greet_swap(where, True)
        part_number = c * 4 + x
        columns_low[...] = low(columns[...])
        normed, _ = normed_of(hidden[...])
        first[...] = low(normed * vector_of(vectors, layer, 0) + vector_of(vectors, layer, 1))
        await_greetings(count)

        def ready(rows):
            join_rows(rows, full, weights, qkv, vectors, layer, part_number)

        def main():
            yield from gather_line(where, first, full, *line, ready)
            spreading = spread_line(where, part, middle, *spread)
            yield from attend_rows(c, qkv, ends, part_number, probs, heads, part, weights, spreading)
            yield from spreading
            middle[...] = middle[...] + hidden[...] + vector_of(vectors, layer, 4)

        weave(
            main(),
            *weights_cargo(where, n, owns, fulls, sems, (0, 2, 4, 8), (0, 2, 5, 9)),
            (swap_in(where, ((columns_low, swapped),), *swap_sems), (4,)),
        )

    return call(
        body,
        "attend_forward",
        number,
        [INSIDE] * (5 + n),
        ATTEND_OUTS + [(FULL_CHUNK, INSIDE)] * n + [(ROWS_LOW, INSIDE)],
        [ROW_SCRATCH, pltpu.VMEM((CAP, D), jnp.bfloat16)]
        + LINE_SEMS
        + spread_scratch()
        + RING_SEMS * n
        + [COLUMN_SCRATCH]
        + SWAP_SEMS,
        (hidden, vectors, ends, weights, *chunks, columns),
    )


def gelu_pair(values):
    square = values * values
    bent = jnp.tanh(0.7978845608028654 * values * (1.0 + 0.044715 * square))
    half = 0.5 * (1.0 + bent)
    bend = 0.7978845608028654 * (1.0 + 3.0 * 0.044715 * square)
    return low(values * half), low(half + 0.5 * values * (1.0 - bent * bent) * bend)


def feed_forward(layer, number, middle, vectors, up, down, chunks):
    n = len(chunks)

    def body(middle, vectors, up, down, *rest):
        owns, rest = rest[:n], rest[n:]
        (full, activated, slope, hidden), rest = rest[:4], rest[4:]
        fulls, rest = rest[:n], rest[n:]
        (second, part), rest = rest[:2], rest[2:]
        line, rest = rest[:3], rest[3:]
        spread, sems = rest[:6], rest[6:]
        where = place()
        h, x, zl, y, c = where
        count = greet_line(where)
        if n:
            count = count + greet_ring(where, True)
        normed, _ = normed_of(middle[...])
        second[...] = low(normed * vector_of(vectors, layer, 5) + vector_of(vectors, layer, 6))
        await_greetings(count)
        bias = up_bias_of(vectors, layer, c * 4 + x)

        def vector(index):
            return vector_of(vectors, layer, index)

        def ready(rows):
            values = dot(full[rows, :], up[...]) + bias
            active, slope[rows, :] = gelu_pair(values)
            activated[rows, :] = active
            part[rows, :] = low(dot_t(active, down[...]))

        def main():
            spreading = spread_line(where, part, hidden, *spread)
            yield from gather_line(where, second, full, *line, ready)
            yield from spreading
            hidden[...] = hidden[...] + middle[...] + vector(7)

        weave(main(), *weights_cargo(where, n, owns, fulls, sems, (0, 2, 5, 6)))

    return call(
        body,
        "feed_forward",
        number,
        [INSIDE] * (4 + n),
        [
            (FULL_ROWS, INSIDE),
            (of((CAP, CHUNK)), INSIDE),
            (of((CAP, CHUNK)), INSIDE),
            (ROWS_WIDE, INSIDE),
        ]
        + [(FULL_CHUNK, INSIDE)] * n,
        [pltpu.VMEM((ROWS, D), jnp.bfloat16), pltpu.VMEM((CAP, D), jnp.bfloat16)]
        + LINE_SEMS
        + spread_scratch()
        + RING_SEMS * n,
        (middle, vectors, up, down, *chunks),
    )


def feed_both(layer, number, middle, vectors, up, down, cotangent):
    def body(
        middle, vectors, up, down, cotangent,
        hidden, grad_middle, down_grad, up_grad, small, small_own,
        second, second_full, activated, slope, part, full, grad_up, grad_part, *rest,
    ):
        line, rest = rest[:3], rest[3:]
        grad_line, rest = rest[:3], rest[3:]
        spread, grad_spread = rest[:6], rest[6:]
        where = place()
        h, x, zl, y, c = where
        count = greet_line(where)
        normed, _ = normed_of(middle[...])
        second[...] = low(normed * vector_of(vectors, layer, 5) + vector_of(vectors, layer, 6))
        await_greetings(count)
        bias = up_bias_of(vectors, layer, c * 4 + x)

        def vector(index):
            return vector_of(vectors, layer, index)

        def ready(rows):
            values = dot(second_full[rows, :], up[...]) + bias
            activated[rows, :], slope[rows, :] = gelu_pair(values)
            part[rows, :] = low(dot_t(activated[rows, :], down[...]))

        def ready_back(rows):
            grad_low = low(dot(full[rows, :], down[...]) * wide(slope[rows, :]))
            grad_up[rows, :] = grad_low
            grad_part[rows, :] = low(dot_t(grad_low, up[...]))

        def weight_grads():
            for tile in range(D // TILE):
                columns = slice(tile * TILE, (tile + 1) * TILE)
                down_grad[columns, :] = low(t_dot(full[:, columns], activated[...]))
                up_grad[columns, :] = low(t_dot(second_full[:, columns], grad_up[...]))
                if tile % 2:
                    yield
            total = jnp.sum(wide(grad_up[...]), axis=0, keepdims=True)
            small_own[...] = jnp.zeros_like(small_own)
            for index in range(CHUNK // 128):
                small_own[index : index + 1, :] = total[:, index * 128 : (index + 1) * 128]

        spread_forth = spread_line(where, part, hidden, *spread)
        spread_back = spread_line(where, grad_part, grad_middle, *grad_spread)
        forth = gather_line(where, second, second_full, *line, ready)
        back = gather_line(where, cotangent, full, *grad_line, ready_back)
        next(forth)
        next(forth)
        next(back)
        finish(forth)
        next(spread_forth)
        next(back)
        next(spread_forth)
        finish(back)
        next(spread_back)
        next(spread_forth)
        next(spread_back)
        finish(spread_forth)
        hidden[...] = hidden[...] + middle[...] + vector(7)
        finish(side_by_side(spread_back, weight_grads()))
        grad_next = wide(cotangent[...])
        gain, shift, grad = norm_back(grad_middle[...], middle[...], vector(5))
        small[...] = jnp.zeros_like(small)
        small[0:1, :] = gain
        small[1:2, :] = shift
        small[2:3, :] = jnp.sum(grad_next, axis=0, keepdims=True)
        grad_middle[...] = grad_next + grad

    return call(
        body,
        "feed_both",
        number,
        [INSIDE] * 5,
        [
            (ROWS_WIDE, INSIDE),
            (ROWS_WIDE, INSIDE),
            (FULL_CHUNK, INSIDE),
            (FULL_CHUNK, INSIDE),
            (SMALL, INSIDE),
            (SMALL_OWN, INSIDE),
        ],
        [
            ROW_SCRATCH,
            pltpu.VMEM((CAP, D), jnp.bfloat16),
            pltpu.VMEM((CAP, CHUNK), jnp.bfloat16),
            pltpu.VMEM((CAP, CHUNK), jnp.bfloat16),
            pltpu.VMEM((CAP, D), jnp.bfloat16),
            pltpu.VMEM((CAP, D), jnp.bfloat16),
            pltpu.VMEM((CAP, CHUNK), jnp.bfloat16),
            pltpu.VMEM((CAP, D), jnp.bfloat16),
        ]
        + LINE_SEMS * 2
        + spread_scratch() * 2,
        (middle, vectors, up, down, cotangent),
    )


def feed_backward(layer, number, grad_next, vectors, middle, up, down, second_full, activated, slope, chunks):
    n = len(chunks)

    def body(grad_next, vectors, middle, up, down, second_full, activated, slope, *rest):
        parts, rest = rest[:n], rest[n:]
        (grad_middle, down_grad, up_grad, small, small_own), rest = rest[:5], rest[5:]
        owns, rest = rest[:n], rest[n:]
        (rows_low, full, grad_up, part), rest = rest[:4], rest[4:]
        line, rest = rest[:3], rest[3:]
        spread, rest = rest[:6], rest[6:]
        where = place()
        count = greet_line(where)
        if n:
            count = count + greet_ring(where, False)
        rows_low[...] = low(grad_next[...])
        await_greetings(count)

        def ready(rows):
            grad_act = dot(full[rows, :], down[...])
            grad_low = low(grad_act * wide(slope[rows, :]))
            grad_up[rows, :] = grad_low
            part[rows, :] = low(dot_t(grad_low, up[...]))

        def weight_grads():
            for tile in range(D // TILE):
                columns = slice(tile * TILE, (tile + 1) * TILE)
                down_grad[columns, :] = low(t_dot(full[:, columns], activated[...]))
                up_grad[columns, :] = low(t_dot(second_full[:, columns], grad_up[...]))
                if tile % 2:
                    yield
            total = jnp.sum(wide(grad_up[...]), axis=0, keepdims=True)
            small_own[...] = jnp.zeros_like(small_own)
            for index in range(CHUNK // 128):
                small_own[index : index + 1, :] = total[:, index * 128 : (index + 1) * 128]

        def main():
            spreading = spread_line(where, part, grad_middle, *spread)
            yield from gather_line(where, rows_low, full, *line, ready)
            next(spreading)
            yield
            yield from side_by_side(spreading, weight_grads())
            gain, shift, grad = norm_back(
                grad_middle[...], middle[...], vectors[8 * layer + 5 : 8 * layer + 6, :]
            )
            small[...] = jnp.zeros_like(small)
            small[0:1, :] = gain
            small[1:2, :] = shift
            small[2:3, :] = jnp.sum(wide(rows_low[...]), axis=0, keepdims=True)
            grad_middle[...] = grad_next[...] + grad

        weave(main(), *grads_cargo(where, n, parts, owns, rest, (0, 2, 5, 7)))

    return call(
        body,
        "feed_backward",
        number,
        [INSIDE] * (8 + n),
        [
            (ROWS_WIDE, INSIDE),
            (FULL_CHUNK, INSIDE),
            (FULL_CHUNK, INSIDE),
            (SMALL, INSIDE),
            (SMALL_OWN, INSIDE),
        ]
        + [(OWN_CHUNK, INSIDE)] * n,
        [
            pltpu.VMEM((ROWS, D), jnp.bfloat16),
            pltpu.VMEM((CAP, D), jnp.bfloat16),
            pltpu.VMEM((CAP, CHUNK), jnp.bfloat16),
            pltpu.VMEM((CAP, D), jnp.bfloat16),
        ]
        + LINE_SEMS
        + spread_scratch()
        + scatter_scratch(DEPTH, (CHUNK,), jnp.bfloat16) * n,
        (grad_next, vectors, middle, up, down, second_full, activated, slope, *chunks),
    )


SUMS = 32


def sum_vectors(where, small, own, total, taken, turned, across, last, out, part_send, part_recv, send, recv):
    h, x, zl, y, c = where
    home = lax.rem(h + c, 2) == 0
    beside = device(h, x, 1 - zl, y, c)
    pairs = [(j, d) for j in range(4) for d in range(2) if j or d]
    started = []

    def go(*args):
        item = push(*args)
        item.start()
        started.append(item)

    for index, (j, d) in enumerate(pairs):
        xx, cc = turn(x, j, 4), turn(c, d, 2)
        go(
            small.at[:, rows_at((cc * 4 + xx) * 128, 128)],
            taken.at[index],
            part_send.at[index],
            part_recv.at[index],
            device(h, xx, zl, y, cc),
        )
    yield
    value = small[:, rows_at((c * 4 + x) * 128, 128)]
    for index in range(7):
        landed(taken.at[index], part_send.at[index], part_recv.at[index])
        value = value + taken[index]
    total[0, :SUMS] = value
    total[0, SUMS:] = own[...]
    for step in (1, 2, 3):
        go(
            total.at[0],
            turned.at[step - 1],
            send.at[step - 1],
            recv.at[step - 1],
            device(h, x, zl, turn(y, step, 4), c),
        )
    yield
    for step in (1, 2, 3):
        landed(turned.at[step - 1], send.at[step - 1], recv.at[step - 1])
    total[1] = total[0] + turned[0] + turned[1] + turned[2]
    go(total.at[1], across, send.at[3], recv.at[3], beside)
    yield
    landed(across, send.at[3], recv.at[3])
    total[2] = total[1] + across[...]
    for d in range(2):
        args = (
            total.at[2],
            last.at[h],
            send.at[4 + d],
            recv.at[4 + h],
            device(c, x, zl, y, turn(c, d, 2)),
        )
        if d == 0:
            move(*args, home)
        else:
            go(*args)
    yield
    for d in range(2):
        hh = turn(h, d, 2)
        args = (last.at[hh], send.at[4 + d], recv.at[4 + hh])
        if d == 0:
            moved_in(*args, home)
        else:
            landed(*args)
    out[...] = last[0] + last[1]
    for item in started:
        item.wait_send()
    moved_out(total.at[2], send.at[4], recv.at[4], beside, home)


def attend_backward(
    layer, number, grad_middle, vectors, hidden, weights, first_full, qkv, probs, heads, chunks,
    output=None, smalls=None,
):
    n = len(chunks)
    swaps = output is not None
    final = smalls is not None

    def body(grad_middle, vectors, hidden, weights, first_full, qkv, probs, heads, *rest):
        parts, rest = rest[:n], rest[n:]
        if swaps:
            output, rest = rest[0], rest[1:]
        if final:
            others, rest = rest[:6], rest[6:]
            (columns, weight_sum, totals), rest = rest[:3], rest[3:]
        else:
            (grad_hidden, weight_grad, small, small_own), rest = rest[:4], rest[4:]
        owns, rest = rest[:n], rest[n:]
        if swaps:
            columns, rest = rest[0], rest[1:]
        (rows_low, full, grad_heads, grad_joined, grad_key, grad_value, part), rest = rest[:7], rest[7:]
        line, rest = rest[:3], rest[3:]
        spread, rest = rest[:6], rest[6:]
        cargo, rest = rest[: 9 * n], rest[9 * n :]
        if final:
            (grad_hidden, weight_grad, small_all, own_all), rest = rest[:4], rest[4:]
            ring_scratch, rest = rest[:9], rest[9:]
            sum_scratch, rest = rest[:9], rest[9:]
            small, small_own = small_all.at[pl.ds(8, 8)], own_all.at[pl.ds(8, 8)]
        where = place()
        h, x, zl, y, c = where
        count = greet_ring(where, False)
        if final:
            greet(device(h, x, zl, turn(y, 2, 4), c))
            count = count + 1 + greet_parts(where)
        else:
            count = count + greet_line(where)
        if swaps or final:
            count = count + greet_swap(where, False)
            rows_out, columns_low, *swap_sems = rest
        rows_low[...] = low(grad_middle[...])
        await_greetings(count)
        planned = grads_cargo(where, n, parts, owns, cargo, (0, 2, 7, 10), (0, 3, 8, 11))
        if swaps:
            rows_out[...] = low(output[...])
            planned.append((swap_out(where, ((rows_out, columns_low),), *swap_sems), (4,)))

        def ready(rows):
            grad_heads[rows, :] = low(dot(full[rows, :], weights[:, 3 * PAIR :]))

        def weight_grads():
            for tile in range(D // TILE):
                features = slice(tile * TILE, (tile + 1) * TILE)
                weight_grad[features, : 3 * PAIR] = low(
                    t_dot(first_full[:, features], grad_joined[...])
                )
                weight_grad[features, 3 * PAIR :] = low(t_dot(full[:, features], heads[...]))
                if tile % 2:
                    yield
            total = jnp.sum(wide(grad_joined[...]), axis=0, keepdims=True)
            small_own[...] = jnp.zeros(small_own.shape, jnp.float32)
            small_own[0:1, :] = total[:, :PAIR]
            small_own[1:2, :] = total[:, 2 * PAIR :]

        def norm_end():
            gain, shift, grad = norm_back(grad_hidden[...], hidden[...], vector_of(vectors, layer, 0))
            small[...] = jnp.zeros(small.shape, jnp.float32)
            small[0:1, :] = gain
            small[1:2, :] = shift
            small[2:3, :] = jnp.sum(wide(rows_low[...]), axis=0, keepdims=True)
            grad_hidden[...] = grad_middle[...] + grad

        def last_steps(spreading):
            for index, first in enumerate((0, 16, 24)):
                small_all[first : first + 8, :] = others[2 * index][...]
                own_all[first : first + 8, :] = others[2 * index + 1][...]
            next(spreading)
            finish(weight_grads())
            ring = scatter_ring(where, rows_view(weight_grad), DEPTH, weight_sum, *ring_scratch)
            next(ring)
            yield
            next(spreading)
            yield
            next(ring)
            next(spreading)
            yield
            finish(spreading)
            norm_end()
            rows_out[...] = low(grad_hidden[...])
            sums = sum_vectors(where, small_all, own_all, *sum_scratch[:5], totals, *sum_scratch[5:])
            next(sums)
            swap = swap_out(where, ((rows_out, columns_low),), *swap_sems)
            next(swap)
            next(ring)
            next(sums)
            next(ring)
            next(sums)
            next(sums)
            finish(ring)
            finish(swap)
            columns[...] = wide(columns_low[...])
            finish(sums)

        def main():
            yield from gather_line(where, rows_low, full, *line, ready)
            masks = head_masks()
            grad_key[...] = jnp.zeros_like(grad_key)
            grad_value[...] = jnp.zeros_like(grad_value)
            for tile in range(CAP // TILE):
                rows, keys = slice(tile * TILE, (tile + 1) * TILE), (tile + 1) * TILE
                query, grad = wide(qkv[rows, :PAIR]), wide(grad_heads[rows, :])
                key, value = qkv[:keys, PAIR : 2 * PAIR], qkv[:keys, 2 * PAIR :]
                grad_query = 0.0
                for head in range(2):
                    grad_one = low(grad * masks[head])
                    soft_low = probs[head, :, probs_at(tile)]
                    soft = wide(soft_low)
                    grad_probs = dot_t(grad_one, value)
                    inner = jnp.sum(soft * grad_probs, axis=1, keepdims=True)
                    grad_scores = low(soft * (grad_probs - inner))
                    grad_query = grad_query + dot(grad_scores, key) * masks[head]
                    grad_key[:keys, :] += t_dot(grad_scores, low(query * masks[head]))
                    grad_value[:keys, :] += t_dot(soft_low, grad_one)
                grad_joined[rows, :PAIR] = low(grad_query * HDIM ** (-0.5))
                yield
            spreading = spread_line(where, part, grad_hidden, *spread)
            for step in range(CAP // TILE):
                rows = rows_at(turn((1 - c) * 2, step, 4) * TILE, TILE)
                grad_joined[rows, PAIR : 2 * PAIR] = low(grad_key[rows, :])
                grad_joined[rows, 2 * PAIR :] = low(grad_value[rows, :])
                part[rows, :] = low(dot_t(grad_joined[rows, :], weights[:, : 3 * PAIR]))
                if step == 1:
                    next(spreading)
            if final:
                yield from last_steps(spreading)
                return
            yield
            yield from side_by_side(spreading, weight_grads())
            norm_end()

        weave(main(), *planned)
        if swaps:
            columns[...] = wide(columns_low[...])

    rows = (2 * SUMS, 128)
    scatter = scatter_scratch(DEPTH, (CHUNK,), jnp.bfloat16)
    if final:
        outs = [(COLUMNS, INSIDE), (OWN_CHUNK, INSIDE), (of(rows, jnp.float32), INSIDE)]
        extra = (
            [
                pltpu.VMEM((ROWS, D), jnp.float32),
                pltpu.VMEM((D, CHUNK), jnp.bfloat16),
                pltpu.VMEM((SUMS, D), jnp.float32),
                pltpu.VMEM((SUMS, 128), jnp.float32),
            ]
            + scatter
            + [
                pltpu.VMEM((3,) + rows, jnp.float32),
                pltpu.VMEM((7, SUMS, 128), jnp.float32),
                pltpu.VMEM((3,) + rows, jnp.float32),
                pltpu.VMEM(rows, jnp.float32),
                pltpu.VMEM((2,) + rows, jnp.float32),
                pltpu.SemaphoreType.DMA((7,)),
                pltpu.SemaphoreType.DMA((7,)),
                pltpu.SemaphoreType.DMA((6,)),
                pltpu.SemaphoreType.DMA((6,)),
            ]
        )
    else:
        outs = [(ROWS_WIDE, INSIDE), (FULL_CHUNK, INSIDE), (SMALL, INSIDE), (SMALL_OWN, INSIDE)]
        extra = []
    return call(
        body,
        "attend_backward_last" if final else "attend_backward",
        number,
        [INSIDE] * (8 + n + swaps + 6 * final),
        outs + [(OWN_CHUNK, INSIDE)] * n + [(COLUMNS, INSIDE)] * swaps,
        [
            ROW_SCRATCH,
            pltpu.VMEM((CAP, D), jnp.bfloat16),
            pltpu.VMEM((CAP, PAIR), jnp.bfloat16),
            pltpu.VMEM((CAP, 3 * PAIR), jnp.bfloat16),
            pltpu.VMEM((CAP, PAIR), jnp.float32),
            pltpu.VMEM((CAP, PAIR), jnp.float32),
            pltpu.VMEM((CAP, D), jnp.bfloat16),
        ]
        + LINE_SEMS
        + spread_scratch()
        + scatter * n
        + extra
        + ([ROW_SCRATCH, COLUMN_SCRATCH] + SWAP_SEMS) * (swaps or final),
        (
            grad_middle, vectors, hidden, weights, first_full, qkv, probs, heads, *chunks,
            *([output] if swaps else []), *(smalls if final else []),
        ),
    )


def local_call(body, name, ins, outs, args):
    return pl.pallas_call(
        body,
        out_shape=tuple(outs),
        in_specs=ins,
        out_specs=tuple(INSIDE for _ in outs),
        compiler_params=pltpu.CompilerParams(vmem_limit_bytes=VMEM_BYTES),
        name=name,
    )(*args)


def reorder(value, order):
    return jnp.concatenate([value[:, i * HDIM : (i + 1) * HDIM] for i in order], axis=1)


def prepare(lengths, small, joined, out_turned):
    def body(lengths, small, joined, out_turned, pack, joined_out):
        row = lax.axis_index("row")
        values = wide(small[...])
        stacked = jnp.concatenate(
            [
                values[layer : layer + 1, 8 * i : 8 * i + 8]
                for layer in range(LAYERS)
                for i in range(8)
            ],
            axis=0,
        )
        lane = lax.broadcasted_iota(jnp.int32, (8, 128), 1)
        index = lax.broadcasted_iota(jnp.int32, (8, 128), 0)
        pack[0:16, :] = dot(low(stacked), low(wide(lane == row * 8 + index)))
        lane = lax.broadcasted_iota(jnp.int32, (32, 128), 1)
        index = lax.broadcasted_iota(jnp.int32, (32, 128), 0)
        placed = wide(lane == lax.rem(row, 4) * 32 + index)
        value = dot(low(values[:, 64:96]), low(placed))
        for quarter in range(4):
            here = wide(jnp.full((1, 128), quarter, jnp.int32) == lax.div(row, 4))
            for layer in range(LAYERS):
                at = 16 + 4 * layer + quarter
                pack[at : at + 1, :] = value[layer : layer + 1] * here
        lane = lax.broadcasted_iota(jnp.int32, (8, 128), 1)
        value = jnp.zeros((8, 128), jnp.float32)
        for slot in range(4):
            value = jnp.where(lane == slot, lengths[0, slot].astype(jnp.float32), value)
        pack[24:32, :] = value
        for layer in range(LAYERS):
            turned = reorder(wide(joined[layer]), (0, 3, 1, 4, 2, 5))
            joined_out[layer, :, : 3 * PAIR] = low(turned)
            joined_out[layer, :, 3 * PAIR :] = out_turned[layer]

    return local_call(
        body,
        "prepare",
        [pl.BlockSpec(memory_space=pltpu.SMEM)] + [INSIDE] * 3,
        [of((32, 128), jnp.float32), of((LAYERS, DEPTH, CHUNK))],
        (lengths, small, joined, out_turned),
    )


def settle(hidden, grad, joined, up, down, totals):
    def body(hidden, grad, joined_0, joined_1, up_0, up_1, down_0, down_1, totals, *outs):
        hidden_out, grad_out, joined_out, query, value, out_out, out_bias, first_gain, first_shift = outs[:9]
        up_out, up_bias, down_out, down_bias, second_gain, second_shift = outs[9:]
        row = lax.axis_index("row")
        hidden_out[...] = hidden[...]
        grad_out[...] = grad[...]
        for layer, ref in enumerate((joined_0, joined_1)):
            joined_out[layer] = reorder(ref[:, : 3 * PAIR], (0, 2, 4, 1, 3, 5))
            out_out[layer] = ref[:, 3 * PAIR :]
        for layer, ref in enumerate((up_0, up_1)):
            up_out[layer] = ref[...]
        for layer, ref in enumerate((down_0, down_1)):
            down_out[layer] = ref[...]
        turned = pltpu.roll(totals[...], lax.rem(128 - row * 8, 128), 1)
        places = (
            (second_gain, 0), (second_shift, 1), (down_bias, 2),
            (first_gain, 8), (first_shift, 9), (out_bias, 10),
            (query, SUMS + 8), (value, SUMS + 9),
        )
        for ref, at in places:
            for layer in range(LAYERS):
                ref[layer : layer + 1, :] = turned[at + 16 * layer : at + 16 * layer + 1, :8]
        for layer in range(LAYERS):
            block = totals[SUMS + 16 * layer : SUMS + 16 * layer + 8, :]
            index = lax.broadcasted_iota(jnp.int32, (8, 128), 0)
            line = jnp.sum(jnp.where(index == lax.div(row, 4), block, 0.0), axis=0, keepdims=True)
            line = pltpu.roll(jnp.broadcast_to(line, (8, 128)), lax.rem(128 - lax.rem(row, 4) * 32, 128), 1)
            up_bias[layer : layer + 1, :] = line[0:1, :32]

    vector = of((LAYERS, 8), jnp.float32)
    return local_call(
        body,
        "settle",
        [INSIDE] * 9,
        [
            COLUMNS,
            COLUMNS,
            of((LAYERS, DEPTH, 3 * PAIR), jnp.float32),
            vector,
            vector,
            of((LAYERS, DEPTH, PAIR), jnp.float32),
            vector,
            vector,
            vector,
            of((LAYERS, DEPTH, CHUNK), jnp.float32),
            of((LAYERS, 32), jnp.float32),
            of((LAYERS, DEPTH, CHUNK), jnp.float32),
            vector,
            vector,
            vector,
        ],
        (hidden, grad, *joined, *up, *down, totals),
    )


def shards(
    hidden_in,
    joined_weight,
    query_bias,
    value_bias,
    out_weight,
    out_bias,
    first_gain,
    first_shift,
    up_weight,
    up_bias,
    down_weight,
    down_bias,
    second_gain,
    second_shift,
    seq_lengths,
    cotangent,
):
    small = jnp.concatenate(
        [
            first_gain,
            first_shift,
            query_bias,
            value_bias,
            out_bias,
            second_gain,
            second_shift,
            down_bias,
            up_bias,
        ],
        axis=1,
    )
    pack, joined_out = prepare(seq_lengths, small, joined_weight, jnp.swapaxes(out_weight, 1, 2))
    down_turned = jnp.swapaxes(down_weight, 1, 2)
    (
        vectors, ends, input_0, joined_0, full_10, qkv_0, probs_0, heads_0, middle_0, up_0, down_0,
    ) = enter_attend(hidden_in, pack, joined_out[0], [up_weight[0], down_turned[0]])
    full_20, active_0, slope_0, hidden, joined_1 = feed_forward(
        0, 2, middle_0, vectors, up_0, down_0, [joined_out[1]]
    )
    input_1 = hidden
    full_11, qkv_1, probs_1, heads_1, middle_1, up_1, down_1, cotangent_rows = attend_forward(
        1, 3, hidden, vectors, ends, joined_1, [up_weight[1], down_turned[1]], cotangent
    )
    hidden, grad_middle, down_part, up_part, feed_small_1, feed_own_1 = feed_both(
        1, 4, middle_1, vectors, up_1, down_1, cotangent_rows
    )
    (
        grad_hidden, joined_part, attend_small_1, attend_own_1, down_sum_1, up_sum_1, hidden_out,
    ) = attend_backward(
        1, 6, grad_middle, vectors, input_1, joined_1, full_11, qkv_1, probs_1, heads_1,
        [down_part, up_part], hidden,
    )
    grad_middle, down_part, up_part, feed_small_0, feed_own_0, joined_sum_1 = feed_backward(
        0, 7, grad_hidden, vectors, middle_0, up_0, down_0, full_20, active_0, slope_0, [joined_part]
    )
    grad_out, joined_sum_0, totals, down_sum_0, up_sum_0 = attend_backward(
        0, 8, grad_middle, vectors, input_0, joined_0, full_10, qkv_0, probs_0, heads_0,
        [down_part, up_part],
        smalls=[
            feed_small_0, feed_own_0, feed_small_1, feed_own_1, attend_small_1, attend_own_1,
        ],
    )
    outs = list(
        settle(
            hidden_out,
            grad_out,
            (joined_sum_0, joined_sum_1),
            (up_sum_0, up_sum_1),
            (down_sum_0, down_sum_1),
            totals,
        )
    )
    outs[5] = jnp.swapaxes(outs[5], 1, 2)
    outs[11] = jnp.swapaxes(outs[11], 1, 2)
    return tuple(outs)


def solution(mesh):
    vector = P(None, ("col", "row"))
    return jax.shard_map(
        shards,
        mesh=mesh,
        in_specs=(
            P("row", "col"),
            P(None, "row", "col"),
            vector,
            vector,
            P(None, "col", "row"),
            vector,
            vector,
            vector,
            P(None, "row", "col"),
            vector,
            P(None, "col", "row"),
            vector,
            vector,
            vector,
            P("row", None),
            P("row", "col"),
        ),
        out_specs=(
            P("row", "col"),
            P("row", "col"),
            P(None, "row", "col"),
            vector,
            vector,
            P(None, "col", "row"),
            vector,
            vector,
            vector,
            P(None, "row", "col"),
            vector,
            P(None, "col", "row"),
            vector,
            vector,
            vector,
        ),
        check_vma=False,
    )
```
